32 devices in a mesh: groups: 2 (over x), ctx: 2 (over core), exp: 8 (over z, y).
Axes of the slice: x: 2, y: 2, z: 4, core: 2. Of those that a mesh axis runs over, the one named last changes fastest.
Arguments:
- resid: bfloat16 [2048, 3584], P(('groups', 'exp'), 'ctx'), parts along dimension 0, may hold values from -8 to 8
- q_nope: bfloat16 [2048, 8192], P(('groups', 'ctx'), 'exp'), parts along dimension 0, may hold values from -6 to 6
- q_rope: bfloat16 [2048, 4096], P(('groups', 'ctx'), 'exp'), parts along dimension 0, may hold values from -8 to 8
- latent: bfloat16 [2048, 512], P(('groups', 'ctx')), parts along dimension 0, may hold values from -6 to 6
- k_rope: bfloat16 [2048, 64], P(('groups', 'ctx')), parts along dimension 0, may hold values from -6 to 6
- w_uk: bfloat16 [512, 8192], P(None, 'exp'), may hold values from -0.25 to 0.25
- w_uv: bfloat16 [512, 8192], P(None, 'exp'), may hold values from -0.25 to 0.25
- w_out: bfloat16 [8192, 3584], P('exp', 'ctx'), may hold values from -0.5 to 0.5
- norm_gain: float32 [3584], P('ctx'), may hold values from 0.25 to 1.75
- w_gate: bfloat16 [16, 3584, 1024], P('exp', 'ctx'), may hold values from -0.09375 to 0.09375
- w_up: bfloat16 [16, 3584, 1024], P('exp', 'ctx'), may hold values from -0.09375 to 0.09375
- w_down: bfloat16 [16, 1024, 3584], P('exp', None, 'ctx'), may hold values from -0.1875 to 0.1875
- routes: int32 [2048, 8], P(('groups', 'exp')), parts along dimension 0, may hold values from 0 to 15, all different within a row; in each aligned block of 128 rows (0 to 127, 128 to 255, ...) at most 80 rows name the same one
- codes: int32 [2048, 8], P(('groups', 'exp')), parts along dimension 0, may hold values from 1 to 255
- block_order: int32 [4], P('groups'), parts along dimension 0, may hold values from 0 to 1, each once
Outputs:
- layer_out: bfloat16 [2048, 3584], P(('groups', 'exp'), 'ctx'), parts along dimension 0
The draws below stay inside these ranges and needn't reach their ends.
There are 2 independent parts, one for each index of `groups`. The reference program is written for one: setup_inputs(seed, part) draws one part's arguments, and reference() takes and returns one part's arrays. A program takes and returns all parts, laid end to end along the dimension named above; an argument that names none is the same for every part. Nothing has to cross between parts.
Inputs may be any that keep to these rules, and one draw needn't show every extreme that they name: `routes`: within the 128 rows of one index of exp, no expert is named by more than 80 rows. `block_order`: each block number appears once.
All inputs are finite; a program needn't handle non-finite values.
Results may differ from the reference program's by a relative error of at most 0.014.
Values may be sent and summed in bfloat16 or wider, within the bound.
No kernel may reach another device: no remote copies, remote signals or barrier semaphores. Data moves between devices by JAX's collectives and lax.ppermute only.
A program may use at most 128 MiB of HBM per device.

```python
import math
import jax
import jax.numpy as jnp
import numpy as np
from jax import lax

D = 3584
FF = 1024
HEADS = 64
NOPE = 128
ROPE = 64
VDIM = 128
LATENT = 512
EXPERTS = 16
TOP = 8
BLOCK = 512
TOK_DEV = 128
SEQ = 1024
BLOCKS = 2
CAP = 80
N_EXP = 8


def draw_resid(key, part):
    key = jax.random.fold_in(key, 11)
    col_key, row_key, base_key = jax.random.split(key, 3)
    columns = 10.0 ** (jax.random.uniform(col_key, (D,)) - 1.0) * 3.0 ** (jnp.arange(D, dtype=jnp.float32) / D)
    row_scale = 10.0 ** (jax.random.uniform(row_key, (SEQ, 1)) - 0.5)
    values = jax.random.normal(base_key, (SEQ, D))
    return jnp.clip(values * row_scale * columns, -8.0, 8.0).astype(jnp.bfloat16)


def draw_q_rope(key, part):
    key = jax.random.fold_in(key, 21)
    values = jax.random.normal(key, (SEQ, HEADS * ROPE))
    return jnp.clip(values, -8.0, 8.0).astype(jnp.bfloat16)


def draw_k_rope(key, part):
    key = jax.random.fold_in(key, 22)
    values = jax.random.normal(key, (SEQ, ROPE))
    return jnp.clip(values, -6.0, 6.0).astype(jnp.bfloat16)


def plant(values, stream_key, least, top_value):
    place = [jax.random.randint(jax.random.fold_in(stream_key, axis), (), 0, length) for axis, length in enumerate(values.shape)]
    widest = values.shape.index(max(values.shape))
    neighbour = place[:widest] + [(place[widest] + 1) % values.shape[widest]] + place[widest + 1:]
    return values.at[tuple(place)].set(least).at[tuple(neighbour)].set(top_value)


def steps_of(own_key, shape, cuts, least, largest):
    gain, own = 1.0, jax.random.fold_in(own_key, 6)
    for dim, blocks in cuts:
        steps = jnp.exp(jax.random.uniform(jax.random.fold_in(own, dim), (blocks,), jnp.float32, least / len(cuts), largest / len(cuts)))
        gain = gain * jnp.repeat(steps, shape[dim] // blocks).reshape([-1 if axis == dim else 1 for axis in range(len(shape))])
    return gain


def shared_out(key, own, number, rows, count, top, reach, skew):
    sequence = jax.random.permutation(key, count)
    packed, ordinary = load_shares(count, rows * top, reach, skew, True), load_shares(count, rows * top, reach, skew, False)
    places = jnp.arange(count)

    def named(lengths, turn):
        used = int((lengths > 0).sum())
        fixed = max(1, used // 4)
        shifted = fixed + (places - fixed + turn * (used - fixed)) % max(1, count - fixed)
        return jnp.zeros((count,), jnp.int32).at[sequence[jnp.where(places < fixed, places, shifted)]].set(jnp.asarray(lengths, jnp.int32))

    lengths = jnp.where(number % 4 == 0, named(packed, number // 4), named(ordinary, number - number // 4 - 1))
    mixed = jax.random.permutation(jax.random.fold_in(own, 3), count)
    giver, sink = mixed[0:count // 2 * 2:2], mixed[1:count // 2 * 2:2]
    room = jnp.minimum(lengths[giver] - 1, reach - lengths[sink]) // 2
    room = jnp.where((giver == sequence[0]) | (sink == sequence[0]) | (lengths[sink] == 0), 0, jnp.maximum(room, 0))
    shifted = jax.random.randint(jax.random.fold_in(own, 4), (count // 2,), 0, 1 << 20) % (room + 1)
    lengths = lengths.at[giver].add(-shifted).at[sink].add(shifted)
    members = jnp.searchsorted(jnp.cumsum(lengths), jnp.arange(rows * top), side="right").astype(jnp.int32)
    listing = members.reshape(top, rows).T
    listing = listing[jax.random.permutation(jax.random.fold_in(own, 1), rows)]
    turn = jax.random.randint(jax.random.fold_in(own, 2), (rows, 1), 0, top)
    return jnp.take_along_axis(listing, (jnp.arange(top)[None, :] + turn) % top, axis=1)


def load_shares(amount, total, bound, lean, full):
    weights = [(1 << 20) // math.isqrt(standing ** lean) + 1 for standing in range(1, amount + 1)]
    largest = bound if full else min(bound, max(-(-total // amount), total * weights[0] // sum(weights)))
    least = 1 if total - largest >= amount - 1 else 0
    holding, spare = [largest] + [least] * (amount - 1), total - largest - least * (amount - 1)
    while spare > 0:
        movable = [i for i in range(1, amount) if holding[i] < largest] or [i for i in range(1, amount) if holding[i] < bound]
        whole, remaining = sum([weights[i] for i in movable]), spare
        for i in movable:
            addition = min(bound - holding[i], max(1, remaining * weights[i] // whole), spare)
            holding[i] = holding[i] + addition
            spare = spare - addition
    return np.array(holding)


def normal_values(rng, extent, spread, reach, pieces=(), kind=jnp.bfloat16):
    entries = spread * jax.random.normal(rng, extent, jnp.float32)
    if pieces:
        entries = entries * steps_of(rng, extent, pieces, -0.22, 0.18)
    return jnp.clip(entries, -reach, reach).astype(kind)


def setup_inputs(seed: int = 0, part: int = 0) -> dict:
    keys = jax.random.split(jax.random.key(seed), 16)
    part_splits = jax.random.split(jax.random.fold_in(keys[15], part), 16)
    resid = draw_resid(jax.random.fold_in(jax.random.fold_in(keys[15], part), 71), part)
    q_nope = normal_values(part_splits[1], (SEQ, HEADS * NOPE), 1.0, 6.0, ((0, 2), (1, 8)))
    q_rope = draw_q_rope(jax.random.fold_in(jax.random.fold_in(keys[15], part), 71), part)
    latent = normal_values(part_splits[3], (SEQ, LATENT), 1.0, 6.0, ((0, 2),))
    k_rope = draw_k_rope(jax.random.fold_in(jax.random.fold_in(keys[15], part), 71), part)
    w_uk = normal_values(keys[5], (LATENT, HEADS * NOPE), LATENT ** -0.5, 0.25, ((1, 8),))
    w_uv = normal_values(keys[6], (LATENT, HEADS * VDIM), LATENT ** -0.5, 0.25, ((1, 8),))
    w_out = normal_values(keys[7], (HEADS * VDIM, D), VDIM ** -0.5, 0.5, ((0, 8), (1, 2)))
    norm_gain = jnp.clip(1.0 + 0.15 * jax.random.normal(keys[8], (D,), jnp.float32), 0.25, 1.75)
    w_gate = normal_values(keys[9], (EXPERTS, D, FF), D ** -0.5, 0.09375, ((0, 8), (1, 2)))
    w_up = normal_values(keys[10], (EXPERTS, D, FF), D ** -0.5, 0.09375, ((0, 8), (1, 2)))
    w_down = normal_values(keys[11], (EXPERTS, FF, D), FF ** -0.5, 0.1875, ((0, 8), (2, 2)))
    routes_keys = jax.random.split(jax.random.fold_in(part_splits[12], 1), SEQ // TOK_DEV)
    routes_turns = jax.random.permutation(jax.random.fold_in(part_splits[12], 3), SEQ // TOK_DEV)
    routes = jax.vmap(lambda own, number: shared_out(jax.random.fold_in(part_splits[12], 2), own, number, TOK_DEV, EXPERTS, TOP, CAP, 2))(routes_keys, routes_turns).reshape((SEQ, TOP))
    codes = plant(jax.random.randint(part_splits[13], (SEQ, TOP), 1, 256), jax.random.fold_in(part_splits[13], 1), 1, 255).astype(jnp.int32)
    block_order = jax.random.permutation(part_splits[14], BLOCKS).astype(jnp.int32)
    return {"resid": resid, "q_nope": q_nope, "q_rope": q_rope, "latent": latent, "k_rope": k_rope, "w_uk": w_uk, "w_uv": w_uv, "w_out": w_out, "norm_gain": norm_gain, "w_gate": w_gate, "w_up": w_up, "w_down": w_down, "routes": routes, "codes": codes, "block_order": block_order}


neg_large = -1e+30
route_factor = 2.5
norm_epsilon = 1e-06

def round_kept(values):
    return lax.optimization_barrier(values.astype(jnp.bfloat16)).astype(jnp.float32)

def reference(resid, q_nope, q_rope, latent, k_rope, w_uk, w_uv, w_out, norm_gain, w_gate, w_up, w_down, routes, codes, block_order):
    highest = lax.Precision.HIGHEST
    keys_nope = jnp.dot(latent, w_uk, preferred_element_type=jnp.float32).astype(jnp.bfloat16)
    values = jnp.dot(latent, w_uv, preferred_element_type=jnp.float32).astype(jnp.bfloat16)
    stored = jnp.arange(SEQ, dtype=jnp.int32)
    position = block_order[stored // BLOCK] * BLOCK + stored % BLOCK
    visible = position[None, :] <= position[:, None]
    rope_keys = k_rope.astype(jnp.float32)
    score_scale = (NOPE + ROPE) ** (-0.5)

    def one_head(head):
        query_part = lax.dynamic_slice_in_dim(q_nope, head * NOPE, NOPE, 1).astype(jnp.float32)
        rope_part = lax.dynamic_slice_in_dim(q_rope, head * ROPE, ROPE, 1).astype(jnp.float32)
        key_part = lax.dynamic_slice_in_dim(keys_nope, head * NOPE, NOPE, 1).astype(jnp.float32)
        value_part = lax.dynamic_slice_in_dim(values, head * VDIM, VDIM, 1)
        scores = jnp.dot(query_part, key_part.T, precision=highest) + jnp.dot(rope_part, rope_keys.T, precision=highest)
        scores = jnp.where(visible, scores * score_scale, neg_large)
        row_best = lax.optimization_barrier(jnp.max(scores, axis=1))
        weights = jnp.where(visible, jnp.exp(scores - row_best[:, None]), 0.0)
        row_total = lax.optimization_barrier(jnp.sum(weights, axis=1))
        probs = weights.astype(jnp.bfloat16)
        summed = jnp.dot(probs, value_part, preferred_element_type=jnp.float32)
        return (summed / row_total[:, None]).astype(jnp.bfloat16)
    heads_out = lax.map(one_head, jnp.arange(HEADS, dtype=jnp.int32))
    group_heads = HEADS // N_EXP
    grouped_out = heads_out.reshape(N_EXP, group_heads, SEQ, VDIM)
    grouped_weights = w_out.reshape(N_EXP, group_heads, VDIM, D)

    def add_group(running, group_pair):
        part_out = jnp.einsum('hqv,hvd->qd', group_pair[0].astype(jnp.float32), group_pair[1].astype(jnp.float32), precision=highest)
        return (running + round_kept(part_out), None)
    attention, _ = lax.scan(add_group, jnp.zeros((SEQ, D), jnp.float32), (grouped_out, grouped_weights))
    residual_state = resid.astype(jnp.float32) + attention
    inverse_rms = lax.rsqrt(lax.optimization_barrier(jnp.mean(residual_state * residual_state, axis=1)) + norm_epsilon)
    normed = (residual_state * inverse_rms[:, None] * norm_gain).astype(jnp.bfloat16)
    route_blocks = routes.reshape(N_EXP, TOK_DEV * TOP)
    onehot = (route_blocks[:, :, None] == jnp.arange(EXPERTS, dtype=jnp.int32)[None, None, :]).astype(jnp.int32)
    earlier = jnp.cumsum(onehot, axis=1) - onehot
    slot_index = lax.optimization_barrier(jnp.sum(earlier * onehot, axis=2))
    block_ids = jnp.broadcast_to(jnp.arange(N_EXP, dtype=jnp.int32)[:, None], route_blocks.shape)
    token_ids = block_ids * TOK_DEV + jnp.arange(TOK_DEV * TOP, dtype=jnp.int32)[None, :] // TOP
    table = jnp.zeros((EXPERTS, N_EXP, CAP), jnp.int32).at[route_blocks, block_ids, slot_index].set(token_ids)

    def run_expert(expert):
        rows = jnp.take(normed, table[expert].reshape(-1), axis=0)
        gate_pre = jnp.dot(rows, w_gate[expert], preferred_element_type=jnp.float32)
        up_pre = jnp.dot(rows, w_up[expert], preferred_element_type=jnp.float32)
        hidden = (jax.nn.silu(gate_pre) * up_pre).astype(jnp.bfloat16)
        return jnp.dot(hidden, w_down[expert], preferred_element_type=jnp.float32).astype(jnp.bfloat16)
    outcome = lax.map(run_expert, jnp.arange(EXPERTS, dtype=jnp.int32))
    place_rows = (block_ids * CAP + slot_index).reshape(SEQ, TOP)
    chosen = outcome[routes, place_rows]
    code_values = codes.astype(jnp.float32)
    route_weight = route_factor * code_values / lax.optimization_barrier(jnp.sum(code_values, axis=1, keepdims=True))
    mixture = lax.optimization_barrier(jnp.sum(route_weight[:, :, None] * chosen.astype(jnp.float32), axis=1))
    return (residual_state + mixture).astype(jnp.bfloat16)
```

```python
import functools
import math

import jax
import jax.numpy as jnp
from jax import lax
from jax.experimental import pallas as pl
from jax.experimental.pallas import tpu as pltpu
from jax.sharding import PartitionSpec as P

D = 3584
NOPE = 128
ROPE = 64
VDIM = 128
BLOCK = 512

neg_large = -1e30
route_factor = 2.5
norm_epsilon = 1e-06
f32 = jnp.float32
bf16 = jnp.bfloat16


def place_of(stored_rows, block_order):
    which_block = stored_rows // BLOCK
    matches = which_block[:, None] == jnp.arange(block_order.shape[0], dtype=jnp.int32)[None, :]
    block_rank = jnp.sum(jnp.where(matches, block_order[None, :], 0), axis=1)
    return block_rank * BLOCK + stored_rows % BLOCK


def attention_kernel(
    q_nope_ref, q_rope_ref, latent_ref, rope_low_ref, rope_high_ref, w_uk_ref, w_uv_ref, q_place_ref, k_place_ref, out_ref
):
    latent = latent_ref[...]
    keys = jnp.dot(latent, w_uk_ref[...], preferred_element_type=f32).astype(bf16)
    values = jnp.dot(latent, w_uv_ref[...], preferred_element_type=f32).astype(bf16)
    scale = (NOPE + ROPE) ** (-0.5) * math.log2(math.e)
    rows = q_nope_ref.shape[0]
    step = math.gcd(rows, 256)
    for head in range(2):
        cols = slice(head * NOPE, (head + 1) * NOPE)
        rope = (rope_low_ref, rope_high_ref)[head][...]
        key_cat = jnp.concatenate([keys[:, cols], rope], axis=1)
        for first in range(0, rows, step):
            part = slice(first, first + step)
            query = jnp.concatenate([q_nope_ref[part, cols], q_rope_ref[part, :]], axis=1)
            scores = lax.dot_general(query, key_cat, (((1,), (1,)), ((), ())), preferred_element_type=f32)
            visible = k_place_ref[...] <= q_place_ref[part, :]
            scores = jnp.where(visible, scores, neg_large)
            best = jnp.max(scores, axis=1, keepdims=True)
            probs = jnp.exp2((scores - best) * scale)
            total = jnp.sum(probs, axis=1, keepdims=True)
            summed = jnp.dot(probs.astype(bf16), values[:, cols], preferred_element_type=f32)
            out_ref[part, cols] = (summed / total).astype(bf16)


def attend(q_nope, q_rope, latent, k_rope, w_uk, w_uv, q_place, k_place):
    rows, keys = q_nope.shape[0], latent.shape[0]
    pairs = q_nope.shape[1] // (2 * NOPE)
    blank = jnp.zeros_like(k_rope)
    rope_low = jnp.concatenate([k_rope, blank], axis=1)
    rope_high = jnp.concatenate([blank, k_rope], axis=1)
    row_block = math.gcd(rows, 512)
    whole = lambda shape: pl.BlockSpec(shape, lambda h, r: (0, 0))
    return pl.pallas_call(
        attention_kernel,
        grid=(pairs, rows // row_block),
        in_specs=[
            pl.BlockSpec((row_block, 2 * NOPE), lambda h, r: (r, h)),
            pl.BlockSpec((row_block, 2 * ROPE), lambda h, r: (r, h)),
            whole((keys, latent.shape[1])),
            whole((keys, 2 * ROPE)),
            whole((keys, 2 * ROPE)),
            pl.BlockSpec((latent.shape[1], 2 * NOPE), lambda h, r: (0, h)),
            pl.BlockSpec((latent.shape[1], 2 * VDIM), lambda h, r: (0, h)),
            pl.BlockSpec((row_block, 1), lambda h, r: (r, 0)),
            whole((1, keys)),
        ],
        out_specs=pl.BlockSpec((row_block, 2 * VDIM), lambda h, r: (r, h)),
        out_shape=jax.ShapeDtypeStruct((rows, q_nope.shape[1]), bf16),
        compiler_params=pltpu.CompilerParams(vmem_limit_bytes=48 * 1024 * 1024),
        cost_estimate=pl.CostEstimate(
            flops=2 * rows * keys * pairs * 2 * 384, bytes_accessed=8 * 1024 * 1024, transcendentals=rows * keys * pairs * 2
        ),
    )(q_nope, q_rope, latent, rope_low, rope_high, w_uk, w_uv, q_place[:, None], k_place[None, :])


class Grid:
    def __init__(self, count):
        self.depth = count // 2
        index = lax.axis_index("exp")
        self.z, self.y = index // 2, index % 2

    def across(self, block, rows):
        return lax.ppermute(block, "exp", [(z * 2 + y, z * 2 + 1 - y) for z in rows for y in (0, 1)])

    def along(self, block, moves):
        return lax.ppermute(block, "exp", [(z * 2 + y, t * 2 + y) for z, t in moves for y in (0, 1)])

    def choose(self, options):
        result = options[0][0]
        for block, rows in options[1:]:
            here = functools.reduce(jnp.logical_or, [self.z == r for r in rows])
            result = jnp.where(here, block, result)
        return result

    def nearest(self, z):
        return sorted((t for t in range(self.depth) if t != z), key=lambda t: (abs(t - z), t))


def gather_rows(grid, own):
    depth = grid.depth
    found = {}
    plus, minus = own, own
    result = [(own, grid.across(own, range(depth)))]
    crossed = {}
    for d in range(1, depth):
        up = [(z, z + 1) for z in range(d - 1, depth - 1)]
        down = [(z, z - 1) for z in range(1, depth - d + 1)]
        if 2 * d > depth + 1:
            both = grid.along(plus, up + down)
        else:
            plus, minus = grid.along(plus, up), grid.along(minus, down)
            if 2 * d >= depth:
                both = jnp.where(grid.z >= d, plus, minus)
        if 2 * d >= depth:
            if 2 * (d + 1) > depth + 1:
                plus = minus = both
            rows = [z for z in range(depth) if z >= d or z + d < depth]
            found[d] = (both, grid.across(both, rows))
        else:
            found[(1, d)] = (plus, grid.across(plus, range(d, depth)))
            found[(-1, d)] = (minus, grid.across(minus, range(depth - d)))
    for j in range(depth - 1):
        options = {}
        for z in range(depth):
            source = grid.nearest(z)[j]
            d = abs(source - z)
            key = d if 2 * d >= depth else (1 if source < z else -1, d)
            options.setdefault(key, []).append(z)
        pick = sorted(options.items(), key=lambda item: -len(item[1]))
        result.append(tuple(grid.choose([(found[key][side], rows) for key, rows in pick]) for side in (0, 1)))
    return result


def scatter_rows(grid, part):
    depth = grid.depth
    plus = minus = None

    def total(terms):
        return functools.reduce(jnp.add, [t.astype(f32) for t in terms if t is not None])

    for d in range(depth - 1, 0, -1):
        up = [(z, z + 1) for z in range(depth - d)]
        down = [(z, z - 1) for z in range(d, depth)]
        if 2 * d >= depth:
            targets = [z + d if z + d < depth else max(z - d, 0) for z in range(depth)]
            rows = [z for z in range(depth) if z + d < depth or z >= d]
            other = grid.across(part(targets, 1).astype(bf16), rows)
            block = total([part(targets, 0), other, plus, minus]).astype(bf16)
            if 2 * d > depth + 1:
                plus, minus = grid.along(block, up + down), None
            else:
                plus, minus = grid.along(block, up), grid.along(block, down)
        else:
            above = [min(z + d, depth - 1) for z in range(depth)]
            below = [max(z - d, 0) for z in range(depth)]
            other_up = grid.across(part(above, 1).astype(bf16), range(depth - d))
            other_down = grid.across(part(below, 1).astype(bf16), range(d, depth))
            block_up = total([part(above, 0), other_up, plus]).astype(bf16)
            block_down = total([part(below, 0), other_down, minus]).astype(bf16)
            plus, minus = grid.along(block_up, up), grid.along(block_down, down)
    here = list(range(depth))
    other = grid.across(part(here, 1).astype(bf16), here)
    return total([part(here, 0), other, plus, minus])


def per_device(
    count,
    resid,
    q_nope,
    q_rope,
    latent,
    k_rope,
    w_uk,
    w_uv,
    w_out,
    norm_gain,
    w_gate,
    w_up,
    w_down,
    routes,
    codes,
    block_order,
):
    grid = Grid(count)
    core = lax.axis_index("ctx")
    swap = lambda block: lax.ppermute(block, "ctx", [(0, 1), (1, 0)])
    query_rows = q_nope.shape[0]
    token_rows = resid.shape[0]
    owned = w_gate.shape[0]

    places = lambda who: place_of(who * query_rows + jnp.arange(query_rows, dtype=jnp.int32), block_order)
    own_place, other_place = places(core), places(1 - core)
    latents = jnp.concatenate([latent, swap(latent)], axis=0)
    ropes = jnp.concatenate([k_rope, swap(k_rope)], axis=0)
    routing = lax.all_gather(jnp.concatenate([routes, codes], axis=1), "exp", axis=0, tiled=False)
    heads = attend(
        q_nope, q_rope, latents, ropes, w_uk, w_uv, own_place, jnp.concatenate([own_place, other_place])
    )
    heads = jnp.concatenate([heads, swap(heads)], axis=0)

    def attention_part(targets, side):
        row = jnp.array(targets, jnp.int32)[grid.z]
        block = row * 2 + (1 - grid.y if side else grid.y)
        first = lax.rem(block + count - core * (count // 2), count) * token_rows
        return jnp.dot(lax.dynamic_slice_in_dim(heads, first, token_rows, 0), w_out, preferred_element_type=f32)

    residual_state = resid.astype(f32) + scatter_rows(grid, attention_part)
    squares = lax.psum(jnp.sum(residual_state * residual_state, axis=1), "ctx")
    inverse_rms = lax.rsqrt(squares / D + norm_epsilon)
    normed = (residual_state * inverse_rms[:, None] * norm_gain).astype(bf16)

    arrived = gather_rows(grid, normed)
    experts = lax.axis_index("exp") * owned + jnp.arange(owned, dtype=jnp.int32)
    outcomes = []
    for j, pair in enumerate(arrived):
        source = jnp.array([[z] + grid.nearest(z) for z in range(grid.depth)], jnp.int32)[grid.z, j]
        blocks = [routing[source * 2 + grid.y], routing[source * 2 + 1 - grid.y]]
        rule = jnp.concatenate(blocks, axis=0)
        top = rule.shape[1] // 2
        code_values = rule[:, top:].astype(f32)
        route_weight = route_factor * code_values / jnp.sum(code_values, axis=1, keepdims=True)
        named = rule[None, :, :top] == experts[:, None, None]
        weight = jnp.sum(jnp.where(named, route_weight[None], 0.0), axis=2)
        rows = jnp.concatenate(pair, axis=0)
        gate_pre = jnp.einsum("td,ldf->ltf", rows, w_gate, preferred_element_type=f32).astype(bf16)
        up_pre = jnp.einsum("td,ldf->ltf", rows, w_up, preferred_element_type=f32).astype(bf16)
        gate_pre = gate_pre.astype(f32) + swap(gate_pre).astype(f32)
        up_pre = up_pre.astype(f32) + swap(up_pre).astype(f32)
        hidden = (jax.nn.silu(gate_pre) * up_pre * weight[:, :, None]).astype(bf16)
        outcome = functools.reduce(
            jnp.add, [jnp.dot(hidden[e], w_down[e], preferred_element_type=f32) for e in range(owned)]
        ).astype(bf16)
        outcomes.append((outcome[:token_rows], outcome[token_rows:]))

    def expert_part(targets, side):
        options = {}
        for z, target in enumerate(targets):
            j = 0 if target == z else 1 + grid.nearest(z).index(target)
            options.setdefault(j, []).append(z)
        pick = sorted(options.items(), key=lambda item: -len(item[1]))
        return grid.choose([(outcomes[j][side], rows) for j, rows in pick])

    return (residual_state + scatter_rows(grid, expert_part)).astype(bf16)


def solution(mesh):
    return jax.shard_map(
        functools.partial(per_device, mesh.shape["exp"]),
        mesh=mesh,
        in_specs=(
            P(("groups", "exp"), "ctx"),
            P(("groups", "ctx"), "exp"),
            P(("groups", "ctx"), "exp"),
            P(("groups", "ctx"), None),
            P(("groups", "ctx"), None),
            P(None, "exp"),
            P(None, "exp"),
            P("exp", "ctx"),
            P("ctx"),
            P("exp", "ctx", None),
            P("exp", "ctx", None),
            P("exp", None, "ctx"),
            P(("groups", "exp"), None),
            P(("groups", "exp"), None),
            P("groups"),
        ),
        out_specs=P(("groups", "exp"), "ctx"),
        check_vma=False,
    )
```

```python
import functools
import math

import jax
import jax.numpy as jnp
from jax import lax
from jax.experimental import pallas as pl
from jax.experimental.pallas import tpu as pltpu
from jax.sharding import PartitionSpec as P

D = 3584
NOPE = 128
ROPE = 64
VDIM = 128
BLOCK = 512

neg_large = -1e30
route_factor = 2.5
norm_epsilon = 1e-06
f32 = jnp.float32
bf16 = jnp.bfloat16


def place_of(stored_rows, block_order):
    which_block = stored_rows // BLOCK
    matches = which_block[:, None] == jnp.arange(block_order.shape[0], dtype=jnp.int32)[None, :]
    block_rank = jnp.sum(jnp.where(matches, block_order[None, :], 0), axis=1)
    return block_rank * BLOCK + stored_rows % BLOCK


def attention_kernel(
    q_nope_ref, q_rope_ref, latent_ref, rope_low_ref, rope_high_ref, w_uk_ref, w_uv_ref, q_place_ref, k_place_ref, out_ref
):
    latent = latent_ref[...]
    keys = jnp.dot(latent, w_uk_ref[...], preferred_element_type=f32).astype(bf16)
    values = jnp.dot(latent, w_uv_ref[...], preferred_element_type=f32).astype(bf16)
    scale = (NOPE + ROPE) ** (-0.5) * math.log2(math.e)
    rows = q_nope_ref.shape[0]
    step = math.gcd(rows, 256)
    for head in range(2):
        cols = slice(head * NOPE, (head + 1) * NOPE)
        rope = (rope_low_ref, rope_high_ref)[head][...]
        key_cat = jnp.concatenate([keys[:, cols], rope], axis=1)
        for first in range(0, rows, step):
            part = slice(first, first + step)
            query = jnp.concatenate([q_nope_ref[part, cols], q_rope_ref[part, :]], axis=1)
            scores = lax.dot_general(query, key_cat, (((1,), (1,)), ((), ())), preferred_element_type=f32)
            visible = k_place_ref[...] <= q_place_ref[part, :]
            scores = jnp.where(visible, scores, neg_large)
            best = jnp.max(scores, axis=1, keepdims=True)
            probs = jnp.exp2((scores - best) * scale)
            total = jnp.sum(probs, axis=1, keepdims=True)
            summed = jnp.dot(probs.astype(bf16), values[:, cols], preferred_element_type=f32)
            out_ref[part, cols] = (summed / total).astype(bf16)


def attend(q_nope, q_rope, latent, k_rope, w_uk, w_uv, q_place, k_place):
    rows, keys = q_nope.shape[0], latent.shape[0]
    pairs = q_nope.shape[1] // (2 * NOPE)
    blank = jnp.zeros_like(k_rope)
    rope_low = jnp.concatenate([k_rope, blank], axis=1)
    rope_high = jnp.concatenate([blank, k_rope], axis=1)
    row_block = math.gcd(rows, 512)
    whole = lambda shape: pl.BlockSpec(shape, lambda h, r: (0, 0))
    return pl.pallas_call(
        attention_kernel,
        grid=(pairs, rows // row_block),
        in_specs=[
            pl.BlockSpec((row_block, 2 * NOPE), lambda h, r: (r, h)),
            pl.BlockSpec((row_block, 2 * ROPE), lambda h, r: (r, h)),
            whole((keys, latent.shape[1])),
            whole((keys, 2 * ROPE)),
            whole((keys, 2 * ROPE)),
            pl.BlockSpec((latent.shape[1], 2 * NOPE), lambda h, r: (0, h)),
            pl.BlockSpec((latent.shape[1], 2 * VDIM), lambda h, r: (0, h)),
            pl.BlockSpec((row_block, 1), lambda h, r: (r, 0)),
            whole((1, keys)),
        ],
        out_specs=pl.BlockSpec((row_block, 2 * VDIM), lambda h, r: (r, h)),
        out_shape=jax.ShapeDtypeStruct((rows, q_nope.shape[1]), bf16),
        compiler_params=pltpu.CompilerParams(vmem_limit_bytes=48 * 1024 * 1024),
        cost_estimate=pl.CostEstimate(
            flops=2 * rows * keys * pairs * 2 * 384, bytes_accessed=8 * 1024 * 1024, transcendentals=rows * keys * pairs * 2
        ),
    )(q_nope, q_rope, latent, rope_low, rope_high, w_uk, w_uv, q_place[:, None], k_place[None, :])


class Ring:
    def __init__(self, count):
        self.count, self.half = count, count // 2
        order = list(range(0, count, 2)) + list(range(count - 1, 0, -2)) if count == 8 else list(range(count))
        self.order = jnp.array(order, jnp.int32)
        self.place = jnp.array([order.index(i) for i in range(count)], jnp.int32)[lax.axis_index("exp")]
        self.up = [(order[p], order[(p + 1) % count]) for p in range(count)]
        self.down = [(t, s) for s, t in self.up]

    def send(self, block, way):
        return lax.ppermute(block, "exp", self.up if way > 0 else self.down)

    def at(self, offset):
        return self.order[lax.rem(self.place + offset + self.count, self.count)]


def after(blocks, work):
    if not work:
        return blocks
    held = lax.optimization_barrier((tuple(blocks), tuple(work)))
    return list(held[0])


def scatter_rows(ring, part):
    total = lambda terms: functools.reduce(jnp.add, [t.astype(f32) for t in terms])
    far = part(ring.half)
    cut = far.shape[0] // 2
    going = {1: ring.send(far[:cut].astype(bf16), 1), -1: ring.send(far[cut:].astype(bf16), -1)}
    for offset in range(ring.half - 1, 0, -1):
        for way in (1, -1):
            own = part(way * offset).astype(f32)
            come = going[way].astype(f32)
            if come.shape[0] == cut:
                if way > 0:
                    block = jnp.concatenate([own[:cut] + come, own[cut:]], axis=0)
                else:
                    block = jnp.concatenate([own[:cut], own[cut:] + come], axis=0)
            else:
                block = own + come
            going[way] = ring.send(block.astype(bf16), way)
    return total([part(0), going[1], going[-1]])


def per_device(
    count,
    resid,
    q_nope,
    q_rope,
    latent,
    k_rope,
    w_uk,
    w_uv,
    w_out,
    norm_gain,
    w_gate,
    w_up,
    w_down,
    routes,
    codes,
    block_order,
):
    ring = Ring(count)
    core, index = lax.axis_index("ctx"), lax.axis_index("exp")
    swap = lambda block: lax.ppermute(block, "ctx", [(0, 1), (1, 0)])
    query_rows = q_nope.shape[0]
    token_rows = resid.shape[0]
    owned = w_gate.shape[0]
    cut = token_rows // 2

    code_values = codes.astype(f32)
    route_weight = route_factor * code_values / jnp.sum(code_values, axis=1, keepdims=True)
    named = routes[None] == jnp.arange(count * owned, dtype=jnp.int32)[:, None, None]
    routing = jnp.sum(jnp.where(named, route_weight[None], 0.0), axis=2)[None]
    for bit in [1 << b for b in range(count.bit_length() - 1)]:
        other = lax.ppermute(routing, "exp", [(i, i ^ bit) for i in range(count)])
        routing = jnp.concatenate([routing, other], axis=0)

    def weight_of(offset):
        entry = lax.dynamic_index_in_dim(routing, jnp.bitwise_xor(ring.at(offset), index), 0, keepdims=False)
        return lax.dynamic_slice_in_dim(entry, index * owned, owned, 0)

    places = lambda who: place_of(who * query_rows + jnp.arange(query_rows, dtype=jnp.int32), block_order)
    own_place, other_place = places(core), places(1 - core)
    latents = jnp.concatenate([latent, swap(latent)], axis=0)
    ropes = jnp.concatenate([k_rope, swap(k_rope)], axis=0)
    heads = attend(
        q_nope, q_rope, latents, ropes, w_uk, w_uv, own_place, jnp.concatenate([own_place, other_place])
    )
    heads = jnp.concatenate([heads, swap(heads)], axis=0)

    def attention_part(offset):
        first = lax.rem(ring.at(offset) + count - core * (count // 2), count) * token_rows
        return jnp.dot(lax.dynamic_slice_in_dim(heads, first, token_rows, 0), w_out, preferred_element_type=f32)

    residual_state = resid.astype(f32) + scatter_rows(ring, attention_part)
    squares = jnp.sum(residual_state * residual_state, axis=1)
    squares = squares + swap(squares)
    inverse_rms = lax.rsqrt(squares / D + norm_epsilon)
    normed = (residual_state * inverse_rms[:, None] * norm_gain).astype(bf16)

    def before_hidden(rows):
        gate_pre = jnp.einsum("td,ldf->ltf", rows, w_gate, preferred_element_type=f32).astype(bf16)
        up_pre = jnp.einsum("td,ldf->ltf", rows, w_up, preferred_element_type=f32).astype(bf16)
        return gate_pre, up_pre

    def after_hidden(gate_pre, up_pre, weight):
        gate_pre = gate_pre.astype(f32) + swap(gate_pre).astype(f32)
        up_pre = up_pre.astype(f32) + swap(up_pre).astype(f32)
        hidden = (jax.nn.silu(gate_pre) * up_pre * weight[:, :, None]).astype(bf16)
        return functools.reduce(
            jnp.add, [jnp.dot(hidden[e], w_down[e], preferred_element_type=f32) for e in range(owned)]
        ).astype(bf16)

    pre = [before_hidden(normed)]
    outcomes = [after_hidden(*pre[0], weight_of(0))]
    below = above = normed
    for step in range(1, ring.half + 1):
        if step > 1:
            below, above = after([below, above], pre[step - 2] + tuple(outcomes[step - 3 : step - 2]))
        if step == ring.half:
            below, above = below[:cut], above[cut:]
        below, above = ring.send(below, 1), ring.send(above, -1)
        pre.append(before_hidden(jnp.concatenate([below, above], axis=0)))
        weight = weight_of(step)
        if step < ring.half:
            weight = jnp.concatenate([weight_of(-step), weight], axis=1)
        outcomes.append(after_hidden(*pre[step], weight))

    def expert_part(offset):
        outcome = outcomes[abs(offset)]
        if abs(offset) in (0, ring.half):
            return outcome
        return outcome[token_rows:] if offset > 0 else outcome[:token_rows]

    return (residual_state + scatter_rows(ring, expert_part)).astype(bf16)


def solution(mesh):
    return jax.shard_map(
        functools.partial(per_device, mesh.shape["exp"]),
        mesh=mesh,
        in_specs=(
            P(("groups", "exp"), "ctx"),
            P(("groups", "ctx"), "exp"),
            P(("groups", "ctx"), "exp"),
            P(("groups", "ctx"), None),
            P(("groups", "ctx"), None),
            P(None, "exp"),
            P(None, "exp"),
            P("exp", "ctx"),
            P("ctx"),
            P("exp", "ctx", None),
            P("exp", "ctx", None),
            P("exp", None, "ctx"),
            P(("groups", "exp"), None),
            P(("groups", "exp"), None),
            P("groups"),
        ),
        out_specs=P(("groups", "exp"), "ctx"),
        check_vma=False,
    )
```

```python
import functools
import math

import jax
import jax.numpy as jnp
from jax import lax
from jax.experimental import pallas as pl
from jax.experimental.pallas import tpu as pltpu
from jax.sharding import PartitionSpec as P

D = 3584
NOPE = 128
ROPE = 64
VDIM = 128
BLOCK = 512

neg_large = -1e30
route_factor = 2.5
norm_epsilon = 1e-06
f32 = jnp.float32
bf16 = jnp.bfloat16


def attention_kernel(
    scalars_ref, q_nope_ref, q_rope_ref, own_latent_ref, other_latent_ref, own_rope_ref, other_rope_ref, w_uk_ref, w_uv_ref, out_ref
):
    core = scalars_ref[0]
    rank_of = lambda block: scalars_ref[1 + block]
    scale = (NOPE + ROPE) ** (-0.5) * math.log2(math.e)
    rows = q_nope_ref.shape[0]
    blocks = rows // BLOCK
    step = 256
    keys_t, values = [], []
    for latent_ref in (own_latent_ref, other_latent_ref):
        latent = latent_ref[...]
        keys_t.append(
            lax.dot_general(w_uk_ref[...], latent, (((0,), (1,)), ((), ())), preferred_element_type=f32).astype(bf16)
        )
        values.append(jnp.dot(latent, w_uv_ref[...], preferred_element_type=f32).astype(bf16))
    ropes = (own_rope_ref[...], other_rope_ref[...])
    blank = jnp.zeros_like(ropes[0])
    ahead = lax.broadcasted_iota(jnp.int32, (step, BLOCK), 1) - lax.broadcasted_iota(jnp.int32, (step, BLOCK), 0)
    for head in range(2):
        cols = slice(head * NOPE, (head + 1) * NOPE)
        key_cat = [
            jnp.concatenate([keys[cols, :]] + ([rope, blank] if head == 0 else [blank, rope]), axis=0)
            for keys, rope in zip(keys_t, ropes)
        ]
        for first in range(0, rows, step):
            part = slice(first, first + step)
            query = jnp.concatenate([q_nope_ref[part, cols], q_rope_ref[part, :]], axis=1)
            query_rank = rank_of(core * blocks + first // BLOCK)
            scores = []
            for side in (0, 1):
                whole = jnp.dot(query, key_cat[side], preferred_element_type=f32)
                for block in range(blocks):
                    owner = core if side == 0 else 1 - core
                    reach = (query_rank - rank_of(owner * blocks + block)) * BLOCK + first % BLOCK
                    piece = whole[:, block * BLOCK : (block + 1) * BLOCK]
                    scores.append(jnp.where(ahead <= reach, piece, neg_large))
            best = functools.reduce(jnp.maximum, [jnp.max(piece, axis=1, keepdims=True) for piece in scores])
            probs = [jnp.exp2((piece - best) * scale) for piece in scores]
            total = functools.reduce(jnp.add, [jnp.sum(piece, axis=1, keepdims=True) for piece in probs])
            summed = 0.0
            for number, piece in enumerate(probs):
                held = values[number // blocks][number % blocks * BLOCK : (number % blocks + 1) * BLOCK, cols]
                summed = summed + jnp.dot(piece.astype(bf16), held, preferred_element_type=f32)
            out_ref[part, cols] = (summed / total).astype(bf16)


def attend(scalars, q_nope, q_rope, latents, ropes, w_uk, w_uv):
    rows, keys = q_nope.shape[0], 2 * latents[0].shape[0]
    pairs = q_nope.shape[1] // (2 * NOPE)
    whole = lambda array: pl.BlockSpec(array.shape, lambda h, s: (0, 0))
    column = lambda array, width: pl.BlockSpec((array.shape[0], width), lambda h, s: (0, h))
    return pl.pallas_call(
        attention_kernel,
        grid_spec=pltpu.PrefetchScalarGridSpec(
            num_scalar_prefetch=1,
            grid=(pairs,),
            in_specs=[column(q_nope, 2 * NOPE), column(q_rope, 2 * ROPE)]
            + [whole(array) for array in (*latents, *ropes)]
            + [column(w_uk, 2 * NOPE), column(w_uv, 2 * VDIM)],
            out_specs=column(q_nope, 2 * VDIM),
        ),
        out_shape=jax.ShapeDtypeStruct((rows, q_nope.shape[1]), bf16),
        compiler_params=pltpu.CompilerParams(vmem_limit_bytes=48 * 1024 * 1024),
        cost_estimate=pl.CostEstimate(
            flops=2 * rows * keys * pairs * 2 * 384, bytes_accessed=8 * 1024 * 1024, transcendentals=rows * keys * pairs * 2
        ),
    )(scalars, q_nope, q_rope, *latents, *ropes, w_uk, w_uv)


def gate_up_kernel(*refs):
    *block_refs, w_gate_ref, w_up_ref, out_ref, rows_ref = refs

    @pl.when((pl.program_id(0) == 0) & (pl.program_id(1) == 0))
    def _():
        first = 0
        for ref in block_refs:
            rows_ref[first : first + ref.shape[0], :] = ref[...]
            first += ref.shape[0]

    rows = rows_ref[...]
    out_ref[0, 0] = jnp.dot(rows, w_gate_ref[0], preferred_element_type=f32).astype(bf16)
    out_ref[1, 0] = jnp.dot(rows, w_up_ref[0], preferred_element_type=f32).astype(bf16)


def gate_up(blocks, w_gate, w_up):
    owned, width, hidden = w_gate.shape
    rows = sum(block.shape[0] for block in blocks)
    tile = 256
    weight = pl.BlockSpec((1, width, tile), lambda e, n: (e, 0, n))
    return pl.pallas_call(
        gate_up_kernel,
        grid=(owned, hidden // tile),
        in_specs=[pl.BlockSpec(block.shape, lambda e, n: (0, 0)) for block in blocks] + [weight, weight],
        out_specs=pl.BlockSpec((2, 1, rows, tile), lambda e, n: (0, e, 0, n)),
        out_shape=jax.ShapeDtypeStruct((2, owned, rows, hidden), bf16),
        scratch_shapes=[pltpu.VMEM((rows, width), bf16)],
        compiler_params=pltpu.CompilerParams(vmem_limit_bytes=16 * 1024 * 1024),
        cost_estimate=pl.CostEstimate(flops=rows * width * hidden, bytes_accessed=1024 * 1024, transcendentals=0),
    )(*blocks, w_gate, w_up)


def down_kernel(own_ref, other_ref, weight_ref, w_down_ref, out_ref, hidden_ref):
    owned, rows, hidden = own_ref.shape[1:]

    @pl.when(pl.program_id(0) == 0)
    def _():
        for e in range(owned):
            gate_pre = own_ref[0, e].astype(f32) + other_ref[0, e].astype(f32)
            up_pre = own_ref[1, e].astype(f32) + other_ref[1, e].astype(f32)
            silu = gate_pre / (1.0 + jnp.exp(-gate_pre))
            hidden_ref[:, e * hidden : (e + 1) * hidden] = (silu * up_pre * weight_ref[:, e : e + 1]).astype(bf16)

    out_ref[...] = jnp.dot(hidden_ref[...], w_down_ref[...], preferred_element_type=f32).astype(bf16)


def down(own, other, weight, w_down):
    owned, rows, hidden = own.shape[1:]
    width = w_down.shape[2]
    tile = 256
    whole = lambda array: pl.BlockSpec(array.shape, lambda n: (0,) * array.ndim)
    return pl.pallas_call(
        down_kernel,
        grid=(width // tile,),
        in_specs=[whole(own), whole(other), whole(weight), pl.BlockSpec((owned * hidden, tile), lambda n: (0, n))],
        out_specs=pl.BlockSpec((rows, tile), lambda n: (0, n)),
        out_shape=jax.ShapeDtypeStruct((rows, width), bf16),
        scratch_shapes=[pltpu.VMEM((rows, owned * hidden), bf16)],
        compiler_params=pltpu.CompilerParams(vmem_limit_bytes=24 * 1024 * 1024),
        cost_estimate=pl.CostEstimate(flops=rows * width * hidden, bytes_accessed=1024 * 1024, transcendentals=0),
    )(own, other, weight, w_down.reshape(owned * hidden, width))


class Ring:
    def __init__(self, count, token_rows):
        self.count, self.half = count, count // 2
        order = list(range(0, count, 2)) + list(range(count - 1, 0, -2)) if count == 8 else list(range(count))
        self.up = [(order[p], order[(p + 1) % count]) for p in range(count)]
        self.down = [(t, s) for s, t in self.up]
        table = []
        for core in range(2):
            for index in range(count):
                there = [order[(order.index(index) + o) % count] for o in range(count)]
                starts = [(t - core * self.half) % count * token_rows for t in there]
                table.append(starts + [t ^ index for t in there])
        here = lax.axis_index("ctx") * count + lax.axis_index("exp")
        row = lax.dynamic_slice_in_dim(jnp.array(table, jnp.int32), here, 1, 0)[0]
        self.rows_of, self.entry_of = row[:count], row[count:]

    def send(self, block, way):
        return lax.ppermute(block, "exp", self.up if way > 0 else self.down)


def after(blocks, work):
    if not work:
        return blocks
    held = lax.optimization_barrier((tuple(blocks), tuple(work)))
    return list(held[0])


def scatter_rows(ring, part):
    rows = part(ring.half).shape[0]
    cut, quarter = rows // 2, rows // 4
    stream = lambda block, k: block[k * cut : (k + 1) * cut]
    far = [stream(part(ring.half), k) for k in (0, 1)]
    going = [{1: ring.send(far[k][:quarter], 1), -1: ring.send(far[k][quarter:], -1)} for k in (0, 1)]
    for offset in range(ring.half - 1, 0, -1):
        for k in (0, 1):
            for way in (1, -1):
                own, come = stream(part(way * offset), k), going[k][way]
                add = lambda x, y: (x.astype(f32) + y.astype(f32)).astype(bf16)
                if offset < ring.half - 1:
                    block = add(own, come)
                elif way > 0:
                    block = jnp.concatenate([add(own[:quarter], come), own[quarter:]], axis=0)
                else:
                    block = jnp.concatenate([own[:quarter], add(own[quarter:], come)], axis=0)
                going[k][way] = ring.send(block, way)
    return [
        functools.reduce(jnp.add, [t.astype(f32) for t in (stream(part(0), k), going[k][1], going[k][-1])]) for k in (0, 1)
    ]


def per_device(
    count,
    resid,
    q_nope,
    q_rope,
    latent,
    k_rope,
    w_uk,
    w_uv,
    w_out,
    norm_gain,
    w_gate,
    w_up,
    w_down,
    routes,
    codes,
    block_order,
):
    token_rows, owned = resid.shape[0], w_gate.shape[0]
    cut = token_rows // 2
    ring = Ring(count, token_rows)
    core, index = lax.axis_index("ctx"), lax.axis_index("exp")
    swap = lambda block: lax.ppermute(block, "ctx", [(0, 1), (1, 0)])

    ropes = k_rope.T
    heads = attend(
        jnp.concatenate([core[None], block_order]), q_nope, q_rope, (latent, swap(latent)), (ropes, swap(ropes)), w_uk, w_uv
    )

    code_values = codes.astype(f32)
    route_weight = route_factor * code_values / jnp.sum(code_values, axis=1, keepdims=True)
    named = routes[:, :, None] == jnp.arange(count * owned, dtype=jnp.int32)
    routing = jnp.sum(jnp.where(named, route_weight[:, :, None], 0.0), axis=1)[None]
    for bit in [1 << b for b in range(count.bit_length() - 1)]:
        other = lax.ppermute(routing, "exp", [(i, i ^ bit) for i in range(count)])
        routing = jnp.concatenate([routing, other], axis=0)
    mine = lax.dynamic_slice_in_dim(routing, index * owned, owned, 2)
    entry = ring.entry_of[:, None] == jnp.arange(count, dtype=jnp.int32)[None, :]
    weights = jnp.sum(jnp.where(entry[:, :, None, None], mine[None], 0.0), axis=1)

    heads = jnp.concatenate([heads, swap(heads)], axis=0)

    @functools.cache
    def attention_part(offset):
        block = lax.dynamic_slice_in_dim(heads, ring.rows_of[offset % count], token_rows, 0)
        return lax.optimization_barrier(jnp.dot(block, w_out, preferred_element_type=f32).astype(bf16))

    states = scatter_rows(ring, attention_part)
    states = [resid[k * cut : (k + 1) * cut].astype(f32) + state for k, state in enumerate(states)]
    normed = []
    for state in states:
        squares = jnp.sum(state * state, axis=1)
        squares = squares + swap(squares)
        inverse_rms = lax.rsqrt(squares / D + norm_epsilon)
        normed.append((state * inverse_rms[:, None] * norm_gain).astype(bf16))
    normed = jnp.concatenate(normed, axis=0)

    arrived, pre, outcomes = {0: [normed]}, {}, {}

    def first_half(step):
        own = gate_up(arrived[step], w_gate, w_up)
        pre[step] = (own, swap(own))

    def second_half(step, behind):
        offsets = {0: (0,), ring.half: (ring.half,)}.get(step, (-step, step))
        weight = jnp.concatenate([weights[o % count] for o in offsets], axis=0)
        own = after([pre[step][0]], behind)[0]
        outcomes[step] = down(own, pre[step][1], weight, w_down)

    below = above = normed
    for step in range(1, ring.half + 1):
        if step > 1:
            work = [pre[step - 2][0]] + ([outcomes[step - 3]] if step > 2 else [])
            below, above = after([below, above], work)
        if step == ring.half:
            below, above = below[:cut], above[cut:]
        below, above = ring.send(below, 1), ring.send(above, -1)
        arrived[step] = [below, above]
        first_half(step - 1)
        if step > 1:
            second_half(step - 2, [pre[step - 1][0]])
    first_half(ring.half)
    second_half(ring.half - 1, [pre[ring.half][0]])
    second_half(ring.half, [])

    def expert_part(offset):
        outcome = outcomes[abs(offset)]
        if abs(offset) in (0, ring.half):
            return outcome
        return outcome[token_rows:] if offset > 0 else outcome[:token_rows]

    sums = scatter_rows(ring, expert_part)
    return jnp.concatenate([(state + total).astype(bf16) for state, total in zip(states, sums)], axis=0)


def solution(mesh):
    return jax.shard_map(
        functools.partial(per_device, mesh.shape["exp"]),
        mesh=mesh,
        in_specs=(
            P(("groups", "exp"), "ctx"),
            P(("groups", "ctx"), "exp"),
            P(("groups", "ctx"), "exp"),
            P(("groups", "ctx"), None),
            P(("groups", "ctx"), None),
            P(None, "exp"),
            P(None, "exp"),
            P("exp", "ctx"),
            P("ctx"),
            P("exp", "ctx", None),
            P("exp", "ctx", None),
            P("exp", None, "ctx"),
            P(("groups", "exp"), None),
            P(("groups", "exp"), None),
            P("groups"),
        ),
        out_specs=P(("groups", "exp"), "ctx"),
        check_vma=False,
    )
```

```python
import functools
import math

import jax
import jax.numpy as jnp
from jax import lax
from jax.experimental import pallas as pl
from jax.experimental.pallas import tpu as pltpu
from jax.sharding import PartitionSpec as P

D = 3584
NOPE = 128
ROPE = 64
VDIM = 128
BLOCK = 512

neg_large = -1e30
route_factor = 2.5
norm_epsilon = 1e-06
f32 = jnp.float32
bf16 = jnp.bfloat16


def attention_kernel(
    scalars_ref, q_nope_ref, q_rope_ref, own_latent_ref, other_latent_ref, own_rope_ref, other_rope_ref, w_uk_ref, w_uv_ref, out_ref
):
    core = scalars_ref[0]
    rank_of = lambda block: scalars_ref[1 + block]
    scale = (NOPE + ROPE) ** (-0.5) * math.log2(math.e)
    rows = q_nope_ref.shape[0]
    blocks = rows // BLOCK
    step = 256
    keys_t, values = [], []
    for latent_ref in (own_latent_ref, other_latent_ref):
        latent = latent_ref[...]
        keys_t.append(
            lax.dot_general(w_uk_ref[...], latent, (((0,), (1,)), ((), ())), preferred_element_type=f32).astype(bf16)
        )
        values.append(jnp.dot(latent, w_uv_ref[...], preferred_element_type=f32).astype(bf16))
    ropes = (own_rope_ref[...], other_rope_ref[...])
    blank = jnp.zeros_like(ropes[0])
    ahead = lax.broadcasted_iota(jnp.int32, (step, BLOCK), 1) - lax.broadcasted_iota(jnp.int32, (step, BLOCK), 0)
    for head in range(2):
        cols = slice(head * NOPE, (head + 1) * NOPE)
        key_cat = [
            jnp.concatenate([keys[cols, :]] + ([rope, blank] if head == 0 else [blank, rope]), axis=0)
            for keys, rope in zip(keys_t, ropes)
        ]
        for first in range(0, rows, step):
            part = slice(first, first + step)
            query = jnp.concatenate([q_nope_ref[part, cols], q_rope_ref[part, :]], axis=1)
            query_rank = rank_of(core * blocks + first // BLOCK)
            scores = []
            for side in (0, 1):
                whole = jnp.dot(query, key_cat[side], preferred_element_type=f32)
                for block in range(blocks):
                    owner = core if side == 0 else 1 - core
                    reach = (query_rank - rank_of(owner * blocks + block)) * BLOCK + first % BLOCK
                    piece = whole[:, block * BLOCK : (block + 1) * BLOCK]
                    scores.append(jnp.where(ahead <= reach, piece, neg_large))
            best = functools.reduce(jnp.maximum, [jnp.max(piece, axis=1, keepdims=True) for piece in scores])
            probs = [jnp.exp2((piece - best) * scale) for piece in scores]
            total = functools.reduce(jnp.add, [jnp.sum(piece, axis=1, keepdims=True) for piece in probs])
            summed = 0.0
            for number, piece in enumerate(probs):
                held = values[number // blocks][number % blocks * BLOCK : (number % blocks + 1) * BLOCK, cols]
                summed = summed + jnp.dot(piece.astype(bf16), held, preferred_element_type=f32)
            out_ref[part, cols] = (summed / total).astype(bf16)


def attend(scalars, q_nope, q_rope, latents, ropes, w_uk, w_uv):
    rows, keys = q_nope.shape[0], 2 * latents[0].shape[0]
    pairs = q_nope.shape[1] // (2 * NOPE)
    whole = lambda array: pl.BlockSpec(array.shape, lambda h, s: (0, 0))
    column = lambda array, width: pl.BlockSpec((array.shape[0], width), lambda h, s: (0, h))
    return pl.pallas_call(
        attention_kernel,
        grid_spec=pltpu.PrefetchScalarGridSpec(
            num_scalar_prefetch=1,
            grid=(pairs,),
            in_specs=[column(q_nope, 2 * NOPE), column(q_rope, 2 * ROPE)]
            + [whole(array) for array in (*latents, *ropes)]
            + [column(w_uk, 2 * NOPE), column(w_uv, 2 * VDIM)],
            out_specs=column(q_nope, 2 * VDIM),
        ),
        out_shape=jax.ShapeDtypeStruct((rows, q_nope.shape[1]), bf16),
        compiler_params=pltpu.CompilerParams(vmem_limit_bytes=60 * 1024 * 1024),
        cost_estimate=pl.CostEstimate(
            flops=2 * rows * keys * pairs * 2 * 384, bytes_accessed=8 * 1024 * 1024, transcendentals=rows * keys * pairs * 2
        ),
    )(scalars, q_nope, q_rope, *latents, *ropes, w_uk, w_uv)


class Ring:
    def __init__(self, count):
        self.count, self.half = count, count // 2
        self.grid = count == 8
        order = [(2 * p if p < count // 2 else 2 * count - 1 - 2 * p) if self.grid else p for p in range(count)]
        self.up = [(order[p], order[(p + 1) % count]) for p in range(count)]
        self.down = [(t, s) for s, t in self.up]
        index = lax.axis_index("exp")
        self.place = jnp.where(index % 2 == 0, index // 2, count - 1 - index // 2) if self.grid else index

    def index_at(self, place):
        return jnp.where(place < self.half, 2 * place, 2 * self.count - 1 - 2 * place) if self.grid else place

    def at(self, offset):
        return self.index_at(lax.rem(self.place + offset, self.count))

    def send(self, block, way):
        return lax.ppermute(block, "exp", self.up if way > 0 else self.down)


def after(blocks, work):
    if not work:
        return blocks
    held = lax.optimization_barrier((tuple(blocks), tuple(work)))
    return list(held[0])


def scatter_rows(ring, part):
    add = lambda *terms: functools.reduce(jnp.add, [t.astype(f32) for t in terms])
    far = part(ring.half, [])
    sent = [far]
    cut = far.shape[0] // 2
    going = {1: ring.send(far[:cut], 1), -1: ring.send(far[cut:], -1)}
    for offset in range(ring.half - 1, 0, -1):
        behind, sent = sent, []
        for way in (1, -1):
            own, come = part(way * offset, behind), going[way]
            if offset < ring.half - 1:
                block = add(own, come).astype(bf16)
            elif way > 0:
                block = jnp.concatenate([add(own[:cut], come).astype(bf16), own[cut:]], axis=0)
            else:
                block = jnp.concatenate([own[:cut], add(own[cut:], come).astype(bf16)], axis=0)
            sent.append(block)
            going[way] = ring.send(block, way)
    return add(part(0, sent), going[1], going[-1])


def per_device(
    count,
    resid,
    q_nope,
    q_rope,
    latent,
    k_rope,
    w_uk,
    w_uv,
    w_out,
    norm_gain,
    w_gate,
    w_up,
    w_down,
    routes,
    codes,
    block_order,
):
    token_rows, owned = resid.shape[0], w_gate.shape[0]
    cut = token_rows // 2
    ring = Ring(count)
    core, index = lax.axis_index("ctx"), lax.axis_index("exp")
    swap = lambda block: lax.ppermute(block, "ctx", [(0, 1), (1, 0)])

    ropes = k_rope.T
    heads = attend(
        jnp.concatenate([core[None], block_order]), q_nope, q_rope, (latent, swap(latent)), (ropes, swap(ropes)), w_uk, w_uv
    )

    heads = jnp.concatenate([heads, swap(heads)], axis=0)

    @functools.cache
    def attention_term(offset):
        first = jnp.bitwise_and(ring.at(offset % count) - core * ring.half, count - 1) * token_rows
        block = lax.dynamic_slice_in_dim(heads, first, token_rows, 0, allow_negative_indices=False)
        return lax.optimization_barrier(jnp.dot(block, w_out, preferred_element_type=f32).astype(bf16))

    code_values = codes.astype(f32)
    route_weight = route_factor * code_values / jnp.sum(code_values, axis=1, keepdims=True)
    named = routes[None] == jnp.arange(count * owned, dtype=jnp.int32)[:, None, None]
    routing = jnp.sum(jnp.where(named, route_weight[None], 0.0), axis=2)[None]
    (routing,) = after([routing], [attention_term(1)])
    for bit in [1 << b for b in range(count.bit_length() - 1)]:
        other = lax.ppermute(routing, "exp", [(i, i ^ bit) for i in range(count)])
        routing = jnp.concatenate([routing, other], axis=0)
    mine = lax.dynamic_slice_in_dim(routing, index * owned, owned, 1, allow_negative_indices=False)
    offsets = jnp.arange(count, dtype=jnp.int32)
    entry = jnp.bitwise_xor(ring.at(offsets), index)[:, None] == offsets[None, :]
    weights = jnp.sum(jnp.where(entry[:, :, None, None], mine[None], 0.0), axis=1)

    residual_state = resid.astype(f32) + scatter_rows(ring, lambda offset, behind: attention_term(offset))
    squares = jnp.sum(residual_state * residual_state, axis=1)
    squares = squares + swap(squares)
    inverse_rms = lax.rsqrt(squares / D + norm_epsilon)
    normed = (residual_state * inverse_rms[:, None] * norm_gain).astype(bf16)

    def before_hidden(rows):
        product = lambda weight: jnp.einsum("td,ldf->ltf", rows, weight, preferred_element_type=f32).astype(bf16)
        own = [product(w_gate), product(w_up)]
        return own, [swap(pre) for pre in own]

    def after_hidden(own, other, weight):
        gate_pre, up_pre = [mine.astype(f32) + theirs.astype(f32) for mine, theirs in zip(own, other)]
        hidden = (jax.nn.silu(gate_pre) * up_pre * weight[:, :, None]).astype(bf16)
        return functools.reduce(
            jnp.add, [jnp.dot(hidden[e], w_down[e], preferred_element_type=f32) for e in range(owned)]
        ).astype(bf16)

    pre = [before_hidden(normed)]
    below = above = normed
    for step in range(1, ring.half + 1):
        if step > 1:
            below, above = after([below, above], pre[step - 2][0])
        if step == ring.half:
            below, above = below[:cut], above[cut:]
        below, above = ring.send(below, 1), ring.send(above, -1)
        rows = jnp.concatenate([below, above], axis=0)
        if step == ring.half:
            (rows,) = after([rows], pre[step - 1][0])
        pre.append(before_hidden(rows))

    outcomes = {}

    def expert_term(offset, behind):
        step = abs(offset)
        if step not in outcomes:
            weight = weights[step]
            if 0 < step < ring.half:
                weight = jnp.concatenate([weights[count - step], weight], axis=1)
            outcomes[step] = after_hidden(after(pre[step][0], behind), pre[step][1], weight)
        if step in (0, ring.half):
            return outcomes[step]
        return outcomes[step][token_rows:] if offset > 0 else outcomes[step][:token_rows]

    return (residual_state + scatter_rows(ring, expert_term)).astype(bf16)


def solution(mesh):
    return jax.shard_map(
        functools.partial(per_device, mesh.shape["exp"]),
        mesh=mesh,
        in_specs=(
            P(("groups", "exp"), "ctx"),
            P(("groups", "ctx"), "exp"),
            P(("groups", "ctx"), "exp"),
            P(("groups", "ctx"), None),
            P(("groups", "ctx"), None),
            P(None, "exp"),
            P(None, "exp"),
            P("exp", "ctx"),
            P("ctx"),
            P("exp", "ctx", None),
            P("exp", "ctx", None),
            P("exp", None, "ctx"),
            P(("groups", "exp"), None),
            P(("groups", "exp"), None),
            P("groups"),
        ),
        out_specs=P(("groups", "exp"), "ctx"),
        check_vma=False,
    )
```

```python
import functools
import math

import jax
import jax.numpy as jnp
from jax import lax
from jax.experimental import pallas as pl
from jax.experimental.pallas import tpu as pltpu
from jax.sharding import PartitionSpec as P

D = 3584
NOPE = 128
ROPE = 64
VDIM = 128
BLOCK = 512

neg_large = -1e30
route_factor = 2.5
norm_epsilon = 1e-06
f32 = jnp.float32
bf16 = jnp.bfloat16


def attention_kernel(
    scalars_ref, q_nope_ref, q_rope_ref, own_latent_ref, other_latent_ref, own_rope_ref, other_rope_ref, w_uk_ref, w_uv_ref, out_ref
):
    core = scalars_ref[0]
    rank_of = lambda block: scalars_ref[1 + block]
    scale = (NOPE + ROPE) ** (-0.5) * math.log2(math.e)
    rows = q_nope_ref.shape[0]
    blocks = rows // BLOCK
    step = 256
    keys_t, values = [], []
    for latent_ref in (own_latent_ref, other_latent_ref):
        latent = latent_ref[...]
        keys_t.append(
            lax.dot_general(w_uk_ref[...], latent, (((0,), (1,)), ((), ())), preferred_element_type=f32).astype(bf16)
        )
        values.append(jnp.dot(latent, w_uv_ref[...], preferred_element_type=f32).astype(bf16))
    ropes = (own_rope_ref[...], other_rope_ref[...])
    blank = jnp.zeros_like(ropes[0])
    diagonal = lax.broadcasted_iota(jnp.int32, (step, step), 1) <= lax.broadcasted_iota(jnp.int32, (step, step), 0)
    for head in range(2):
        cols = slice(head * NOPE, (head + 1) * NOPE)
        key_cat = [
            jnp.concatenate([keys[cols, :]] + ([rope, blank] if head == 0 else [blank, rope]), axis=0)
            for keys, rope in zip(keys_t, ropes)
        ]
        value_cat = [jnp.concatenate([held[:, cols], jnp.ones_like(held[:, cols])], axis=1) for held in values]
        for first in range(0, rows, step):
            part = slice(first, first + step)
            query = jnp.concatenate([q_nope_ref[part, cols], q_rope_ref[part, :]], axis=1)
            query_block, inside = first // BLOCK, first % BLOCK
            scores = []
            for side in (0, 1):
                owner = core if side == 0 else 1 - core
                for block in range(blocks):
                    start = block * BLOCK
                    if side == 0 and block == query_block:
                        seen = slice(start, start + inside + step)
                        piece = jnp.dot(query, key_cat[side][:, seen], preferred_element_type=f32)
                        last = jnp.where(diagonal, piece[:, inside:], neg_large)
                        piece = jnp.concatenate([piece[:, :inside], last], axis=1) if inside else last
                    else:
                        seen = slice(start, start + BLOCK)
                        piece = jnp.dot(query, key_cat[side][:, seen], preferred_element_type=f32)
                        earlier = rank_of(owner * blocks + block) < rank_of(core * blocks + query_block)
                        piece = piece + jnp.where(earlier, 0.0, neg_large)
                    scores.append((side, seen, piece))
            best = functools.reduce(jnp.maximum, [jnp.max(piece, axis=1, keepdims=True) for _, _, piece in scores])
            summed = 0.0
            for side, seen, piece in scores:
                probs = jnp.exp2((piece - best) * scale).astype(bf16)
                summed = summed + jnp.dot(probs, value_cat[side][seen, :], preferred_element_type=f32)
            out_ref[part, cols] = (summed[:, :VDIM] / summed[:, VDIM:]).astype(bf16)


def attend(scalars, q_nope, q_rope, latents, ropes, w_uk, w_uv):
    rows, keys = q_nope.shape[0], 2 * latents[0].shape[0]
    pairs = q_nope.shape[1] // (2 * NOPE)
    whole = lambda array: pl.BlockSpec(array.shape, lambda h, s: (0, 0))
    column = lambda array, width: pl.BlockSpec((array.shape[0], width), lambda h, s: (0, h))
    return pl.pallas_call(
        attention_kernel,
        grid_spec=pltpu.PrefetchScalarGridSpec(
            num_scalar_prefetch=1,
            grid=(pairs,),
            in_specs=[column(q_nope, 2 * NOPE), column(q_rope, 2 * ROPE)]
            + [whole(array) for array in (*latents, *ropes)]
            + [column(w_uk, 2 * NOPE), column(w_uv, 2 * VDIM)],
            out_specs=column(q_nope, 2 * VDIM),
        ),
        out_shape=jax.ShapeDtypeStruct((rows, q_nope.shape[1]), bf16),
        compiler_params=pltpu.CompilerParams(vmem_limit_bytes=60 * 1024 * 1024),
        cost_estimate=pl.CostEstimate(
            flops=2 * rows * keys * pairs * 2 * 384, bytes_accessed=8 * 1024 * 1024, transcendentals=rows * keys * pairs * 2
        ),
    )(scalars, q_nope, q_rope, *latents, *ropes, w_uk, w_uv)


class Ring:
    def __init__(self, count):
        self.count, self.half = count, count // 2
        self.grid = count == 8
        order = [(2 * p if p < count // 2 else 2 * count - 1 - 2 * p) if self.grid else p for p in range(count)]
        self.up = [(order[p], order[(p + 1) % count]) for p in range(count)]
        self.down = [(t, s) for s, t in self.up]
        index = lax.axis_index("exp")
        self.place = jnp.where(index % 2 == 0, index // 2, count - 1 - index // 2) if self.grid else index

    def index_at(self, place):
        return jnp.where(place < self.half, 2 * place, 2 * self.count - 1 - 2 * place) if self.grid else place

    def at(self, offset):
        return self.index_at(lax.rem(self.place + offset, self.count))

    def send(self, block, way):
        return lax.ppermute(block, "exp", self.up if way > 0 else self.down)


def after(blocks, work):
    if not work:
        return blocks
    held = lax.optimization_barrier((tuple(blocks), tuple(work)))
    return list(held[0])


def scatter_rows(ring, part):
    add = lambda *terms: functools.reduce(jnp.add, [t.astype(f32) for t in terms])
    far = part(ring.half, [])
    sent = [far]
    cut = far.shape[0] // 2
    going = {1: ring.send(far[:cut], 1), -1: ring.send(far[cut:], -1)}
    for offset in range(ring.half - 1, 0, -1):
        behind, sent = sent, []
        for way in (1, -1):
            own, come = part(way * offset, behind), going[way]
            if offset < ring.half - 1:
                block = add(own, come).astype(bf16)
            elif way > 0:
                block = jnp.concatenate([add(own[:cut], come).astype(bf16), own[cut:]], axis=0)
            else:
                block = jnp.concatenate([own[:cut], add(own[cut:], come).astype(bf16)], axis=0)
            sent.append(block)
            going[way] = ring.send(block, way)
    return add(part(0, sent), going[1], going[-1])


def per_device(
    count,
    resid,
    q_nope,
    q_rope,
    latent,
    k_rope,
    w_uk,
    w_uv,
    w_out,
    norm_gain,
    w_gate,
    w_up,
    w_down,
    routes,
    codes,
    block_order,
):
    token_rows, owned = resid.shape[0], w_gate.shape[0]
    cut = token_rows // 2
    ring = Ring(count)
    core, index = lax.axis_index("ctx"), lax.axis_index("exp")
    swap = lambda block: lax.ppermute(block, "ctx", [(0, 1), (1, 0)])

    ropes = k_rope.T
    heads = attend(
        jnp.concatenate([core[None], block_order]), q_nope, q_rope, (latent, swap(latent)), (ropes, swap(ropes)), w_uk, w_uv
    )

    heads = jnp.concatenate([heads, swap(heads)], axis=0)

    @functools.cache
    def attention_term(offset):
        first = jnp.bitwise_and(ring.at(offset % count) - core * ring.half, count - 1) * token_rows
        block = lax.dynamic_slice_in_dim(heads, first, token_rows, 0, allow_negative_indices=False)
        return lax.optimization_barrier(jnp.dot(block, w_out, preferred_element_type=f32).astype(bf16))

    ring_blocks = []

    def attention_part(offset, behind):
        if offset == max(ring.half - 2, 0):
            ring_blocks.extend(behind)
        return attention_term(offset)

    residual_state = resid.astype(f32) + scatter_rows(ring, attention_part)

    code_values = codes.astype(f32)
    route_weight = route_factor * code_values / jnp.sum(code_values, axis=1, keepdims=True)
    named = routes[None] == jnp.arange(count * owned, dtype=jnp.int32)[:, None, None]
    routing = jnp.sum(jnp.where(named, route_weight[None], 0.0), axis=2)[None]
    (routing,) = after([routing], ring_blocks)
    for bit in [1 << b for b in range(count.bit_length() - 1)]:
        other = lax.ppermute(routing, "exp", [(i, i ^ bit) for i in range(count)])
        routing = jnp.concatenate([routing, other], axis=0)
    mine = lax.dynamic_slice_in_dim(routing, index * owned, owned, 1, allow_negative_indices=False)
    offsets = jnp.arange(count, dtype=jnp.int32)
    entry = jnp.bitwise_xor(ring.at(offsets), index)[:, None] == offsets[None, :]
    weights = jnp.sum(jnp.where(entry[:, :, None, None], mine[None], 0.0), axis=1)

    squares = jnp.sum(residual_state * residual_state, axis=1)
    squares = squares + swap(squares)
    inverse_rms = lax.rsqrt(squares / D + norm_epsilon)
    normed = (residual_state * inverse_rms[:, None] * norm_gain).astype(bf16)

    def before_hidden(rows):
        product = lambda weight: jnp.einsum("td,ldf->ltf", rows, weight, preferred_element_type=f32).astype(bf16)
        own = [product(w_gate), product(w_up)]
        return own, [swap(pre) for pre in own]

    def after_hidden(own, other, weight):
        gate_pre, up_pre = [mine.astype(f32) + theirs.astype(f32) for mine, theirs in zip(own, other)]
        hidden = (jax.nn.silu(gate_pre) * up_pre * weight[:, :, None]).astype(bf16)
        return functools.reduce(
            jnp.add, [jnp.dot(hidden[e], w_down[e], preferred_element_type=f32) for e in range(owned)]
        ).astype(bf16)

    pre = [before_hidden(normed)]
    below = above = normed
    for step in range(1, ring.half + 1):
        if step > 1:
            below, above = after([below, above], pre[step - 2][0] + (pre[step - 4][1] if step > 3 else []))
        if step == ring.half:
            below, above = below[:cut], above[cut:]
        below, above = ring.send(below, 1), ring.send(above, -1)
        rows = jnp.concatenate([below, above], axis=0)
        if step == ring.half:
            (rows,) = after([rows], pre[step - 1][0] + (pre[step - 3][1] if step > 2 else []))
        pre.append(before_hidden(rows))

    outcomes = {}

    def outcome(step, behind):
        weight = weights[step]
        if 0 < step < ring.half:
            weight = jnp.concatenate([weights[count - step], weight], axis=1)
        outcomes[step] = after_hidden(after(pre[step][0], behind), pre[step][1], weight)

    def expert_term(offset, behind):
        step = abs(offset)
        if step == ring.half and step > 1:
            outcome(step - 1, pre[step][0] + pre[step - 2][1])
            behind = [outcomes[step - 1]]
        if step not in outcomes:
            outcome(step, behind)
        if step in (0, ring.half):
            return outcomes[step]
        return outcomes[step][token_rows:] if offset > 0 else outcomes[step][:token_rows]

    return (residual_state + scatter_rows(ring, expert_term)).astype(bf16)


def solution(mesh):
    return jax.shard_map(
        functools.partial(per_device, mesh.shape["exp"]),
        mesh=mesh,
        in_specs=(
            P(("groups", "exp"), "ctx"),
            P(("groups", "ctx"), "exp"),
            P(("groups", "ctx"), "exp"),
            P(("groups", "ctx"), None),
            P(("groups", "ctx"), None),
            P(None, "exp"),
            P(None, "exp"),
            P("exp", "ctx"),
            P("ctx"),
            P("exp", "ctx", None),
            P("exp", "ctx", None),
            P("exp", None, "ctx"),
            P(("groups", "exp"), None),
            P(("groups", "exp"), None),
            P("groups"),
        ),
        out_specs=P(("groups", "exp"), "ctx"),
        check_vma=False,
    )
```

```python
import functools
import math

import jax
import jax.numpy as jnp
from jax import lax
from jax.experimental import pallas as pl
from jax.experimental.pallas import tpu as pltpu
from jax.sharding import PartitionSpec as P

D = 3584
NOPE = 128
ROPE = 64
VDIM = 128
BLOCK = 512
LANES = 128

neg_large = -1e30
route_factor = 2.5
norm_epsilon = 1e-06
f32 = jnp.float32
bf16 = jnp.bfloat16


def attention_kernel(
    scalars_ref, q_nope_ref, q_rope_ref, own_latent_ref, other_latent_ref, own_rope_ref, other_rope_ref, w_uk_ref, w_uv_ref, out_ref
):
    core = scalars_ref[0]
    rank_of = lambda block: scalars_ref[1 + block]
    scale = (NOPE + ROPE) ** (-0.5) * math.log2(math.e)
    rows = q_nope_ref.shape[0]
    blocks = rows // BLOCK
    step = 256
    keys_t, values = [], []
    for latent_ref in (own_latent_ref, other_latent_ref):
        latent = latent_ref[...]
        keys_t.append(
            lax.dot_general(w_uk_ref[...], latent, (((0,), (1,)), ((), ())), preferred_element_type=f32).astype(bf16)
        )
        values.append(jnp.dot(latent, w_uv_ref[...], preferred_element_type=f32).astype(bf16))
    ropes = (own_rope_ref[...], other_rope_ref[...])
    blank = jnp.zeros_like(ropes[0])
    diagonal = lax.broadcasted_iota(jnp.int32, (step, step), 1) <= lax.broadcasted_iota(jnp.int32, (step, step), 0)
    key_cat, value_cat = [], []
    for head in range(2):
        cols = slice(head * NOPE, (head + 1) * NOPE)
        key_cat.append([
            jnp.concatenate([keys[cols, :]] + ([rope, blank] if head == 0 else [blank, rope]), axis=0)
            for keys, rope in zip(keys_t, ropes)
        ])
        value_cat.append([jnp.concatenate([held[:, cols], jnp.ones_like(held[:, cols])], axis=1) for held in values])

    def score(head, first):
        cols, part = slice(head * NOPE, (head + 1) * NOPE), slice(first, first + step)
        query = jnp.concatenate([q_nope_ref[part, cols], q_rope_ref[part, :]], axis=1)
        query_block, inside = first // BLOCK, first % BLOCK
        scores = []
        for side in (0, 1):
            owner = core if side == 0 else 1 - core
            for block in range(blocks):
                start = block * BLOCK
                if side == 0 and block == query_block:
                    seen = slice(start, start + inside + step)
                    piece = jnp.dot(query, key_cat[head][side][:, seen], preferred_element_type=f32)
                    last = jnp.where(diagonal, piece[:, inside:], neg_large)
                    piece = jnp.concatenate([piece[:, :inside], last], axis=1) if inside else last
                else:
                    seen = slice(start, start + BLOCK)
                    piece = jnp.dot(query, key_cat[head][side][:, seen], preferred_element_type=f32)
                    earlier = rank_of(owner * blocks + block) < rank_of(core * blocks + query_block)
                    piece = piece + jnp.where(earlier, 0.0, neg_large)
                scores.append((side, seen, piece))
        return scores

    units = [(head, first) for first in range(0, rows, step) for head in range(2)]
    ready = score(*units[0])
    for number, (head, first) in enumerate(units):
        scores = ready
        if number + 1 < len(units):
            ready = score(*units[number + 1])
        best = functools.reduce(jnp.maximum, [jnp.max(piece, axis=1, keepdims=True) for _, _, piece in scores])
        summed = 0.0
        for side, seen, piece in scores:
            probs = jnp.exp2((piece - best) * scale).astype(bf16)
            summed = summed + jnp.dot(probs, value_cat[head][side][seen, :], preferred_element_type=f32)
        out_ref[first : first + step, head * VDIM : (head + 1) * VDIM] = (summed[:, :VDIM] / summed[:, VDIM:]).astype(bf16)


def attend(scalars, q_nope, q_rope, latents, ropes, w_uk, w_uv):
    rows, keys = q_nope.shape[0], 2 * latents[0].shape[0]
    pairs = q_nope.shape[1] // (2 * NOPE)
    whole = lambda array: pl.BlockSpec(array.shape, lambda h, s: (0, 0))
    column = lambda array, width: pl.BlockSpec((array.shape[0], width), lambda h, s: (0, h))
    return pl.pallas_call(
        attention_kernel,
        grid_spec=pltpu.PrefetchScalarGridSpec(
            num_scalar_prefetch=1,
            grid=(pairs,),
            in_specs=[column(q_nope, 2 * NOPE), column(q_rope, 2 * ROPE)]
            + [whole(array) for array in (*latents, *ropes)]
            + [column(w_uk, 2 * NOPE), column(w_uv, 2 * VDIM)],
            out_specs=column(q_nope, 2 * VDIM),
        ),
        out_shape=jax.ShapeDtypeStruct((rows, q_nope.shape[1]), bf16),
        compiler_params=pltpu.CompilerParams(vmem_limit_bytes=60 * 1024 * 1024),
        cost_estimate=pl.CostEstimate(
            flops=2 * rows * keys * pairs * 2 * 384, bytes_accessed=8 * 1024 * 1024, transcendentals=rows * keys * pairs * 2
        ),
    )(scalars, q_nope, q_rope, *latents, *ropes, w_uk, w_uv)


class Ring:
    def __init__(self, count, rows):
        self.count, self.half, self.cut = count, count // 2, rows // 2
        self.grid = count == 8
        order = [(2 * p if p < count // 2 else 2 * count - 1 - 2 * p) if self.grid else p for p in range(count)]
        self.up = [(order[p], order[(p + 1) % count]) for p in range(count)]
        self.down = [(t, s) for s, t in self.up]
        index = lax.axis_index("exp")
        self.place = jnp.where(index % 2 == 0, index // 2, count - 1 - index // 2) if self.grid else index

    def index_at(self, place):
        return jnp.where(place < self.half, 2 * place, 2 * self.count - 1 - 2 * place) if self.grid else place

    def at(self, offset):
        return self.index_at(lax.rem(self.place + offset, self.count))

    def send(self, block, way):
        return lax.ppermute(block, "exp", self.up if way > 0 else self.down)


def after(blocks, work):
    if not work:
        return blocks
    held = lax.optimization_barrier((tuple(blocks), tuple(work)))
    return list(held[0])


def scatter_rows(ring, part):
    add = lambda *terms: functools.reduce(jnp.add, [t.astype(f32) for t in terms])
    low, high, every = slice(0, ring.cut), slice(ring.cut, 2 * ring.cut), slice(0, 2 * ring.cut)
    near = ring.half - 1
    far = part(ring.half, every, [])
    sent = {way: [far[rows], part(way * near, other, [])] for way, rows, other in ((1, low, high), (-1, high, low))}
    sent = {1: jnp.concatenate(sent[1], axis=0), -1: jnp.concatenate(sent[-1][::-1], axis=0)}
    come = {way: ring.send(sent[way], way) for way in (1, -1)}
    for offset in range(near, 0, -1):
        behind, sent, went = list(sent.values()), {}, come
        come = {}
        for way, rows in ((1, low), (-1, high)):
            if offset < near:
                sent[way] = add(part(way * offset, every, behind), went[way]).astype(bf16)
                come[way] = ring.send(sent[way], way)
            else:
                sent[way] = add(part(way * offset, rows, behind), went[way][rows]).astype(bf16)
                joined = ring.send(sent[way], way)
                come[way] = jnp.concatenate([joined, went[1][high]] if way > 0 else [went[-1][low], joined], axis=0)
    return add(part(0, every, list(sent.values())), come[1], come[-1])


def per_device(
    count,
    resid,
    q_nope,
    q_rope,
    latent,
    k_rope,
    w_uk,
    w_uv,
    w_out,
    norm_gain,
    w_gate,
    w_up,
    w_down,
    routes,
    codes,
    block_order,
):
    token_rows, owned = resid.shape[0], w_gate.shape[0]
    cut = token_rows // 2
    ring = Ring(count, token_rows)
    core, index = lax.axis_index("ctx"), lax.axis_index("exp")
    swap = lambda block: lax.ppermute(block, "ctx", [(0, 1), (1, 0)])

    ropes = k_rope.T
    heads = attend(
        jnp.concatenate([core[None], block_order]), q_nope, q_rope, (latent, swap(latent)), (ropes, swap(ropes)), w_uk, w_uv
    )

    heads = jnp.concatenate([heads, swap(heads)], axis=0)

    @functools.cache
    def attention_term(offset):
        first = jnp.bitwise_and(ring.at(offset % count) - core * ring.half, count - 1) * token_rows
        block = lax.dynamic_slice_in_dim(heads, first, token_rows, 0, allow_negative_indices=False)
        return lax.optimization_barrier(jnp.dot(block, w_out, preferred_element_type=f32).astype(bf16))

    residual_state = resid.astype(f32) + scatter_rows(ring, lambda offset, rows, behind: attention_term(offset)[rows])

    squares = jnp.sum(residual_state * residual_state, axis=1)
    squares = squares + swap(squares)
    inverse_rms = lax.rsqrt(squares / D + norm_epsilon)
    normed = (residual_state * inverse_rms[:, None] * norm_gain).astype(bf16)

    code_values = codes.astype(f32)
    route_weight = route_factor * code_values / jnp.sum(code_values, axis=1, keepdims=True)
    experts = jnp.arange(count * owned, dtype=jnp.int32)
    weights = jnp.sum(jnp.where(routes[:, :, None] == experts, route_weight[:, :, None], 0.0), axis=1)
    upper = weights.astype(bf16)
    lower = (weights - upper.astype(f32)).astype(bf16)
    spare = jnp.zeros((token_rows, LANES - 2 * count * owned), bf16)
    normed = jnp.concatenate([normed, upper, lower, spare], axis=1)
    width = resid.shape[1]

    def before_hidden(rows):
        product = lambda weight: jnp.einsum("td,ldf->ltf", rows, weight, preferred_element_type=f32).astype(bf16)
        extra = rows[:, width:].astype(f32)
        rows = rows[:, :width]
        own = [product(w_gate), product(w_up)]
        lane = lax.rem(jnp.arange(LANES, dtype=jnp.int32), count * owned)
        weight = [jnp.sum(jnp.where(lane == index * owned + e, extra, 0.0), axis=1) for e in range(owned)]
        return own, [swap(pre) for pre in own], jnp.stack(weight)

    def after_hidden(own, other, weight):
        gate_pre, up_pre = [mine.astype(f32) + theirs.astype(f32) for mine, theirs in zip(own, other)]
        hidden = (jax.nn.silu(gate_pre) * up_pre * weight[:, :, None]).astype(bf16)
        return functools.reduce(
            jnp.add, [jnp.dot(hidden[e], w_down[e], preferred_element_type=f32) for e in range(owned)]
        ).astype(bf16)

    near, half = ring.half - 1, ring.half
    pre = {0: before_hidden(normed)}
    below = above = normed
    for step in range(1, near):
        if step > 1:
            below, above = after([below, above], pre[step - 2][0] + (pre[step - 4][1] if step > 3 else []))
        below, above = ring.send(below, 1), ring.send(above, -1)
        if step < near - 1:
            pre[step] = before_hidden(jnp.concatenate([below, above], axis=0))
    below, above = after([below, above], pre[near - 2][0])
    first = [ring.send(below[:cut], 1), ring.send(above[cut:], -1)]
    ahead = after(first, pre[near - 3][1])
    last = [
        ring.send(jnp.concatenate([ahead[0], below[cut:]], axis=0), 1),
        ring.send(jnp.concatenate([above[:cut], ahead[1]], axis=0), -1),
    ]
    pre["first"] = before_hidden(jnp.concatenate(first, axis=0))
    last = after(last, pre["first"][0])
    pre[half] = before_hidden(jnp.concatenate([last[0][:cut], last[1][cut:]], axis=0))

    outcomes = {}

    def outcome(name, behind):
        if name not in outcomes:
            own, other, weight = pre[name]
            outcomes[name] = after_hidden(after(own, behind), other, weight)
        return outcomes[name]

    def expert_term(offset, rows, behind):
        step = abs(offset)
        if step == half:
            outcome("first", pre[half][0] + pre[near - 2][1])
            outcome(half, [outcomes["first"]])
            return outcomes[half]
        if step == 0:
            return outcome(0, behind)
        if step < near:
            return outcome(step, behind)[token_rows:] if offset > 0 else outcome(step, behind)[:token_rows]
        low = rows.start == 0
        if "second" not in pre and low == (offset > 0):
            later = after([*last, below, above], behind)
            pre["second"] = before_hidden(jnp.concatenate([later[0][cut:], later[1][:cut]], axis=0))
            if near > 1:
                later = after(later, pre["second"][0])
                pre[near - 1] = before_hidden(jnp.concatenate(later[2:], axis=0))
        if low == (offset > 0):
            return outcome("second", behind)[cut:] if low else outcome("second", behind)[:cut]
        return outcomes["first"][:cut] if low else outcomes["first"][cut:]

    return (residual_state + scatter_rows(ring, expert_term)).astype(bf16)


def solution(mesh):
    return jax.shard_map(
        functools.partial(per_device, mesh.shape["exp"]),
        mesh=mesh,
        in_specs=(
            P(("groups", "exp"), "ctx"),
            P(("groups", "ctx"), "exp"),
            P(("groups", "ctx"), "exp"),
            P(("groups", "ctx"), None),
            P(("groups", "ctx"), None),
            P(None, "exp"),
            P(None, "exp"),
            P("exp", "ctx"),
            P("ctx"),
            P("exp", "ctx", None),
            P("exp", "ctx", None),
            P("exp", None, "ctx"),
            P(("groups", "exp"), None),
            P(("groups", "exp"), None),
            P("groups"),
        ),
        out_specs=P(("groups", "exp"), "ctx"),
        check_vma=False,
    )
```

```python
import functools
import math

import jax
import jax.numpy as jnp
from jax import lax
from jax.experimental import pallas as pl
from jax.experimental.pallas import tpu as pltpu
from jax.sharding import PartitionSpec as P

D = 3584
NOPE = 128
ROPE = 64
VDIM = 128
BLOCK = 512

neg_large = -1e30
route_factor = 2.5
norm_epsilon = 1e-06
f32 = jnp.float32
bf16 = jnp.bfloat16


def attention_kernel(
    order_ref, q_nope_ref, q_rope_ref, own_latent_ref, other_latent_ref, own_rope_ref, other_rope_ref, w_uk_ref, w_uv_ref, out_ref
):
    core = lax.axis_index("ctx")
    rank_of = lambda block: order_ref[block]
    scale = (NOPE + ROPE) ** (-0.5) * math.log2(math.e)
    rows = q_nope_ref.shape[0]
    blocks = rows // BLOCK
    step = 256
    keys_t, values = [], []
    for latent_ref in (own_latent_ref, other_latent_ref):
        latent = latent_ref[...]
        keys_t.append(
            lax.dot_general(w_uk_ref[...], latent, (((0,), (1,)), ((), ())), preferred_element_type=f32).astype(bf16)
        )
        values.append(jnp.dot(latent, w_uv_ref[...], preferred_element_type=f32).astype(bf16))
    ropes = (own_rope_ref[...], other_rope_ref[...])
    blank = jnp.zeros_like(ropes[0])
    diagonal = lax.broadcasted_iota(jnp.int32, (step, step), 1) <= lax.broadcasted_iota(jnp.int32, (step, step), 0)
    key_cat, value_cat = [], []
    for head in range(2):
        cols = slice(head * NOPE, (head + 1) * NOPE)
        key_cat.append([
            jnp.concatenate([keys[cols, :]] + ([rope, blank] if head == 0 else [blank, rope]), axis=0)
            for keys, rope in zip(keys_t, ropes)
        ])
        value_cat.append([jnp.concatenate([held[:, cols], jnp.ones_like(held[:, cols])], axis=1) for held in values])

    def score(head, first):
        cols, part = slice(head * NOPE, (head + 1) * NOPE), slice(first, first + step)
        query = jnp.concatenate([q_nope_ref[part, cols], q_rope_ref[part, :]], axis=1)
        query_block, inside = first // BLOCK, first % BLOCK
        scores = []
        for side in (0, 1):
            owner = core if side == 0 else 1 - core
            for block in range(blocks):
                start = block * BLOCK
                if side == 0 and block == query_block:
                    seen = slice(start, start + inside + step)
                    piece = jnp.dot(query, key_cat[head][side][:, seen], preferred_element_type=f32)
                    last = jnp.where(diagonal, piece[:, inside:], neg_large)
                    piece = jnp.concatenate([piece[:, :inside], last], axis=1) if inside else last
                else:
                    seen = slice(start, start + BLOCK)
                    piece = jnp.dot(query, key_cat[head][side][:, seen], preferred_element_type=f32)
                    earlier = rank_of(owner * blocks + block) < rank_of(core * blocks + query_block)
                    piece = piece + jnp.where(earlier, 0.0, neg_large)
                scores.append((side, seen, piece))
        return scores

    units = [(head, first) for first in range(0, rows, step) for head in range(2)]
    ready = score(*units[0])
    for number, (head, first) in enumerate(units):
        scores = ready
        if number + 1 < len(units):
            ready = score(*units[number + 1])
        best = functools.reduce(jnp.maximum, [jnp.max(piece, axis=1, keepdims=True) for _, _, piece in scores])
        summed = 0.0
        for side, seen, piece in scores:
            probs = jnp.exp2((piece - best) * scale).astype(bf16)
            summed = summed + jnp.dot(probs, value_cat[head][side][seen, :], preferred_element_type=f32)
        out_ref[first : first + step, head * VDIM : (head + 1) * VDIM] = (summed[:, :VDIM] / summed[:, VDIM:]).astype(bf16)


def attend(block_order, q_nope, q_rope, latents, ropes, w_uk, w_uv):
    rows, keys = q_nope.shape[0], 2 * latents[0].shape[0]
    pairs = q_nope.shape[1] // (2 * NOPE)
    whole = lambda array: pl.BlockSpec(array.shape, lambda h, s: (0, 0))
    column = lambda array, width: pl.BlockSpec((array.shape[0], width), lambda h, s: (0, h))
    return pl.pallas_call(
        attention_kernel,
        grid_spec=pltpu.PrefetchScalarGridSpec(
            num_scalar_prefetch=1,
            grid=(pairs,),
            in_specs=[column(q_nope, 2 * NOPE), column(q_rope, 2 * ROPE)]
            + [whole(array) for array in (*latents, *ropes)]
            + [column(w_uk, 2 * NOPE), column(w_uv, 2 * VDIM)],
            out_specs=column(q_nope, 2 * VDIM),
        ),
        out_shape=jax.ShapeDtypeStruct((rows, q_nope.shape[1]), bf16),
        compiler_params=pltpu.CompilerParams(vmem_limit_bytes=60 * 1024 * 1024),
        cost_estimate=pl.CostEstimate(
            flops=2 * rows * keys * pairs * 2 * 384, bytes_accessed=8 * 1024 * 1024, transcendentals=rows * keys * pairs * 2
        ),
    )(block_order, q_nope, q_rope, *latents, *ropes, w_uk, w_uv)


class Ring:
    def __init__(self, count):
        self.count, self.half = count, count // 2
        self.grid = count == 8
        order = [(2 * p if p < count // 2 else 2 * count - 1 - 2 * p) if self.grid else p for p in range(count)]
        self.up = [(order[p], order[(p + 1) % count]) for p in range(count)]
        self.down = [(t, s) for s, t in self.up]
        index = lax.axis_index("exp")
        self.place = jnp.where(index % 2 == 0, index // 2, count - 1 - index // 2) if self.grid else index

    def index_at(self, place):
        return jnp.where(place < self.half, 2 * place, 2 * self.count - 1 - 2 * place) if self.grid else place

    def at(self, offset):
        return self.index_at(lax.rem(self.place + offset, self.count))

    def send(self, block, way):
        return lax.ppermute(block, "exp", self.up if way > 0 else self.down)


def after(blocks, work):
    if not work:
        return blocks
    held = lax.optimization_barrier((tuple(blocks), tuple(work)))
    return list(held[0])


def scatter_rows(ring, part):
    add = lambda *terms: functools.reduce(jnp.add, [t.astype(f32) for t in terms])
    far = part(ring.half, [])
    sent = [far]
    cut = far.shape[0] // 2
    going = {1: ring.send(far[:cut], 1), -1: ring.send(far[cut:], -1)}
    for offset in range(ring.half - 1, 0, -1):
        behind, sent = sent, []
        for way in (1, -1):
            own, come = part(way * offset, behind), going[way]
            if offset < ring.half - 1:
                block = add(own, come).astype(bf16)
            elif way > 0:
                block = jnp.concatenate([add(own[:cut], come).astype(bf16), own[cut:]], axis=0)
            else:
                block = jnp.concatenate([own[:cut], add(own[cut:], come).astype(bf16)], axis=0)
            sent.append(block)
            going[way] = ring.send(block, way)
    return add(part(0, sent), going[1], going[-1])


def per_device(
    count,
    resid,
    q_nope,
    q_rope,
    latent,
    k_rope,
    w_uk,
    w_uv,
    w_out,
    norm_gain,
    w_gate,
    w_up,
    w_down,
    routes,
    codes,
    block_order,
):
    token_rows, owned = resid.shape[0], w_gate.shape[0]
    cut = token_rows // 2
    ring = Ring(count)
    core, index = lax.axis_index("ctx"), lax.axis_index("exp")
    swap = lambda block: lax.ppermute(block, "ctx", [(0, 1), (1, 0)])

    ropes = k_rope.T
    heads = attend(
        block_order, q_nope, q_rope, (latent, swap(latent)), (ropes, swap(ropes)), w_uk, w_uv
    )

    heads = jnp.concatenate([heads, swap(heads)], axis=0)

    @functools.cache
    def attention_term(offset):
        first = jnp.bitwise_and(ring.at(offset % count) - core * ring.half, count - 1) * token_rows
        block = lax.dynamic_slice_in_dim(heads, first, token_rows, 0, allow_negative_indices=False)
        return lax.optimization_barrier(jnp.dot(block, w_out, preferred_element_type=f32).astype(bf16))

    residual_state = resid.astype(f32) + scatter_rows(ring, lambda offset, behind: attention_term(offset))

    code_values = codes.astype(f32)
    route_weight = route_factor * code_values / jnp.sum(code_values, axis=1, keepdims=True)
    named = routes[None] == jnp.arange(count * owned, dtype=jnp.int32)[:, None, None]
    routing = jnp.sum(jnp.where(named, route_weight[None], 0.0), axis=2)[None]
    squares = jnp.sum(residual_state * residual_state, axis=1)
    squares = squares + swap(squares)
    inverse_rms = lax.rsqrt(squares / D + norm_epsilon)
    normed = (residual_state * inverse_rms[:, None] * norm_gain).astype(bf16)

    def before_hidden(rows):
        product = lambda weight: jnp.einsum("td,ldf->ltf", rows, weight, preferred_element_type=f32).astype(bf16)
        own = [product(w_gate), product(w_up)]
        return own, [swap(pre) for pre in own]

    def after_hidden(own, other, weight):
        gate_pre, up_pre = [mine.astype(f32) + theirs.astype(f32) for mine, theirs in zip(own, other)]
        hidden = (jax.nn.silu(gate_pre) * up_pre * weight[:, :, None]).astype(bf16)
        return functools.reduce(
            jnp.add, [jnp.dot(hidden[e], w_down[e], preferred_element_type=f32) for e in range(owned)]
        ).astype(bf16)

    pre = [before_hidden(normed)]
    below = above = normed
    hops = count.bit_length() - 1

    def hop(routing, number):
        other = lax.ppermute(routing, "exp", [(i, i ^ (1 << number)) for i in range(count)])
        return jnp.concatenate([routing, other], axis=0)

    (routing,) = after([routing], [normed])
    for step in range(1, ring.half + 1):
        if step > 1:
            work = pre[step - 2][0] + (pre[0][1] if step == 3 else [])
            if step - 2 < hops - 1:
                (routing,) = after([hop(routing, step - 2)], [below])
                work = work + [routing]
            below, above = after([below, above], work)
        if step == ring.half:
            below, above = below[:cut], above[cut:]
        below, above = ring.send(below, 1), ring.send(above, -1)
        rows = jnp.concatenate([below, above], axis=0)
        if step == ring.half:
            for number in range(max(min(step - 1, hops - 1), 0), hops):
                routing = hop(routing, number)
            (rows,) = after([rows], pre[step - 1][0] + (pre[step - 3][1] if step > 2 else []))
        pre.append(before_hidden(rows))

    mine = lax.dynamic_slice_in_dim(routing, index * owned, owned, 1, allow_negative_indices=False)
    offsets = jnp.arange(count, dtype=jnp.int32)
    entry = jnp.bitwise_xor(ring.at(offsets), index)[:, None] == offsets[None, :]
    weights = jnp.sum(jnp.where(entry[:, :, None, None], mine[None], 0.0), axis=1)

    outcomes = {}

    def outcome(step, behind):
        weight = weights[step]
        if 0 < step < ring.half:
            weight = jnp.concatenate([weights[count - step], weight], axis=1)
        outcomes[step] = after_hidden(after(pre[step][0], behind), pre[step][1], weight)

    def expert_term(offset, behind):
        step = abs(offset)
        if step == ring.half and step > 1:
            outcome(step - 1, pre[step][0] + pre[step - 2][1])
            behind = [outcomes[step - 1]]
        if step not in outcomes:
            outcome(step, behind)
        if step in (0, ring.half):
            return outcomes[step]
        return outcomes[step][token_rows:] if offset > 0 else outcomes[step][:token_rows]

    return (residual_state + scatter_rows(ring, expert_term)).astype(bf16)


def solution(mesh):
    return jax.shard_map(
        functools.partial(per_device, mesh.shape["exp"]),
        mesh=mesh,
        in_specs=(
            P(("groups", "exp"), "ctx"),
            P(("groups", "ctx"), "exp"),
            P(("groups", "ctx"), "exp"),
            P(("groups", "ctx"), None),
            P(("groups", "ctx"), None),
            P(None, "exp"),
            P(None, "exp"),
            P("exp", "ctx"),
            P("ctx"),
            P("exp", "ctx", None),
            P("exp", "ctx", None),
            P("exp", None, "ctx"),
            P(("groups", "exp"), None),
            P(("groups", "exp"), None),
            P("groups"),
        ),
        out_specs=P(("groups", "exp"), "ctx"),
        check_vma=False,
    )
```

```python
import functools
import math

import jax
import jax.numpy as jnp
from jax import lax
from jax.experimental import pallas as pl
from jax.experimental.pallas import tpu as pltpu
from jax.sharding import PartitionSpec as P

D = 3584
NOPE = 128
ROPE = 64
VDIM = 128
BLOCK = 512

neg_large = -1e30
route_factor = 2.5
norm_epsilon = 1e-06
f32 = jnp.float32
bf16 = jnp.bfloat16


def attention_kernel(
    order_ref, q_nope_ref, q_rope_ref, own_latent_ref, other_latent_ref, own_rope_ref, other_rope_ref, w_uk_ref, w_uv_ref, out_ref
):
    core = lax.axis_index("ctx")
    rank_of = lambda block: order_ref[block]
    scale = (NOPE + ROPE) ** (-0.5) * math.log2(math.e)
    rows = q_nope_ref.shape[0]
    blocks = rows // BLOCK
    step = 256
    keys_t, values = [], []
    for latent_ref in (own_latent_ref, other_latent_ref):
        latent = latent_ref[...]
        keys_t.append(
            lax.dot_general(w_uk_ref[...], latent, (((0,), (1,)), ((), ())), preferred_element_type=f32).astype(bf16)
        )
        values.append(jnp.dot(latent, w_uv_ref[...], preferred_element_type=f32).astype(bf16))
    ropes = (own_rope_ref[...], other_rope_ref[...])
    blank = jnp.zeros_like(ropes[0])
    diagonal = lax.broadcasted_iota(jnp.int32, (step, step), 1) <= lax.broadcasted_iota(jnp.int32, (step, step), 0)
    key_cat, value_cat = [], []
    for head in range(2):
        cols = slice(head * NOPE, (head + 1) * NOPE)
        key_cat.append([
            jnp.concatenate([keys[cols, :]] + ([rope, blank] if head == 0 else [blank, rope]), axis=0)
            for keys, rope in zip(keys_t, ropes)
        ])
        value_cat.append([jnp.concatenate([held[:, cols], jnp.ones_like(held[:, cols])], axis=1) for held in values])

    def score(head, first):
        cols, part = slice(head * NOPE, (head + 1) * NOPE), slice(first, first + step)
        query = jnp.concatenate([q_nope_ref[part, cols], q_rope_ref[part, :]], axis=1)
        query_block, inside = first // BLOCK, first % BLOCK
        scores = []
        for side in (0, 1):
            owner = core if side == 0 else 1 - core
            for block in range(blocks):
                start = block * BLOCK
                if side == 0 and block == query_block:
                    seen = slice(start, start + inside + step)
                    piece = jnp.dot(query, key_cat[head][side][:, seen], preferred_element_type=f32)
                    last = jnp.where(diagonal, piece[:, inside:], neg_large)
                    piece = jnp.concatenate([piece[:, :inside], last], axis=1) if inside else last
                else:
                    seen = slice(start, start + BLOCK)
                    piece = jnp.dot(query, key_cat[head][side][:, seen], preferred_element_type=f32)
                    earlier = rank_of(owner * blocks + block) < rank_of(core * blocks + query_block)
                    piece = piece + jnp.where(earlier, 0.0, neg_large)
                scores.append((side, seen, piece))
        return scores

    units = [(head, first) for first in range(0, rows, step) for head in range(2)]
    ready = score(*units[0])
    for number, (head, first) in enumerate(units):
        scores = ready
        if number + 1 < len(units):
            ready = score(*units[number + 1])
        best = functools.reduce(jnp.maximum, [jnp.max(piece, axis=1, keepdims=True) for _, _, piece in scores])
        summed = 0.0
        for side, seen, piece in scores:
            probs = jnp.exp2((piece - best) * scale).astype(bf16)
            summed = summed + jnp.dot(probs, value_cat[head][side][seen, :], preferred_element_type=f32)
        out_ref[first : first + step, head * VDIM : (head + 1) * VDIM] = (summed[:, :VDIM] / summed[:, VDIM:]).astype(bf16)


def attend(block_order, q_nope, q_rope, latents, ropes, w_uk, w_uv):
    rows, keys = q_nope.shape[0], 2 * latents[0].shape[0]
    pairs = q_nope.shape[1] // (2 * NOPE)
    whole = lambda array: pl.BlockSpec(array.shape, lambda h, s: (0, 0))
    column = lambda array, width: pl.BlockSpec((array.shape[0], width), lambda h, s: (0, h))
    return pl.pallas_call(
        attention_kernel,
        grid_spec=pltpu.PrefetchScalarGridSpec(
            num_scalar_prefetch=1,
            grid=(pairs,),
            in_specs=[column(q_nope, 2 * NOPE), column(q_rope, 2 * ROPE)]
            + [whole(array) for array in (*latents, *ropes)]
            + [column(w_uk, 2 * NOPE), column(w_uv, 2 * VDIM)],
            out_specs=column(q_nope, 2 * VDIM),
        ),
        out_shape=jax.ShapeDtypeStruct((rows, q_nope.shape[1]), bf16),
        compiler_params=pltpu.CompilerParams(vmem_limit_bytes=60 * 1024 * 1024),
        cost_estimate=pl.CostEstimate(
            flops=2 * rows * keys * pairs * 2 * 384, bytes_accessed=8 * 1024 * 1024, transcendentals=rows * keys * pairs * 2
        ),
    )(block_order, q_nope, q_rope, *latents, *ropes, w_uk, w_uv)


class Ring:
    def __init__(self, count):
        self.count, self.half = count, count // 2
        self.grid = count == 8
        order = [(2 * p if p < count // 2 else 2 * count - 1 - 2 * p) if self.grid else p for p in range(count)]
        self.up = [(order[p], order[(p + 1) % count]) for p in range(count)]
        self.down = [(t, s) for s, t in self.up]
        index = lax.axis_index("exp")
        self.place = jnp.where(index % 2 == 0, index // 2, count - 1 - index // 2) if self.grid else index

    def index_at(self, place):
        return jnp.where(place < self.half, 2 * place, 2 * self.count - 1 - 2 * place) if self.grid else place

    def at(self, offset):
        return self.index_at(lax.rem(self.place + offset, self.count))

    def send(self, block, way):
        return lax.ppermute(block, "exp", self.up if way > 0 else self.down)


def after(blocks, work):
    if not work:
        return blocks
    held = lax.optimization_barrier((tuple(blocks), tuple(work)))
    return list(held[0])


def scatter_rows(ring, part):
    add = lambda *terms: functools.reduce(jnp.add, [t.astype(f32) for t in terms])
    far = part(ring.half, [])
    sent = [far]
    cut = far.shape[0] // 2
    going = {1: ring.send(far[:cut], 1), -1: ring.send(far[cut:], -1)}
    for offset in range(ring.half - 1, 0, -1):
        behind, sent = sent, []
        for way in (1, -1):
            own, come = part(way * offset, behind), going[way]
            if offset < ring.half - 1:
                block = add(own, come).astype(bf16)
            elif way > 0:
                block = jnp.concatenate([add(own[:cut], come).astype(bf16), own[cut:]], axis=0)
            else:
                block = jnp.concatenate([own[:cut], add(own[cut:], come).astype(bf16)], axis=0)
            sent.append(block)
            going[way] = ring.send(block, way)
    return add(part(0, sent), going[1], going[-1])


def per_device(
    count,
    resid,
    q_nope,
    q_rope,
    latent,
    k_rope,
    w_uk,
    w_uv,
    w_out,
    norm_gain,
    w_gate,
    w_up,
    w_down,
    routes,
    codes,
    block_order,
):
    token_rows, owned = resid.shape[0], w_gate.shape[0]
    cut = token_rows // 2
    ring = Ring(count)
    core, index = lax.axis_index("ctx"), lax.axis_index("exp")
    swap = lambda block: lax.ppermute(block, "ctx", [(0, 1), (1, 0)])

    ropes = k_rope.T
    heads = attend(
        block_order, q_nope, q_rope, (latent, swap(latent)), (ropes, swap(ropes)), w_uk, w_uv
    )

    other_heads = swap(heads)
    project = lambda rows: jnp.dot(rows, w_out, preferred_element_type=f32).astype(bf16)
    own_terms = project(heads)

    def block_of(offset):
        return jnp.bitwise_and(ring.at(offset % count) - core * ring.half, count - 1)

    def pick(own, other, block):
        first = jnp.minimum(block, ring.half - 1) * token_rows
        second = jnp.maximum(block - ring.half, 0) * token_rows
        part = lambda rows, at: lax.dynamic_slice_in_dim(rows, at, token_rows, 0, allow_negative_indices=False)
        return jnp.where(block < ring.half, part(own, first), part(other, second))

    nearby = {}

    def attention_term(offset, behind):
        if abs(offset) >= ring.half - 1:
            rows = pick(heads, other_heads, block_of(offset))
            return project(after([rows], behind)[0])
        if not nearby:
            nearby["other"] = project(after([other_heads], behind)[0])
        return pick(own_terms, nearby["other"], block_of(offset))

    residual_state = resid.astype(f32) + scatter_rows(ring, attention_term)

    code_values = codes.astype(f32)
    route_weight = route_factor * code_values / jnp.sum(code_values, axis=1, keepdims=True)
    named = routes[None] == jnp.arange(count * owned, dtype=jnp.int32)[:, None, None]
    routing = jnp.sum(jnp.where(named, route_weight[None], 0.0), axis=2)[None]
    scaled = (residual_state * norm_gain).astype(bf16)
    squares = jnp.sum(residual_state * residual_state, axis=1)
    squares = squares + swap(squares)
    inverse_rms = lax.rsqrt(squares / D + norm_epsilon)
    routing = jnp.concatenate([routing, inverse_rms[None, None]], axis=1)

    def before_hidden(rows):
        product = lambda weight: jnp.einsum("td,ldf->ltf", rows, weight, preferred_element_type=f32).astype(bf16)
        own = [product(w_gate), product(w_up)]
        return own, [swap(pre) for pre in own]

    def after_hidden(own, other, weight, scale):
        gate_pre, up_pre = [mine.astype(f32) + theirs.astype(f32) for mine, theirs in zip(own, other)]
        gate_pre = gate_pre * scale[:, None]
        hidden = (jax.nn.silu(gate_pre) * up_pre * (weight * scale)[:, :, None]).astype(bf16)
        return functools.reduce(
            jnp.add, [jnp.dot(hidden[e], w_down[e], preferred_element_type=f32) for e in range(owned)]
        ).astype(bf16)

    pre = [before_hidden(scaled)]
    below = above = scaled
    hops = count.bit_length() - 1

    def hop(routing, number):
        other = lax.ppermute(routing, "exp", [(i, i ^ (1 << number)) for i in range(count)])
        return jnp.concatenate([routing, other], axis=0)

    for step in range(1, ring.half + 1):
        if step > 1:
            work = pre[step - 2][0] + (pre[0][1] if step == 3 else [])
            if step <= hops:
                (routing,) = after([hop(routing, step - 2)], [below])
                work = work + [routing]
            below, above = after([below, above], work)
        if step == ring.half:
            below, above = below[:cut], above[cut:]
        below, above = ring.send(below, 1), ring.send(above, -1)
        rows = jnp.concatenate([below, above], axis=0)
        if step == ring.half:
            for number in range(min(step - 1, hops - 1), hops):
                routing = hop(routing, number)
            (rows,) = after([rows], pre[step - 1][0] + (pre[step - 3][1] if step > 2 else []))
        pre.append(before_hidden(rows))

    mine = lax.dynamic_slice_in_dim(routing, index * owned, owned, 1, allow_negative_indices=False)
    offsets = jnp.arange(count, dtype=jnp.int32)
    entry = jnp.bitwise_xor(ring.at(offsets), index)[:, None] == offsets[None, :]
    weights = jnp.sum(jnp.where(entry[:, :, None, None], mine[None], 0.0), axis=1)
    scales = jnp.sum(jnp.where(entry[:, :, None], routing[None, :, -1], 0.0), axis=1)

    outcomes = {}

    def outcome(step, behind):
        offsets = (-step % count, step) if 0 < step < ring.half else (step,)
        weight = jnp.concatenate([weights[o] for o in offsets], axis=1)
        scale = jnp.concatenate([scales[o] for o in offsets], axis=0)
        outcomes[step] = after_hidden(after(pre[step][0], behind), pre[step][1], weight, scale)

    def expert_term(offset, behind):
        step = abs(offset)
        if step == ring.half and step > 1:
            outcome(step - 1, pre[step][0] + pre[step - 2][1])
            behind = [outcomes[step - 1]]
        if step not in outcomes:
            outcome(step, behind)
        if step in (0, ring.half):
            return outcomes[step]
        return outcomes[step][token_rows:] if offset > 0 else outcomes[step][:token_rows]

    return (residual_state + scatter_rows(ring, expert_term)).astype(bf16)


def solution(mesh):
    return jax.shard_map(
        functools.partial(per_device, mesh.shape["exp"]),
        mesh=mesh,
        in_specs=(
            P(("groups", "exp"), "ctx"),
            P(("groups", "ctx"), "exp"),
            P(("groups", "ctx"), "exp"),
            P(("groups", "ctx"), None),
            P(("groups", "ctx"), None),
            P(None, "exp"),
            P(None, "exp"),
            P("exp", "ctx"),
            P("ctx"),
            P("exp", "ctx", None),
            P("exp", "ctx", None),
            P("exp", None, "ctx"),
            P(("groups", "exp"), None),
            P(("groups", "exp"), None),
            P("groups"),
        ),
        out_specs=P(("groups", "exp"), "ctx"),
        check_vma=False,
    )
```

```python
import functools
import math

import jax
import jax.numpy as jnp
from jax import lax
from jax.experimental import pallas as pl
from jax.experimental.pallas import tpu as pltpu
from jax.sharding import PartitionSpec as P

D = 3584
NOPE = 128
ROPE = 64
VDIM = 128
BLOCK = 512

neg_large = -1e30
route_factor = 2.5
norm_epsilon = 1e-06
f32 = jnp.float32
bf16 = jnp.bfloat16


def attention_kernel(
    order_ref, q_nope_ref, q_rope_ref, own_latent_ref, other_latent_ref, own_rope_ref, other_rope_ref, w_uk_ref, w_uv_ref, out_ref
):
    core = lax.axis_index("ctx")
    rank_of = lambda block: order_ref[block]
    scale = (NOPE + ROPE) ** (-0.5) * math.log2(math.e)
    rows = q_nope_ref.shape[0]
    blocks = rows // BLOCK
    step = 256
    keys_t, values = [], []
    for latent_ref in (own_latent_ref, other_latent_ref):
        latent = latent_ref[...]
        keys_t.append(
            lax.dot_general(w_uk_ref[...], latent, (((0,), (1,)), ((), ())), preferred_element_type=f32).astype(bf16)
        )
        values.append(jnp.dot(latent, w_uv_ref[...], preferred_element_type=f32).astype(bf16))
    ropes = (own_rope_ref[...], other_rope_ref[...])
    blank = jnp.zeros_like(ropes[0])
    diagonal = lax.broadcasted_iota(jnp.int32, (step, step), 1) <= lax.broadcasted_iota(jnp.int32, (step, step), 0)
    key_cat, value_cat = [], []
    for head in range(2):
        cols = slice(head * NOPE, (head + 1) * NOPE)
        key_cat.append([
            jnp.concatenate([keys[cols, :]] + ([rope, blank] if head == 0 else [blank, rope]), axis=0)
            for keys, rope in zip(keys_t, ropes)
        ])
        value_cat.append([jnp.concatenate([held[:, cols], jnp.ones_like(held[:, cols])], axis=1) for held in values])

    def score(head, first):
        cols, part = slice(head * NOPE, (head + 1) * NOPE), slice(first, first + step)
        query = jnp.concatenate([q_nope_ref[part, cols], q_rope_ref[part, :]], axis=1)
        query_block, inside = first // BLOCK, first % BLOCK
        scores = []
        for side in (0, 1):
            owner = core if side == 0 else 1 - core
            for block in range(blocks):
                start = block * BLOCK
                if side == 0 and block == query_block:
                    seen = slice(start, start + inside + step)
                    piece = jnp.dot(query, key_cat[head][side][:, seen], preferred_element_type=f32)
                    last = jnp.where(diagonal, piece[:, inside:], neg_large)
                    piece = jnp.concatenate([piece[:, :inside], last], axis=1) if inside else last
                else:
                    seen = slice(start, start + BLOCK)
                    piece = jnp.dot(query, key_cat[head][side][:, seen], preferred_element_type=f32)
                    earlier = rank_of(owner * blocks + block) < rank_of(core * blocks + query_block)
                    piece = piece + jnp.where(earlier, 0.0, neg_large)
                scores.append((side, seen, piece))
        return scores

    units = [(head, first) for first in range(0, rows, step) for head in range(2)]
    ready = score(*units[0])
    for number, (head, first) in enumerate(units):
        scores = ready
        if number + 1 < len(units):
            ready = score(*units[number + 1])
        best = functools.reduce(jnp.maximum, [jnp.max(piece, axis=1, keepdims=True) for _, _, piece in scores])
        summed = 0.0
        for side, seen, piece in scores:
            probs = jnp.exp2((piece - best) * scale).astype(bf16)
            summed = summed + jnp.dot(probs, value_cat[head][side][seen, :], preferred_element_type=f32)
        out_ref[first : first + step, head * VDIM : (head + 1) * VDIM] = (summed[:, :VDIM] / summed[:, VDIM:]).astype(bf16)


def attend(block_order, q_nope, q_rope, latents, ropes, w_uk, w_uv):
    rows, keys = q_nope.shape[0], 2 * latents[0].shape[0]
    pairs = q_nope.shape[1] // (2 * NOPE)
    whole = lambda array: pl.BlockSpec(array.shape, lambda h, s: (0, 0))
    column = lambda array, width: pl.BlockSpec((array.shape[0], width), lambda h, s: (0, h))
    return pl.pallas_call(
        attention_kernel,
        grid_spec=pltpu.PrefetchScalarGridSpec(
            num_scalar_prefetch=1,
            grid=(pairs,),
            in_specs=[column(q_nope, 2 * NOPE), column(q_rope, 2 * ROPE)]
            + [whole(array) for array in (*latents, *ropes)]
            + [column(w_uk, 2 * NOPE), column(w_uv, 2 * VDIM)],
            out_specs=column(q_nope, 2 * VDIM),
        ),
        out_shape=jax.ShapeDtypeStruct((rows, q_nope.shape[1]), bf16),
        compiler_params=pltpu.CompilerParams(vmem_limit_bytes=60 * 1024 * 1024),
        cost_estimate=pl.CostEstimate(
            flops=2 * rows * keys * pairs * 2 * 384, bytes_accessed=8 * 1024 * 1024, transcendentals=rows * keys * pairs * 2
        ),
    )(block_order, q_nope, q_rope, *latents, *ropes, w_uk, w_uv)


class Ring:
    def __init__(self, count):
        self.count, self.half = count, count // 2
        self.grid = count == 8
        order = [(2 * p if p < count // 2 else 2 * count - 1 - 2 * p) if self.grid else p for p in range(count)]
        self.up = [(order[p], order[(p + 1) % count]) for p in range(count)]
        self.down = [(t, s) for s, t in self.up]
        index = lax.axis_index("exp")
        self.place = jnp.where(index % 2 == 0, index // 2, count - 1 - index // 2) if self.grid else index

    def index_at(self, place):
        return jnp.where(place < self.half, 2 * place, 2 * self.count - 1 - 2 * place) if self.grid else place

    def at(self, offset):
        return self.index_at(lax.rem(self.place + offset, self.count))

    def send(self, block, way):
        return lax.ppermute(block, "exp", self.up if way > 0 else self.down)


def after(blocks, work):
    if not work:
        return blocks
    held = lax.optimization_barrier((tuple(blocks), tuple(work)))
    return list(held[0])


def scatter_rows(ring, part):
    add = lambda *terms: functools.reduce(jnp.add, [t.astype(f32) for t in terms])
    far = part(ring.half, [])
    sent = [far]
    cut = far.shape[0] // 2
    going = {1: ring.send(far[:cut], 1), -1: ring.send(far[cut:], -1)}
    for offset in range(ring.half - 1, 0, -1):
        behind, sent = sent, []
        for way in (1, -1):
            own, come = part(way * offset, behind), going[way]
            if offset == ring.half - 1:
                come = jnp.pad(come, ((0, cut) if way > 0 else (cut, 0), (0, 0)))
            block = add(own, come).astype(bf16)
            sent.append(block)
            going[way] = ring.send(block, way)
    return add(part(0, sent), going[1], going[-1])


def per_device(
    count,
    resid,
    q_nope,
    q_rope,
    latent,
    k_rope,
    w_uk,
    w_uv,
    w_out,
    norm_gain,
    w_gate,
    w_up,
    w_down,
    routes,
    codes,
    block_order,
):
    token_rows, owned = resid.shape[0], w_gate.shape[0]
    cut = token_rows // 2
    ring = Ring(count)
    core, index = lax.axis_index("ctx"), lax.axis_index("exp")
    swap = lambda block: lax.ppermute(block, "ctx", [(0, 1), (1, 0)])

    ropes = k_rope.T
    heads = attend(
        block_order, q_nope, q_rope, (latent, swap(latent)), (ropes, swap(ropes)), w_uk, w_uv
    )

    other_heads = swap(heads)
    project = lambda rows: jnp.dot(rows, w_out, preferred_element_type=f32).astype(bf16)
    own_terms = project(heads)

    def block_of(offset):
        return jnp.bitwise_and(ring.at(offset % count) - core * ring.half, count - 1)

    def pick(own, other, block):
        first = jnp.minimum(block, ring.half - 1) * token_rows
        second = jnp.maximum(block - ring.half, 0) * token_rows
        part = lambda rows, at: lax.dynamic_slice_in_dim(rows, at, token_rows, 0, allow_negative_indices=False)
        return jnp.where(block < ring.half, part(own, first), part(other, second))

    nearby = {}

    def attention_term(offset, behind):
        if abs(offset) >= ring.half - 1:
            rows = pick(heads, other_heads, block_of(offset))
            return lax.optimization_barrier(project(after([rows], behind)[0]))
        if not nearby:
            nearby["other"] = project(after([other_heads], behind)[0])
        return lax.optimization_barrier(pick(own_terms, nearby["other"], block_of(offset)))

    residual_state = resid.astype(f32) + scatter_rows(ring, attention_term)

    code_values = codes.astype(f32)
    route_weight = route_factor * code_values / jnp.sum(code_values, axis=1, keepdims=True)
    named = routes[None] == jnp.arange(count * owned, dtype=jnp.int32)[:, None, None]
    routing = jnp.sum(jnp.where(named, route_weight[None], 0.0), axis=2)[None]
    scaled = (residual_state * norm_gain).astype(bf16)
    squares = jnp.sum(residual_state * residual_state, axis=1)
    squares = squares + swap(squares)
    inverse_rms = lax.rsqrt(squares / D + norm_epsilon)
    routing = jnp.concatenate([routing, inverse_rms[None, None]], axis=1)

    def before_hidden(rows):
        product = lambda weight: jnp.einsum("td,ldf->ltf", rows, weight, preferred_element_type=f32).astype(bf16)
        own = [product(w_gate), product(w_up)]
        return own, [swap(pre) for pre in own]

    def after_hidden(own, other, weight, scale):
        gate_pre, up_pre = [mine.astype(f32) + theirs.astype(f32) for mine, theirs in zip(own, other)]
        gate_pre = gate_pre * scale[:, None]
        hidden = (jax.nn.silu(gate_pre) * up_pre * (weight * scale)[:, :, None]).astype(bf16)
        return functools.reduce(
            jnp.add, [jnp.dot(hidden[e], w_down[e], preferred_element_type=f32) for e in range(owned)]
        ).astype(bf16)

    pre = [before_hidden(scaled)]
    below = above = scaled
    hops = count.bit_length() - 1

    def hop(routing, number):
        other = lax.ppermute(routing, "exp", [(i, i ^ (1 << number)) for i in range(count)])
        return jnp.concatenate([routing, other], axis=0)

    for step in range(1, ring.half + 1):
        if step > 1:
            work = pre[step - 2][0] + (pre[0][1] if step == 3 else [])
            if step <= hops:
                (routing,) = after([hop(routing, step - 2)], [below])
                work = work + [routing]
            below, above = after([below, above], work)
        if step == ring.half:
            below, above = below[:cut], above[cut:]
        below, above = ring.send(below, 1), ring.send(above, -1)
        rows = jnp.concatenate([below, above], axis=0)
        if step == ring.half:
            for number in range(min(step - 1, hops - 1), hops):
                routing = hop(routing, number)
            (rows,) = after([rows], pre[step - 1][0] + (pre[step - 3][1] if step > 2 else []))
        pre.append(before_hidden(rows))

    mine = lax.dynamic_slice_in_dim(routing, index * owned, owned, 1, allow_negative_indices=False)
    offsets = jnp.arange(count, dtype=jnp.int32)
    entry = jnp.bitwise_xor(ring.at(offsets), index)[:, None] == offsets[None, :]
    weights = jnp.sum(jnp.where(entry[:, :, None, None], mine[None], 0.0), axis=1)
    scales = jnp.sum(jnp.where(entry[:, :, None], routing[None, :, -1], 0.0), axis=1)

    outcomes = {}

    def outcome(step, behind):
        offsets = (-step % count, step) if 0 < step < ring.half else (step,)
        weight = jnp.concatenate([weights[o] for o in offsets], axis=1)
        scale = jnp.concatenate([scales[o] for o in offsets], axis=0)
        outcomes[step] = after_hidden(after(pre[step][0], behind), pre[step][1], weight, scale)

    def expert_term(offset, behind):
        step = abs(offset)
        if step == ring.half and step > 1:
            outcome(step - 1, pre[step][0] + pre[step - 2][1])
            behind = [outcomes[step - 1]]
        if step not in outcomes:
            outcome(step, behind)
        if step in (0, ring.half):
            return outcomes[step]
        return outcomes[step][token_rows:] if offset > 0 else outcomes[step][:token_rows]

    return (residual_state + scatter_rows(ring, expert_term)).astype(bf16)


def solution(mesh):
    return jax.shard_map(
        functools.partial(per_device, mesh.shape["exp"]),
        mesh=mesh,
        in_specs=(
            P(("groups", "exp"), "ctx"),
            P(("groups", "ctx"), "exp"),
            P(("groups", "ctx"), "exp"),
            P(("groups", "ctx"), None),
            P(("groups", "ctx"), None),
            P(None, "exp"),
            P(None, "exp"),
            P("exp", "ctx"),
            P("ctx"),
            P("exp", "ctx", None),
            P("exp", "ctx", None),
            P("exp", None, "ctx"),
            P(("groups", "exp"), None),
            P(("groups", "exp"), None),
            P("groups"),
        ),
        out_specs=P(("groups", "exp"), "ctx"),
        check_vma=False,
    )
```

```python
import functools
import math

import jax
import jax.numpy as jnp
from jax import lax
from jax.experimental import pallas as pl
from jax.experimental.pallas import tpu as pltpu
from jax.sharding import PartitionSpec as P

D = 3584
NOPE = 128
ROPE = 64
VDIM = 128
BLOCK = 512

neg_large = -1e30
route_factor = 2.5
norm_epsilon = 1e-06
f32 = jnp.float32
bf16 = jnp.bfloat16


def attention_kernel(
    order_ref, q_nope_ref, q_rope_ref, own_latent_ref, other_latent_ref, own_rope_ref, other_rope_ref, w_uk_ref, w_uv_ref, out_ref
):
    core = lax.axis_index("ctx")
    rank_of = lambda block: order_ref[block]
    scale = (NOPE + ROPE) ** (-0.5) * math.log2(math.e)
    rows = q_nope_ref.shape[0]
    blocks = rows // BLOCK
    step = 256
    keys_t, values = [], []
    for latent_ref in (own_latent_ref, other_latent_ref):
        latent = latent_ref[...]
        keys_t.append(
            lax.dot_general(w_uk_ref[...], latent, (((0,), (1,)), ((), ())), preferred_element_type=f32).astype(bf16)
        )
        values.append(jnp.dot(latent, w_uv_ref[...], preferred_element_type=f32).astype(bf16))
    ropes = (own_rope_ref[...], other_rope_ref[...])
    blank = jnp.zeros_like(ropes[0])
    diagonal = lax.broadcasted_iota(jnp.int32, (step, step), 1) <= lax.broadcasted_iota(jnp.int32, (step, step), 0)
    key_cat, value_cat = [], []
    for head in range(2):
        cols = slice(head * NOPE, (head + 1) * NOPE)
        key_cat.append([
            jnp.concatenate([keys[cols, :]] + ([rope, blank] if head == 0 else [blank, rope]), axis=0)
            for keys, rope in zip(keys_t, ropes)
        ])
        value_cat.append([jnp.concatenate([held[:, cols], jnp.ones_like(held[:, cols])], axis=1) for held in values])

    def score(head, first):
        cols, part = slice(head * NOPE, (head + 1) * NOPE), slice(first, first + step)
        query = jnp.concatenate([q_nope_ref[part, cols], q_rope_ref[part, :]], axis=1)
        query_block, inside = first // BLOCK, first % BLOCK
        scores = []
        for side in (0, 1):
            owner = core if side == 0 else 1 - core
            for block in range(blocks):
                start = block * BLOCK
                if side == 0 and block == query_block:
                    seen = slice(start, start + inside + step)
                    piece = jnp.dot(query, key_cat[head][side][:, seen], preferred_element_type=f32)
                    last = jnp.where(diagonal, piece[:, inside:], neg_large)
                    piece = jnp.concatenate([piece[:, :inside], last], axis=1) if inside else last
                else:
                    seen = slice(start, start + BLOCK)
                    piece = jnp.dot(query, key_cat[head][side][:, seen], preferred_element_type=f32)
                    earlier = rank_of(owner * blocks + block) < rank_of(core * blocks + query_block)
                    piece = piece + jnp.where(earlier, 0.0, neg_large)
                scores.append((side, seen, piece))
        return scores

    units = [(head, first) for first in range(0, rows, step) for head in range(2)]
    ready = score(*units[0])
    for number, (head, first) in enumerate(units):
        scores = ready
        if number + 1 < len(units):
            ready = score(*units[number + 1])
        best = functools.reduce(jnp.maximum, [jnp.max(piece, axis=1, keepdims=True) for _, _, piece in scores])
        summed = 0.0
        for side, seen, piece in scores:
            probs = jnp.exp2((piece - best) * scale).astype(bf16)
            summed = summed + jnp.dot(probs, value_cat[head][side][seen, :], preferred_element_type=f32)
        out_ref[first : first + step, head * VDIM : (head + 1) * VDIM] = (summed[:, :VDIM] / summed[:, VDIM:]).astype(bf16)


def attend(block_order, q_nope, q_rope, latents, ropes, w_uk, w_uv):
    rows, keys = q_nope.shape[0], 2 * latents[0].shape[0]
    pairs = q_nope.shape[1] // (2 * NOPE)
    held = lambda array: pltpu.with_memory_space_constraint(array, pltpu.HBM)
    whole = lambda array: pl.BlockSpec(array.shape, lambda h, s: (0, 0))
    column = lambda array, width: pl.BlockSpec((array.shape[0], width), lambda h, s: (0, h))
    return pl.pallas_call(
        attention_kernel,
        grid_spec=pltpu.PrefetchScalarGridSpec(
            num_scalar_prefetch=1,
            grid=(pairs,),
            in_specs=[column(q_nope, 2 * NOPE), column(q_rope, 2 * ROPE)]
            + [whole(array) for array in (*latents, *ropes)]
            + [column(w_uk, 2 * NOPE), column(w_uv, 2 * VDIM)],
            out_specs=column(q_nope, 2 * VDIM),
        ),
        out_shape=jax.ShapeDtypeStruct((rows, q_nope.shape[1]), bf16),
        compiler_params=pltpu.CompilerParams(vmem_limit_bytes=24 * 1024 * 1024),
        cost_estimate=pl.CostEstimate(
            flops=2 * rows * keys * pairs * 2 * 384, bytes_accessed=8 * 1024 * 1024, transcendentals=rows * keys * pairs * 2
        ),
    )(block_order, held(q_nope), held(q_rope), held(latents[0]), latents[1], held(ropes[0]), ropes[1], held(w_uk), held(w_uv))


class Ring:
    def __init__(self, count):
        self.count, self.half = count, count // 2
        self.grid = count == 8
        order = [(2 * p if p < count // 2 else 2 * count - 1 - 2 * p) if self.grid else p for p in range(count)]
        self.up = [(order[p], order[(p + 1) % count]) for p in range(count)]
        self.down = [(t, s) for s, t in self.up]
        index = lax.axis_index("exp")
        self.place = jnp.where(index % 2 == 0, index // 2, count - 1 - index // 2) if self.grid else index

    def index_at(self, place):
        return jnp.where(place < self.half, 2 * place, 2 * self.count - 1 - 2 * place) if self.grid else place

    def at(self, offset):
        return self.index_at(lax.rem(self.place + offset, self.count))

    def send(self, block, way):
        return lax.ppermute(block, "exp", self.up if way > 0 else self.down)


def after(blocks, work):
    if not work:
        return blocks
    held = lax.optimization_barrier((tuple(blocks), tuple(work)))
    return list(held[0])


def scatter_rows(ring, part):
    add = lambda *terms: functools.reduce(jnp.add, [t.astype(f32) for t in terms])
    far = part(ring.half, [])
    sent = [far]
    cut = far.shape[0] // 2
    going = {1: ring.send(far[:cut], 1), -1: ring.send(far[cut:], -1)}
    for offset in range(ring.half - 1, 0, -1):
        behind, sent = sent, []
        for way in (1, -1):
            own, come = part(way * offset, behind), going[way]
            if offset == ring.half - 1:
                come = jnp.pad(come, ((0, cut) if way > 0 else (cut, 0), (0, 0)))
            block = add(own, come).astype(bf16)
            sent.append(block)
            going[way] = ring.send(block, way)
    return add(part(0, sent), going[1], going[-1])


def per_device(
    count,
    resid,
    q_nope,
    q_rope,
    latent,
    k_rope,
    w_uk,
    w_uv,
    w_out,
    norm_gain,
    w_gate,
    w_up,
    w_down,
    routes,
    codes,
    block_order,
):
    token_rows, owned = resid.shape[0], w_gate.shape[0]
    cut = token_rows // 2
    ring = Ring(count)
    core, index = lax.axis_index("ctx"), lax.axis_index("exp")
    swap = lambda block: lax.ppermute(block, "ctx", [(0, 1), (1, 0)])

    ropes = k_rope.T
    heads = attend(
        block_order, q_nope, q_rope, (latent, swap(latent)), (ropes, swap(ropes)), w_uk, w_uv
    )

    other_heads = swap(heads)
    project = lambda rows: jnp.dot(rows, w_out, preferred_element_type=f32).astype(bf16)
    own_terms = project(heads)

    def block_of(offset):
        return jnp.bitwise_and(ring.at(offset % count) - core * ring.half, count - 1)

    def pick(own, other, block):
        first = jnp.minimum(block, ring.half - 1) * token_rows
        second = jnp.maximum(block - ring.half, 0) * token_rows
        part = lambda rows, at: lax.dynamic_slice_in_dim(rows, at, token_rows, 0, allow_negative_indices=False)
        return jnp.where(block < ring.half, part(own, first), part(other, second))

    nearby = {}

    def attention_term(offset, behind):
        if abs(offset) >= ring.half - 1:
            rows = pick(heads, other_heads, block_of(offset))
            return lax.optimization_barrier(project(after([rows], behind)[0]))
        if not nearby:
            nearby["other"] = project(after([other_heads], behind)[0])
        return lax.optimization_barrier(pick(own_terms, nearby["other"], block_of(offset)))

    residual_state = resid.astype(f32) + scatter_rows(ring, attention_term)

    code_values = codes.astype(f32)
    route_weight = route_factor * code_values / jnp.sum(code_values, axis=1, keepdims=True)
    named = routes[None] == jnp.arange(count * owned, dtype=jnp.int32)[:, None, None]
    routing = jnp.sum(jnp.where(named, route_weight[None], 0.0), axis=2)[None]
    scaled = (residual_state * norm_gain).astype(bf16)
    squares = jnp.sum(residual_state * residual_state, axis=1)
    squares = squares + swap(squares)
    inverse_rms = lax.rsqrt(squares / D + norm_epsilon)
    routing = jnp.concatenate([routing, inverse_rms[None, None]], axis=1)

    def before_hidden(rows):
        product = lambda weight: jnp.einsum("td,ldf->ltf", rows, weight, preferred_element_type=f32).astype(bf16)
        own = [product(w_gate), product(w_up)]
        return own, [swap(pre) for pre in own]

    def after_hidden(own, other, weight, scale):
        gate_pre, up_pre = [mine.astype(f32) + theirs.astype(f32) for mine, theirs in zip(own, other)]
        gate_pre = gate_pre * scale[:, None]
        hidden = (jax.nn.silu(gate_pre) * up_pre * (weight * scale)[:, :, None]).astype(bf16)
        return functools.reduce(
            jnp.add, [jnp.dot(hidden[e], w_down[e], preferred_element_type=f32) for e in range(owned)]
        ).astype(bf16)

    pre = [before_hidden(scaled)]
    below = above = scaled
    hops = count.bit_length() - 1

    def hop(routing, number):
        other = lax.ppermute(routing, "exp", [(i, i ^ (1 << number)) for i in range(count)])
        return jnp.concatenate([routing, other], axis=0)

    for step in range(1, ring.half + 1):
        if step > 1:
            work = pre[step - 2][0] + (pre[0][1] if step == 3 else [])
            if step <= hops:
                (routing,) = after([hop(routing, step - 2)], [below])
                work = work + [routing]
            below, above = after([below, above], work)
        if step == ring.half:
            below, above = below[:cut], above[cut:]
        below, above = ring.send(below, 1), ring.send(above, -1)
        rows = jnp.concatenate([below, above], axis=0)
        if step == ring.half:
            for number in range(min(step - 1, hops - 1), hops):
                routing = hop(routing, number)
            (rows,) = after([rows], pre[step - 1][0] + (pre[step - 3][1] if step > 2 else []))
        pre.append(before_hidden(rows))

    mine = lax.dynamic_slice_in_dim(routing, index * owned, owned, 1, allow_negative_indices=False)
    offsets = jnp.arange(count, dtype=jnp.int32)
    entry = jnp.bitwise_xor(ring.at(offsets), index)[:, None] == offsets[None, :]
    weights = jnp.sum(jnp.where(entry[:, :, None, None], mine[None], 0.0), axis=1)
    scales = jnp.sum(jnp.where(entry[:, :, None], routing[None, :, -1], 0.0), axis=1)

    outcomes = {}

    def outcome(step, behind):
        offsets = (-step % count, step) if 0 < step < ring.half else (step,)
        weight = jnp.concatenate([weights[o] for o in offsets], axis=1)
        scale = jnp.concatenate([scales[o] for o in offsets], axis=0)
        outcomes[step] = after_hidden(after(pre[step][0], behind), pre[step][1], weight, scale)

    def expert_term(offset, behind):
        step = abs(offset)
        if step == ring.half and step > 1:
            outcome(step - 1, pre[step][0] + pre[step - 2][1])
            behind = [outcomes[step - 1]]
        if step not in outcomes:
            outcome(step, behind)
        if step in (0, ring.half):
            return outcomes[step]
        return outcomes[step][token_rows:] if offset > 0 else outcomes[step][:token_rows]

    return (residual_state + scatter_rows(ring, expert_term)).astype(bf16)


def solution(mesh):
    return jax.shard_map(
        functools.partial(per_device, mesh.shape["exp"]),
        mesh=mesh,
        in_specs=(
            P(("groups", "exp"), "ctx"),
            P(("groups", "ctx"), "exp"),
            P(("groups", "ctx"), "exp"),
            P(("groups", "ctx"), None),
            P(("groups", "ctx"), None),
            P(None, "exp"),
            P(None, "exp"),
            P("exp", "ctx"),
            P("ctx"),
            P("exp", "ctx", None),
            P("exp", "ctx", None),
            P("exp", None, "ctx"),
            P(("groups", "exp"), None),
            P(("groups", "exp"), None),
            P("groups"),
        ),
        out_specs=P(("groups", "exp"), "ctx"),
        check_vma=False,
    )
```

```python
import functools
import math

import jax
import jax.numpy as jnp
from jax import lax
from jax.experimental import pallas as pl
from jax.experimental.pallas import tpu as pltpu
from jax.sharding import PartitionSpec as P

D = 3584
NOPE = 128
ROPE = 64
VDIM = 128
BLOCK = 512

neg_large = -1e30
route_factor = 2.5
norm_epsilon = 1e-06
f32 = jnp.float32
bf16 = jnp.bfloat16


def attention_kernel(
    order_ref, q_nope_ref, q_rope_ref, own_latent_ref, other_latent_ref, own_rope_ref, other_rope_ref, w_uk_ref, w_uv_ref, out_ref
):
    core = lax.axis_index("ctx")
    rank_of = lambda block: order_ref[block]
    scale = (NOPE + ROPE) ** (-0.5) * math.log2(math.e)
    rows = q_nope_ref.shape[0]
    blocks = rows // BLOCK
    step = 256
    keys_t, values = [], []
    for latent_ref in (own_latent_ref, other_latent_ref):
        latent = latent_ref[...]
        keys_t.append(
            lax.dot_general(w_uk_ref[...], latent, (((0,), (1,)), ((), ())), preferred_element_type=f32).astype(bf16)
        )
        values.append(jnp.dot(latent, w_uv_ref[...], preferred_element_type=f32).astype(bf16))
    ropes = (own_rope_ref[...], other_rope_ref[...])
    blank = jnp.zeros_like(ropes[0])
    diagonal = lax.broadcasted_iota(jnp.int32, (step, step), 1) <= lax.broadcasted_iota(jnp.int32, (step, step), 0)
    key_cat, value_cat = [], []
    for head in range(2):
        cols = slice(head * NOPE, (head + 1) * NOPE)
        key_cat.append([
            jnp.concatenate([keys[cols, :]] + ([rope, blank] if head == 0 else [blank, rope]), axis=0)
            for keys, rope in zip(keys_t, ropes)
        ])
        value_cat.append([jnp.concatenate([held[:, cols], jnp.ones_like(held[:, cols])], axis=1) for held in values])

    def score(head, first):
        cols, part = slice(head * NOPE, (head + 1) * NOPE), slice(first, first + step)
        query = jnp.concatenate([q_nope_ref[part, cols], q_rope_ref[part, :]], axis=1)
        query_block, inside = first // BLOCK, first % BLOCK
        scores = []
        for side in (0, 1):
            owner = core if side == 0 else 1 - core
            for block in range(blocks):
                start = block * BLOCK
                if side == 0 and block == query_block:
                    seen = slice(start, start + inside + step)
                    piece = jnp.dot(query, key_cat[head][side][:, seen], preferred_element_type=f32)
                    last = jnp.where(diagonal, piece[:, inside:], neg_large)
                    piece = jnp.concatenate([piece[:, :inside], last], axis=1) if inside else last
                else:
                    seen = slice(start, start + BLOCK)
                    piece = jnp.dot(query, key_cat[head][side][:, seen], preferred_element_type=f32)
                    earlier = rank_of(owner * blocks + block) < rank_of(core * blocks + query_block)
                    piece = piece + jnp.where(earlier, 0.0, neg_large)
                scores.append((side, seen, piece))
        return scores

    units = [(head, first) for first in range(0, rows, step) for head in range(2)]
    ready = score(*units[0])
    for number, (head, first) in enumerate(units):
        scores = ready
        if number + 1 < len(units):
            ready = score(*units[number + 1])
        best = functools.reduce(jnp.maximum, [jnp.max(piece, axis=1, keepdims=True) for _, _, piece in scores])
        summed = 0.0
        for side, seen, piece in scores:
            probs = jnp.exp2((piece - best) * scale).astype(bf16)
            summed = summed + jnp.dot(probs, value_cat[head][side][seen, :], preferred_element_type=f32)
        out_ref[first : first + step, head * VDIM : (head + 1) * VDIM] = (summed[:, :VDIM] / summed[:, VDIM:]).astype(bf16)


def attend(block_order, q_nope, q_rope, latents, ropes, w_uk, w_uv):
    rows, keys = q_nope.shape[0], 2 * latents[0].shape[0]
    pairs = q_nope.shape[1] // (2 * NOPE)
    held = lambda array: pltpu.with_memory_space_constraint(array, pltpu.HBM)
    whole = lambda array: pl.BlockSpec(array.shape, lambda h, s: (0, 0))
    column = lambda array, width: pl.BlockSpec((array.shape[0], width), lambda h, s: (0, h))
    return pl.pallas_call(
        attention_kernel,
        grid_spec=pltpu.PrefetchScalarGridSpec(
            num_scalar_prefetch=1,
            grid=(pairs,),
            in_specs=[column(q_nope, 2 * NOPE), column(q_rope, 2 * ROPE)]
            + [whole(array) for array in (*latents, *ropes)]
            + [column(w_uk, 2 * NOPE), column(w_uv, 2 * VDIM)],
            out_specs=column(q_nope, 2 * VDIM),
        ),
        out_shape=jax.ShapeDtypeStruct((rows, q_nope.shape[1]), bf16),
        compiler_params=pltpu.CompilerParams(vmem_limit_bytes=12 * 1024 * 1024),
        cost_estimate=pl.CostEstimate(
            flops=2 * rows * keys * pairs * 2 * 384, bytes_accessed=8 * 1024 * 1024, transcendentals=rows * keys * pairs * 2
        ),
    )(block_order, held(q_nope), held(q_rope), held(latents[0]), latents[1], held(ropes[0]), ropes[1], held(w_uk), held(w_uv))


class Ring:
    def __init__(self, count):
        self.count, self.half = count, count // 2
        self.grid = count == 8
        order = [(2 * p if p < count // 2 else 2 * count - 1 - 2 * p) if self.grid else p for p in range(count)]
        self.up = [(order[p], order[(p + 1) % count]) for p in range(count)]
        self.down = [(t, s) for s, t in self.up]
        index = lax.axis_index("exp")
        self.place = jnp.where(index % 2 == 0, index // 2, count - 1 - index // 2) if self.grid else index

    def index_at(self, place):
        return jnp.where(place < self.half, 2 * place, 2 * self.count - 1 - 2 * place) if self.grid else place

    def at(self, offset):
        return self.index_at(lax.rem(self.place + offset, self.count))

    def send(self, block, way):
        return lax.ppermute(block, "exp", self.up if way > 0 else self.down)


def after(blocks, work):
    if not work:
        return blocks
    held = lax.optimization_barrier((tuple(blocks), tuple(work)))
    return list(held[0])


def scatter_rows(ring, part):
    add = lambda *terms: functools.reduce(jnp.add, [t.astype(f32) for t in terms])
    far = part(ring.half, [])
    sent = [far]
    cut = far.shape[0] // 2
    going = {1: ring.send(far[:cut], 1), -1: ring.send(far[cut:], -1)}
    for offset in range(ring.half - 1, 0, -1):
        behind, sent = sent, []
        for way in (1, -1):
            own, come = part(way * offset, behind), going[way]
            if offset == ring.half - 1:
                come = jnp.pad(come, ((0, cut) if way > 0 else (cut, 0), (0, 0)))
            block = add(own, come).astype(bf16)
            sent.append(block)
            going[way] = ring.send(block, way)
    return add(part(0, sent), going[1], going[-1])


def per_device(
    count,
    resid,
    q_nope,
    q_rope,
    latent,
    k_rope,
    w_uk,
    w_uv,
    w_out,
    norm_gain,
    w_gate,
    w_up,
    w_down,
    routes,
    codes,
    block_order,
):
    token_rows, owned = resid.shape[0], w_gate.shape[0]
    cut = token_rows // 2
    ring = Ring(count)
    core, index = lax.axis_index("ctx"), lax.axis_index("exp")
    swap = lambda block: lax.ppermute(block, "ctx", [(0, 1), (1, 0)])

    ropes = k_rope.T
    heads = attend(
        block_order, q_nope, q_rope, (latent, swap(latent)), (ropes, swap(ropes)), w_uk, w_uv
    )

    other_heads = swap(heads)
    project = lambda rows: jnp.dot(rows, w_out, preferred_element_type=f32).astype(bf16)
    own_terms = project(heads)

    def block_of(offset):
        return jnp.bitwise_and(ring.at(offset % count) - core * ring.half, count - 1)

    def pick(own, other, block):
        first = jnp.minimum(block, ring.half - 1) * token_rows
        second = jnp.maximum(block - ring.half, 0) * token_rows
        part = lambda rows, at: lax.dynamic_slice_in_dim(rows, at, token_rows, 0, allow_negative_indices=False)
        return jnp.where(block < ring.half, part(own, first), part(other, second))

    nearby = {}

    def attention_term(offset, behind):
        if abs(offset) >= ring.half - 1:
            rows = pick(heads, other_heads, block_of(offset))
            return lax.optimization_barrier(project(after([rows], behind)[0]))
        if not nearby:
            nearby["other"] = project(after([other_heads], behind)[0])
        return lax.optimization_barrier(pick(own_terms, nearby["other"], block_of(offset)))

    residual_state = resid.astype(f32) + scatter_rows(ring, attention_term)

    code_values = codes.astype(f32)
    route_weight = route_factor * code_values / jnp.sum(code_values, axis=1, keepdims=True)
    named = routes[None] == jnp.arange(count * owned, dtype=jnp.int32)[:, None, None]
    routing = jnp.sum(jnp.where(named, route_weight[None], 0.0), axis=2)[None]
    scaled = (residual_state * norm_gain).astype(bf16)
    squares = jnp.sum(residual_state * residual_state, axis=1)
    squares = squares + swap(squares)
    inverse_rms = lax.rsqrt(squares / D + norm_epsilon)
    routing = jnp.concatenate([routing, inverse_rms[None, None]], axis=1)

    def before_hidden(rows):
        product = lambda weight: jnp.einsum("td,ldf->ltf", rows, weight, preferred_element_type=f32).astype(bf16)
        own = [product(w_gate), product(w_up)]
        return own, [swap(pre) for pre in own]

    def after_hidden(own, other, weight, scale):
        gate_pre, up_pre = [mine.astype(f32) + theirs.astype(f32) for mine, theirs in zip(own, other)]
        gate_pre = gate_pre * scale[:, None]
        hidden = (jax.nn.silu(gate_pre) * up_pre * (weight * scale)[:, :, None]).astype(bf16)
        return functools.reduce(
            jnp.add, [jnp.dot(hidden[e], w_down[e], preferred_element_type=f32) for e in range(owned)]
        ).astype(bf16)

    pre = [before_hidden(scaled)]
    below = above = scaled
    hops = count.bit_length() - 1
    far_first = [count >> (1 + number) for number in range(hops)]

    def hop(routing, number):
        other = lax.ppermute(routing, "exp", [(i, i ^ far_first[number]) for i in range(count)])
        return jnp.concatenate([routing, other], axis=0)

    for step in range(1, ring.half + 1):
        if step > 1:
            work = pre[step - 2][0] + (pre[0][1] if step == 3 else [])
            if step <= hops:
                (routing,) = after([hop(routing, step - 2)], [below])
                work = work + [routing]
            below, above = after([below, above], work)
        if step == ring.half:
            below, above = below[:cut], above[cut:]
        below, above = ring.send(below, 1), ring.send(above, -1)
        rows = jnp.concatenate([below, above], axis=0)
        if step == ring.half:
            for number in range(min(step - 1, hops - 1), hops):
                routing = hop(routing, number)
            (rows,) = after([rows], pre[step - 1][0] + (pre[step - 3][1] if step > 2 else []))
        pre.append(before_hidden(rows))

    mine = lax.dynamic_slice_in_dim(routing, index * owned, owned, 1, allow_negative_indices=False)
    offsets = jnp.arange(count, dtype=jnp.int32)
    held = [sum(bit for number, bit in enumerate(far_first) if p >> number & 1) for p in range(count)]
    entry = jnp.bitwise_xor(ring.at(offsets), index)[:, None] == jnp.array(held, jnp.int32)[None, :]
    weights = jnp.sum(jnp.where(entry[:, :, None, None], mine[None], 0.0), axis=1)
    scales = jnp.sum(jnp.where(entry[:, :, None], routing[None, :, -1], 0.0), axis=1)

    outcomes = {}

    def outcome(step, behind):
        offsets = (-step % count, step) if 0 < step < ring.half else (step,)
        weight = jnp.concatenate([weights[o] for o in offsets], axis=1)
        scale = jnp.concatenate([scales[o] for o in offsets], axis=0)
        outcomes[step] = after_hidden(after(pre[step][0], behind), pre[step][1], weight, scale)

    def expert_term(offset, behind):
        step = abs(offset)
        if step == ring.half and step > 1:
            outcome(step - 1, pre[step][0] + pre[step - 2][1])
            behind = [outcomes[step - 1]]
        if step not in outcomes:
            outcome(step, behind)
        if step in (0, ring.half):
            return outcomes[step]
        return outcomes[step][token_rows:] if offset > 0 else outcomes[step][:token_rows]

    return (residual_state + scatter_rows(ring, expert_term)).astype(bf16)


def solution(mesh):
    return jax.shard_map(
        functools.partial(per_device, mesh.shape["exp"]),
        mesh=mesh,
        in_specs=(
            P(("groups", "exp"), "ctx"),
            P(("groups", "ctx"), "exp"),
            P(("groups", "ctx"), "exp"),
            P(("groups", "ctx"), None),
            P(("groups", "ctx"), None),
            P(None, "exp"),
            P(None, "exp"),
            P("exp", "ctx"),
            P("ctx"),
            P("exp", "ctx", None),
            P("exp", "ctx", None),
            P("exp", None, "ctx"),
            P(("groups", "exp"), None),
            P(("groups", "exp"), None),
            P("groups"),
        ),
        out_specs=P(("groups", "exp"), "ctx"),
        check_vma=False,
    )
```

```python
import functools
import math

import jax
import jax.numpy as jnp
from jax import lax
from jax.experimental import pallas as pl
from jax.experimental.pallas import tpu as pltpu
from jax.sharding import PartitionSpec as P

D = 3584
NOPE = 128
ROPE = 64
VDIM = 128
BLOCK = 512

neg_large = -1e30
route_factor = 2.5
norm_epsilon = 1e-06
f32 = jnp.float32
bf16 = jnp.bfloat16


def attention_kernel(
    order_ref, q_nope_ref, q_rope_ref, own_latent_ref, other_latent_ref, own_rope_ref, other_rope_ref, w_uk_ref, w_uv_ref, out_ref
):
    core = lax.axis_index("ctx")
    rank_of = lambda block: order_ref[block]
    scale = (NOPE + ROPE) ** (-0.5) * math.log2(math.e)
    rows = q_nope_ref.shape[0]
    blocks = rows // BLOCK
    step = 256
    keys_t, values = [], []
    for latent_ref in (own_latent_ref, other_latent_ref):
        latent = latent_ref[...]
        keys_t.append(
            lax.dot_general(w_uk_ref[...], latent, (((0,), (1,)), ((), ())), preferred_element_type=f32).astype(bf16)
        )
        values.append(jnp.dot(latent, w_uv_ref[...], preferred_element_type=f32).astype(bf16))
    ropes = (own_rope_ref[...], other_rope_ref[...])
    blank = jnp.zeros_like(ropes[0])
    diagonal = lax.broadcasted_iota(jnp.int32, (step, step), 1) <= lax.broadcasted_iota(jnp.int32, (step, step), 0)
    key_cat, value_cat = [], []
    for head in range(2):
        cols = slice(head * NOPE, (head + 1) * NOPE)
        key_cat.append([
            jnp.concatenate([keys[cols, :]] + ([rope, blank] if head == 0 else [blank, rope]), axis=0)
            for keys, rope in zip(keys_t, ropes)
        ])
        value_cat.append([jnp.concatenate([held[:, cols], jnp.ones_like(held[:, cols])], axis=1) for held in values])

    def score(head, first):
        cols, part = slice(head * NOPE, (head + 1) * NOPE), slice(first, first + step)
        query = jnp.concatenate([q_nope_ref[part, cols], q_rope_ref[part, :]], axis=1)
        query_block, inside = first // BLOCK, first % BLOCK
        scores = []
        for side in (0, 1):
            owner = core if side == 0 else 1 - core
            for block in range(blocks):
                start = block * BLOCK
                if side == 0 and block == query_block:
                    seen = slice(start, start + inside + step)
                    piece = jnp.dot(query, key_cat[head][side][:, seen], preferred_element_type=f32)
                    last = jnp.where(diagonal, piece[:, inside:], neg_large)
                    piece = jnp.concatenate([piece[:, :inside], last], axis=1) if inside else last
                else:
                    seen = slice(start, start + BLOCK)
                    piece = jnp.dot(query, key_cat[head][side][:, seen], preferred_element_type=f32)
                    earlier = rank_of(owner * blocks + block) < rank_of(core * blocks + query_block)
                    piece = piece + jnp.where(earlier, 0.0, neg_large)
                scores.append((side, seen, piece))
        return scores

    units = [(head, first) for first in range(0, rows, step) for head in range(2)]
    ready = score(*units[0])
    for number, (head, first) in enumerate(units):
        scores = ready
        if number + 1 < len(units):
            ready = score(*units[number + 1])
        best = functools.reduce(jnp.maximum, [jnp.max(piece, axis=1, keepdims=True) for _, _, piece in scores])
        summed = 0.0
        for side, seen, piece in scores:
            probs = jnp.exp2((piece - best) * scale).astype(bf16)
            summed = summed + jnp.dot(probs, value_cat[head][side][seen, :], preferred_element_type=f32)
        out_ref[first : first + step, head * VDIM : (head + 1) * VDIM] = (summed[:, :VDIM] / summed[:, VDIM:]).astype(bf16)


def attend(block_order, q_nope, q_rope, latents, ropes, w_uk, w_uv):
    rows, keys = q_nope.shape[0], 2 * latents[0].shape[0]
    pairs = q_nope.shape[1] // (2 * NOPE)
    held = lambda array: pltpu.with_memory_space_constraint(array, pltpu.HBM)
    whole = lambda array: pl.BlockSpec(array.shape, lambda h, s: (0, 0))
    column = lambda array, width: pl.BlockSpec((array.shape[0], width), lambda h, s: (0, h))
    return pl.pallas_call(
        attention_kernel,
        grid_spec=pltpu.PrefetchScalarGridSpec(
            num_scalar_prefetch=1,
            grid=(pairs,),
            in_specs=[column(q_nope, 2 * NOPE), column(q_rope, 2 * ROPE)]
            + [whole(array) for array in (*latents, *ropes)]
            + [column(w_uk, 2 * NOPE), column(w_uv, 2 * VDIM)],
            out_specs=column(q_nope, 2 * VDIM),
        ),
        out_shape=jax.ShapeDtypeStruct((rows, q_nope.shape[1]), bf16),
        compiler_params=pltpu.CompilerParams(vmem_limit_bytes=12 * 1024 * 1024),
        cost_estimate=pl.CostEstimate(
            flops=2 * rows * keys * pairs * 2 * 384, bytes_accessed=8 * 1024 * 1024, transcendentals=rows * keys * pairs * 2
        ),
    )(held(block_order), held(q_nope), held(q_rope), held(latents[0]), latents[1], held(ropes[0]), ropes[1], held(w_uk), held(w_uv))


class Ring:
    def __init__(self, count):
        self.count, self.half = count, count // 2
        self.grid = count == 8
        order = [(2 * p if p < count // 2 else 2 * count - 1 - 2 * p) if self.grid else p for p in range(count)]
        forth = [(order[p], order[(p + 1) % count]) for p in range(count)]
        back = [(t, s) for s, t in forth]
        both = lambda first, second: first + [(count + s, count + t) for s, t in second]
        self.up, self.down = both(forth, back), both(back, forth)
        index = lax.axis_index("exp")
        self.place = jnp.where(index % 2 == 0, index // 2, count - 1 - index // 2) if self.grid else index
        self.mirrored = lax.axis_index("ctx") == 1

    def at(self, offset, mirrored):
        place = lax.rem(self.place + jnp.where(mirrored, self.count - offset, offset), self.count)
        return jnp.where(place < self.half, 2 * place, 2 * self.count - 1 - 2 * place) if self.grid else place

    def send(self, block, way):
        return lax.ppermute(block, ("ctx", "exp"), self.up if way > 0 else self.down)


def after(blocks, work):
    if not work:
        return blocks
    held = lax.optimization_barrier((tuple(blocks), tuple(work)))
    return list(held[0])


def scatter_rows(ring, part):
    add = lambda *terms: functools.reduce(jnp.add, [t.astype(f32) for t in terms])
    far = part(ring.half, [])
    sent = [far]
    cut = far.shape[0] // 2
    going = {1: ring.send(far[:cut], 1), -1: ring.send(far[cut:], -1)}
    for offset in range(ring.half - 1, 0, -1):
        behind, sent = sent, []
        for way in (1, -1):
            own, come = part(way * offset, behind), going[way]
            if offset == ring.half - 1:
                come = jnp.pad(come, ((0, cut) if way > 0 else (cut, 0), (0, 0)))
            block = add(own, come).astype(bf16)
            sent.append(block)
            going[way] = ring.send(block, way)
    return add(part(0, sent), going[1], going[-1])


def per_device(
    count,
    resid,
    q_nope,
    q_rope,
    latent,
    k_rope,
    w_uk,
    w_uv,
    w_out,
    norm_gain,
    w_gate,
    w_up,
    w_down,
    routes,
    codes,
    block_order,
):
    token_rows, owned = resid.shape[0], w_gate.shape[0]
    cut = token_rows // 2
    ring = Ring(count)
    core, index = lax.axis_index("ctx"), lax.axis_index("exp")
    swap = lambda block: lax.ppermute(block, "ctx", [(0, 1), (1, 0)])

    ropes = k_rope.T
    heads = attend(
        block_order, q_nope, q_rope, (latent, swap(latent)), (ropes, swap(ropes)), w_uk, w_uv
    )

    other_heads = swap(heads)
    project = lambda rows: jnp.dot(rows, w_out, preferred_element_type=f32).astype(bf16)
    own_terms = project(heads)

    def block_of(offset):
        return jnp.bitwise_and(ring.at(offset % count, ring.mirrored) - core * ring.half, count - 1)

    def pick(own, other, block):
        first = jnp.minimum(block, ring.half - 1) * token_rows
        second = jnp.maximum(block - ring.half, 0) * token_rows
        part = lambda rows, at: lax.dynamic_slice_in_dim(rows, at, token_rows, 0, allow_negative_indices=False)
        return jnp.where(block < ring.half, part(own, first), part(other, second))

    nearby = {}

    def attention_term(offset, behind):
        if abs(offset) >= ring.half - 1:
            rows = pick(heads, other_heads, block_of(offset))
            return lax.optimization_barrier(project(after([rows], behind)[0]))
        if not nearby:
            nearby["other"] = project(after([other_heads], behind)[0])
        return lax.optimization_barrier(pick(own_terms, nearby["other"], block_of(offset)))

    residual_state = resid.astype(f32) + scatter_rows(ring, attention_term)

    code_values = codes.astype(f32)
    route_weight = route_factor * code_values / jnp.sum(code_values, axis=1, keepdims=True)
    named = routes[None] == jnp.arange(count * owned, dtype=jnp.int32)[:, None, None]
    routing = jnp.sum(jnp.where(named, route_weight[None], 0.0), axis=2)[None]
    scaled = (residual_state * norm_gain).astype(bf16)
    squares = jnp.sum(residual_state * residual_state, axis=1)
    squares = squares + swap(squares)
    inverse_rms = lax.rsqrt(squares / D + norm_epsilon)
    routing = jnp.concatenate([routing, inverse_rms[None, None]], axis=1)

    def before_hidden(rows):
        product = lambda weight: jnp.einsum("td,ldf->ltf", rows, weight, preferred_element_type=f32).astype(bf16)
        own = [product(w_gate), product(w_up)]
        return own, [swap(pre) for pre in own]

    def after_hidden(own, other, weight, scale):
        gate_pre, up_pre = [mine.astype(f32) + theirs.astype(f32) for mine, theirs in zip(own, other)]
        gate_pre = gate_pre * scale[:, None]
        hidden = (jax.nn.silu(gate_pre) * up_pre * (weight * scale)[:, :, None]).astype(bf16)
        return functools.reduce(
            jnp.add, [jnp.dot(hidden[e], w_down[e], preferred_element_type=f32) for e in range(owned)]
        ).astype(bf16)

    pre = [before_hidden(scaled)]
    below = above = scaled
    hops = count.bit_length() - 1
    far_first = [count >> (1 + number) for number in range(hops)]

    def hop(routing, number):
        other = lax.ppermute(routing, "exp", [(i, i ^ far_first[number]) for i in range(count)])
        return jnp.concatenate([routing, other], axis=0)

    for step in range(1, ring.half + 1):
        if step > 1:
            work = pre[step - 2][0] + (pre[0][1] if step == 3 else [])
            if step <= hops:
                (routing,) = after([hop(routing, step - 2)], [below])
                work = work + [routing]
            below, above = after([below, above], work)
        if step == ring.half:
            below, above = below[:cut], above[cut:]
        below, above = ring.send(below, 1), ring.send(above, -1)
        rows = jnp.concatenate([below, above], axis=0)
        if step == ring.half:
            for number in range(min(step - 1, hops - 1), hops):
                routing = hop(routing, number)
            (rows,) = after([rows], pre[step - 1][0] + (pre[step - 3][1] if step > 2 else []))
        pre.append(before_hidden(rows))

    mine = lax.dynamic_slice_in_dim(routing, index * owned, owned, 1, allow_negative_indices=False)
    offsets = jnp.arange(count, dtype=jnp.int32)
    held = [sum(bit for number, bit in enumerate(far_first) if p >> number & 1) for p in range(count)]
    entry = jnp.bitwise_xor(ring.at(offsets, ring.mirrored), index)[:, None] == jnp.array(held, jnp.int32)[None, :]
    weights = jnp.sum(jnp.where(entry[:, :, None, None], mine[None], 0.0), axis=1)
    scales = jnp.sum(jnp.where(entry[:, :, None], routing[None, :, -1], 0.0), axis=1)

    outcomes = {}

    def outcome(step, behind):
        own, other = after(pre[step][0], behind), pre[step][1]
        if step in (0, ring.half):
            outcomes[step] = [after_hidden(own, other, weights[step], scales[step])]
            return
        sides = (slice(0, token_rows), slice(token_rows, 2 * token_rows))
        outcomes[step] = [
            after_hidden([x[:, mine] for x in own], [x[:, theirs] for x in other], weights[o], scales[o])
            for o, mine, theirs in ((count - step, sides[0], sides[1]), (step, sides[1], sides[0]))
        ]

    def expert_term(offset, behind):
        step = abs(offset)
        if step == ring.half and step > 1:
            outcome(step - 1, pre[step][0] + pre[step - 2][1])
            behind = outcomes[step - 1]
        if step not in outcomes:
            outcome(step, behind)
        return outcomes[step][-1 if offset > 0 else 0]

    return (residual_state + scatter_rows(ring, expert_term)).astype(bf16)


def solution(mesh):
    return jax.shard_map(
        functools.partial(per_device, mesh.shape["exp"]),
        mesh=mesh,
        in_specs=(
            P(("groups", "exp"), "ctx"),
            P(("groups", "ctx"), "exp"),
            P(("groups", "ctx"), "exp"),
            P(("groups", "ctx"), None),
            P(("groups", "ctx"), None),
            P(None, "exp"),
            P(None, "exp"),
            P("exp", "ctx"),
            P("ctx"),
            P("exp", "ctx", None),
            P("exp", "ctx", None),
            P("exp", None, "ctx"),
            P(("groups", "exp"), None),
            P(("groups", "exp"), None),
            P("groups"),
        ),
        out_specs=P(("groups", "exp"), "ctx"),
        check_vma=False,
    )
```

```python
import functools
import math

import jax
import jax.numpy as jnp
from jax import lax
from jax.experimental import pallas as pl
from jax.experimental.pallas import tpu as pltpu
from jax.sharding import PartitionSpec as P

D = 3584
NOPE = 128
ROPE = 64
VDIM = 128
BLOCK = 512

neg_large = -1e30
route_factor = 2.5
norm_epsilon = 1e-06
f32 = jnp.float32
bf16 = jnp.bfloat16


def attention_kernel(
    order_ref, q_nope_ref, q_rope_ref, own_latent_ref, other_latent_ref, own_rope_ref, other_rope_ref, w_uk_ref, w_uv_ref, out_ref
):
    core = lax.axis_index("ctx")
    rank_of = lambda block: order_ref[block]
    scale = (NOPE + ROPE) ** (-0.5) * math.log2(math.e)
    rows = q_nope_ref.shape[0]
    blocks = rows // BLOCK
    step = 256
    keys_t, values = [], []
    for latent_ref in (own_latent_ref, other_latent_ref):
        latent = latent_ref[...]
        keys_t.append(
            lax.dot_general(w_uk_ref[...], latent, (((0,), (1,)), ((), ())), preferred_element_type=f32).astype(bf16)
        )
        values.append(jnp.dot(latent, w_uv_ref[...], preferred_element_type=f32).astype(bf16))
    ropes = (own_rope_ref[...], other_rope_ref[...])
    blank = jnp.zeros_like(ropes[0])
    diagonal = lax.broadcasted_iota(jnp.int32, (step, step), 1) <= lax.broadcasted_iota(jnp.int32, (step, step), 0)
    key_cat, value_cat = [], []
    for head in range(2):
        cols = slice(head * NOPE, (head + 1) * NOPE)
        key_cat.append([
            jnp.concatenate([keys[cols, :]] + ([rope, blank] if head == 0 else [blank, rope]), axis=0)
            for keys, rope in zip(keys_t, ropes)
        ])
        value_cat.append([jnp.concatenate([held[:, cols], jnp.ones_like(held[:, cols])], axis=1) for held in values])

    def score(head, first):
        cols, part = slice(head * NOPE, (head + 1) * NOPE), slice(first, first + step)
        query = jnp.concatenate([q_nope_ref[part, cols], q_rope_ref[part, :]], axis=1)
        query_block, inside = first // BLOCK, first % BLOCK
        scores = []
        for side in (0, 1):
            owner = core if side == 0 else 1 - core
            for block in range(blocks):
                start = block * BLOCK
                if side == 0 and block == query_block:
                    seen = slice(start, start + inside + step)
                    piece = jnp.dot(query, key_cat[head][side][:, seen], preferred_element_type=f32)
                    last = jnp.where(diagonal, piece[:, inside:], neg_large)
                    piece = jnp.concatenate([piece[:, :inside], last], axis=1) if inside else last
                else:
                    seen = slice(start, start + BLOCK)
                    piece = jnp.dot(query, key_cat[head][side][:, seen], preferred_element_type=f32)
                    earlier = rank_of(owner * blocks + block) < rank_of(core * blocks + query_block)
                    piece = piece + jnp.where(earlier, 0.0, neg_large)
                scores.append((side, seen, piece))
        return scores

    units = [(head, first) for first in range(0, rows, step) for head in range(2)]
    ready = score(*units[0])
    for number, (head, first) in enumerate(units):
        scores = ready
        if number + 1 < len(units):
            ready = score(*units[number + 1])
        best = functools.reduce(jnp.maximum, [jnp.max(piece, axis=1, keepdims=True) for _, _, piece in scores])
        summed = 0.0
        for side, seen, piece in scores:
            probs = jnp.exp2((piece - best) * scale).astype(bf16)
            summed = summed + jnp.dot(probs, value_cat[head][side][seen, :], preferred_element_type=f32)
        out_ref[first : first + step, head * VDIM : (head + 1) * VDIM] = (summed[:, :VDIM] / summed[:, VDIM:]).astype(bf16)


def attend(block_order, q_nope, q_rope, latents, ropes, w_uk, w_uv):
    rows, keys = q_nope.shape[0], 2 * latents[0].shape[0]
    pairs = q_nope.shape[1] // (2 * NOPE)
    held = lambda array: pltpu.with_memory_space_constraint(array, pltpu.HBM)
    whole = lambda array: pl.BlockSpec(array.shape, lambda h, s: (0, 0))
    column = lambda array, width: pl.BlockSpec((array.shape[0], width), lambda h, s: (0, h))
    return pl.pallas_call(
        attention_kernel,
        grid_spec=pltpu.PrefetchScalarGridSpec(
            num_scalar_prefetch=1,
            grid=(pairs,),
            in_specs=[column(q_nope, 2 * NOPE), column(q_rope, 2 * ROPE)]
            + [whole(array) for array in (*latents, *ropes)]
            + [column(w_uk, 2 * NOPE), column(w_uv, 2 * VDIM)],
            out_specs=column(q_nope, 2 * VDIM),
        ),
        out_shape=jax.ShapeDtypeStruct((rows, q_nope.shape[1]), bf16),
        compiler_params=pltpu.CompilerParams(vmem_limit_bytes=12 * 1024 * 1024),
        cost_estimate=pl.CostEstimate(
            flops=7 * rows * keys * pairs * 2 * 384, bytes_accessed=8 * 1024 * 1024, transcendentals=rows * keys * pairs * 2
        ),
    )(held(block_order), held(q_nope), held(q_rope), held(latents[0]), latents[1], held(ropes[0]), ropes[1], held(w_uk), held(w_uv))


class Ring:
    def __init__(self, count):
        self.count, self.half = count, count // 2
        self.grid = count == 8
        order = [(2 * p if p < count // 2 else 2 * count - 1 - 2 * p) if self.grid else p for p in range(count)]
        self.up = [(order[p], order[(p + 1) % count]) for p in range(count)]
        self.down = [(t, s) for s, t in self.up]
        index = lax.axis_index("exp")
        self.place = jnp.where(index % 2 == 0, index // 2, count - 1 - index // 2) if self.grid else index

    def index_at(self, place):
        return jnp.where(place < self.half, 2 * place, 2 * self.count - 1 - 2 * place) if self.grid else place

    def at(self, offset):
        return self.index_at(lax.rem(self.place + offset, self.count))

    def send(self, block, way):
        return lax.ppermute(block, "exp", self.up if way > 0 else self.down)


def after(blocks, work):
    if not work:
        return blocks
    held = lax.optimization_barrier((tuple(blocks), tuple(work)))
    return list(held[0])


def scatter_rows(ring, part):
    add = lambda *terms: functools.reduce(jnp.add, [t.astype(f32) for t in terms])
    far = part(ring.half, [])
    sent = [far]
    cut = far.shape[0] // 2
    going = {1: ring.send(far[:cut], 1), -1: ring.send(far[cut:], -1)}
    for offset in range(ring.half - 1, 0, -1):
        behind, sent = sent, []
        for way in (1, -1):
            own, come = part(way * offset, behind), going[way]
            if offset == ring.half - 1:
                come = jnp.pad(come, ((0, cut) if way > 0 else (cut, 0), (0, 0)))
            block = add(own, come).astype(bf16)
            sent.append(block)
            going[way] = ring.send(block, way)
    return add(part(0, sent), going[1], going[-1])


def per_device(
    count,
    resid,
    q_nope,
    q_rope,
    latent,
    k_rope,
    w_uk,
    w_uv,
    w_out,
    norm_gain,
    w_gate,
    w_up,
    w_down,
    routes,
    codes,
    block_order,
):
    token_rows, owned = resid.shape[0], w_gate.shape[0]
    cut = token_rows // 2
    ring = Ring(count)
    core, index = lax.axis_index("ctx"), lax.axis_index("exp")
    swap = lambda block: lax.ppermute(block, "ctx", [(0, 1), (1, 0)])

    ropes = k_rope.T
    heads = attend(
        block_order, q_nope, q_rope, (latent, swap(latent)), (ropes, swap(ropes)), w_uk, w_uv
    )

    other_heads = swap(heads)
    project = lambda rows: jnp.dot(rows, w_out, preferred_element_type=f32).astype(bf16)
    own_terms = project(heads)

    def block_of(offset):
        return jnp.bitwise_and(ring.at(offset % count) - core * ring.half, count - 1)

    def pick(own, other, block):
        first = jnp.minimum(block, ring.half - 1) * token_rows
        second = jnp.maximum(block - ring.half, 0) * token_rows
        part = lambda rows, at: lax.dynamic_slice_in_dim(rows, at, token_rows, 0, allow_negative_indices=False)
        return jnp.where(block < ring.half, part(own, first), part(other, second))

    nearby = {}

    def attention_term(offset, behind):
        if abs(offset) >= ring.half - 1:
            rows = pick(heads, other_heads, block_of(offset))
            return lax.optimization_barrier(project(after([rows], behind)[0]))
        if not nearby:
            nearby["other"] = project(after([other_heads], behind)[0])
        return lax.optimization_barrier(pick(own_terms, nearby["other"], block_of(offset)))

    residual_state = resid.astype(f32) + scatter_rows(ring, attention_term)

    code_values = codes.astype(f32)
    route_weight = route_factor * code_values / jnp.sum(code_values, axis=1, keepdims=True)
    named = routes[None] == jnp.arange(count * owned, dtype=jnp.int32)[:, None, None]
    routing = jnp.sum(jnp.where(named, route_weight[None], 0.0), axis=2)[None]
    scaled = (residual_state * norm_gain).astype(bf16)
    squares = jnp.sum(residual_state * residual_state, axis=1)
    squares = squares + swap(squares)
    inverse_rms = lax.rsqrt(squares / D + norm_epsilon)
    routing = jnp.concatenate([routing, inverse_rms[None, None]], axis=1)

    def before_hidden(rows):
        product = lambda weight: jnp.einsum("td,ldf->ltf", rows, weight, preferred_element_type=f32).astype(bf16)
        own = [product(w_gate), product(w_up)]
        return own, [swap(pre) for pre in own]

    def after_hidden(own, other, weight, scale):
        gate_pre, up_pre = [mine.astype(f32) + theirs.astype(f32) for mine, theirs in zip(own, other)]
        gate_pre = gate_pre * scale[:, None]
        hidden = (jax.nn.silu(gate_pre) * up_pre * (weight * scale)[:, :, None]).astype(bf16)
        return functools.reduce(
            jnp.add, [jnp.dot(hidden[e], w_down[e], preferred_element_type=f32) for e in range(owned)]
        ).astype(bf16)

    pre = [before_hidden(scaled)]
    below = above = scaled
    hops = count.bit_length() - 1
    far_first = [count >> (1 + number) for number in range(hops)]

    def hop(routing, number):
        other = lax.ppermute(routing, "exp", [(i, i ^ far_first[number]) for i in range(count)])
        return jnp.concatenate([routing, other], axis=0)

    for step in range(1, ring.half + 1):
        if step > 1:
            work = pre[step - 2][0] + (pre[0][1] if step == 3 else [])
            if step <= hops:
                (routing,) = after([hop(routing, step - 2)], [below])
                work = work + [routing]
            below, above = after([below, above], work)
        if step == ring.half:
            below, above = below[:cut], above[cut:]
        below, above = ring.send(below, 1), ring.send(above, -1)
        rows = jnp.concatenate([below, above], axis=0)
        if step == ring.half:
            for number in range(min(step - 1, hops - 1), hops):
                routing = hop(routing, number)
            (rows,) = after([rows], pre[step - 1][0] + (pre[step - 3][1] if step > 2 else []))
        pre.append(before_hidden(rows))

    mine = lax.dynamic_slice_in_dim(routing, index * owned, owned, 1, allow_negative_indices=False)
    offsets = jnp.arange(count, dtype=jnp.int32)
    held = [sum(bit for number, bit in enumerate(far_first) if p >> number & 1) for p in range(count)]
    entry = jnp.bitwise_xor(ring.at(offsets), index)[:, None] == jnp.array(held, jnp.int32)[None, :]
    weights = jnp.sum(jnp.where(entry[:, :, None, None], mine[None], 0.0), axis=1)
    scales = jnp.sum(jnp.where(entry[:, :, None], routing[None, :, -1], 0.0), axis=1)

    outcomes = {}

    def outcome(step, behind):
        offsets = (-step % count, step) if 0 < step < ring.half else (step,)
        weight = jnp.concatenate([weights[o] for o in offsets], axis=1)
        scale = jnp.concatenate([scales[o] for o in offsets], axis=0)
        outcomes[step] = after_hidden(after(pre[step][0], behind), pre[step][1], weight, scale)

    def expert_term(offset, behind):
        step = abs(offset)
        if step == ring.half and step > 1:
            outcome(step - 1, pre[step][0] + pre[step - 2][1])
            behind = [outcomes[step - 1]]
        if step not in outcomes:
            outcome(step, behind)
        if step in (0, ring.half):
            return outcomes[step]
        return outcomes[step][token_rows:] if offset > 0 else outcomes[step][:token_rows]

    return (residual_state + scatter_rows(ring, expert_term)).astype(bf16)


def solution(mesh):
    return jax.shard_map(
        functools.partial(per_device, mesh.shape["exp"]),
        mesh=mesh,
        in_specs=(
            P(("groups", "exp"), "ctx"),
            P(("groups", "ctx"), "exp"),
            P(("groups", "ctx"), "exp"),
            P(("groups", "ctx"), None),
            P(("groups", "ctx"), None),
            P(None, "exp"),
            P(None, "exp"),
            P("exp", "ctx"),
            P("ctx"),
            P("exp", "ctx", None),
            P("exp", "ctx", None),
            P("exp", None, "ctx"),
            P(("groups", "exp"), None),
            P(("groups", "exp"), None),
            P("groups"),
        ),
        out_specs=P(("groups", "exp"), "ctx"),
        check_vma=False,
    )
```

```python
import functools
import math

import jax
import jax.numpy as jnp
from jax import lax
from jax.experimental import pallas as pl
from jax.experimental.pallas import tpu as pltpu
from jax.sharding import PartitionSpec as P

D = 3584
NOPE = 128
ROPE = 64
VDIM = 128
BLOCK = 512

neg_large = -1e30
route_factor = 2.5
norm_epsilon = 1e-06
f32 = jnp.float32
bf16 = jnp.bfloat16


def attention_kernel(
    order_ref, q_nope_ref, q_rope_ref, own_latent_ref, other_latent_ref, own_rope_ref, other_rope_ref, w_uk_ref, w_uv_ref, out_ref
):
    core = lax.axis_index("ctx")
    rank_of = lambda block: order_ref[block]
    scale = (NOPE + ROPE) ** (-0.5) * math.log2(math.e)
    rows = q_nope_ref.shape[0]
    blocks = rows // BLOCK
    step = 256
    keys_t, values = [], []
    for latent_ref in (own_latent_ref, other_latent_ref):
        latent = latent_ref[...]
        keys_t.append(
            lax.dot_general(w_uk_ref[...], latent, (((0,), (1,)), ((), ())), preferred_element_type=f32).astype(bf16)
        )
        values.append(jnp.dot(latent, w_uv_ref[...], preferred_element_type=f32).astype(bf16))
    ropes = (own_rope_ref[...], other_rope_ref[...])
    blank = jnp.zeros_like(ropes[0])
    diagonal = lax.broadcasted_iota(jnp.int32, (step, step), 1) <= lax.broadcasted_iota(jnp.int32, (step, step), 0)
    key_cat, value_cat = [], []
    for head in range(2):
        cols = slice(head * NOPE, (head + 1) * NOPE)
        key_cat.append([
            jnp.concatenate([keys[cols, :]] + ([rope, blank] if head == 0 else [blank, rope]), axis=0)
            for keys, rope in zip(keys_t, ropes)
        ])
        value_cat.append([jnp.concatenate([held[:, cols], jnp.ones_like(held[:, cols])], axis=1) for held in values])

    def score(head, first):
        cols, part = slice(head * NOPE, (head + 1) * NOPE), slice(first, first + step)
        query = jnp.concatenate([q_nope_ref[part, cols], q_rope_ref[part, :]], axis=1)
        query_block, inside = first // BLOCK, first % BLOCK
        scores = []
        for side in (0, 1):
            owner = core if side == 0 else 1 - core
            for block in range(blocks):
                start = block * BLOCK
                if side == 0 and block == query_block:
                    seen = slice(start, start + inside + step)
                    piece = jnp.dot(query, key_cat[head][side][:, seen], preferred_element_type=f32)
                    last = jnp.where(diagonal, piece[:, inside:], neg_large)
                    piece = jnp.concatenate([piece[:, :inside], last], axis=1) if inside else last
                else:
                    seen = slice(start, start + BLOCK)
                    piece = jnp.dot(query, key_cat[head][side][:, seen], preferred_element_type=f32)
                    earlier = rank_of(owner * blocks + block) < rank_of(core * blocks + query_block)
                    piece = piece + jnp.where(earlier, 0.0, neg_large)
                scores.append((side, seen, piece))
        return scores

    units = [(head, first) for first in range(0, rows, step) for head in range(2)]
    ready = score(*units[0])
    for number, (head, first) in enumerate(units):
        scores = ready
        if number + 1 < len(units):
            ready = score(*units[number + 1])
        best = functools.reduce(jnp.maximum, [jnp.max(piece, axis=1, keepdims=True) for _, _, piece in scores])
        summed = 0.0
        for side, seen, piece in scores:
            probs = jnp.exp2((piece - best) * scale).astype(bf16)
            summed = summed + jnp.dot(probs, value_cat[head][side][seen, :], preferred_element_type=f32)
        out_ref[first : first + step, head * VDIM : (head + 1) * VDIM] = (summed[:, :VDIM] / summed[:, VDIM:]).astype(bf16)


def attend(block_order, q_nope, q_rope, latents, ropes, w_uk, w_uv):
    rows, keys = q_nope.shape[0], 2 * latents[0].shape[0]
    pairs = q_nope.shape[1] // (2 * NOPE)
    held = lambda array: pltpu.with_memory_space_constraint(array, pltpu.HBM)
    whole = lambda array: pl.BlockSpec(array.shape, lambda h, s: (0, 0))
    column = lambda array, width: pl.BlockSpec((array.shape[0], width), lambda h, s: (0, h))
    return pl.pallas_call(
        attention_kernel,
        grid_spec=pltpu.PrefetchScalarGridSpec(
            num_scalar_prefetch=1,
            grid=(pairs,),
            in_specs=[column(q_nope, 2 * NOPE), column(q_rope, 2 * ROPE)]
            + [whole(array) for array in (*latents, *ropes)]
            + [column(w_uk, 2 * NOPE), column(w_uv, 2 * VDIM)],
            out_specs=column(q_nope, 2 * VDIM),
        ),
        out_shape=jax.ShapeDtypeStruct((rows, q_nope.shape[1]), bf16),
        compiler_params=pltpu.CompilerParams(vmem_limit_bytes=12 * 1024 * 1024),
        cost_estimate=pl.CostEstimate(
            flops=7 * rows * keys * pairs * 2 * 384, bytes_accessed=8 * 1024 * 1024, transcendentals=rows * keys * pairs * 2
        ),
    )(held(block_order), held(q_nope), held(q_rope), held(latents[0]), latents[1], held(ropes[0]), ropes[1], held(w_uk), held(w_uv))


class Ring:
    def __init__(self, count):
        self.count, self.half = count, count // 2
        self.grid = count == 8
        order = [(2 * p if p < count // 2 else 2 * count - 1 - 2 * p) if self.grid else p for p in range(count)]
        self.up = [(order[p], order[(p + 1) % count]) for p in range(count)]
        self.down = [(t, s) for s, t in self.up]
        index = lax.axis_index("exp")
        self.place = jnp.where(index % 2 == 0, index // 2, count - 1 - index // 2) if self.grid else index

    def index_at(self, place):
        return jnp.where(place < self.half, 2 * place, 2 * self.count - 1 - 2 * place) if self.grid else place

    def at(self, offset):
        return self.index_at(lax.rem(self.place + offset, self.count))

    def send(self, block, way):
        return lax.ppermute(block, "exp", self.up if way > 0 else self.down)


def after(blocks, work):
    if not work:
        return blocks
    held = lax.optimization_barrier((tuple(blocks), tuple(work)))
    return list(held[0])


def scatter_rows(ring, part):
    add = lambda *terms: functools.reduce(jnp.add, [t.astype(f32) for t in terms])
    far = part(ring.half, [])
    sent = [far]
    cut = far.shape[0] // 2
    going = {1: ring.send(far[:cut], 1), -1: ring.send(far[cut:], -1)}
    for offset in range(ring.half - 1, 0, -1):
        behind, sent = sent, []
        for way in (1, -1):
            own, come = part(way * offset, behind), going[way]
            if offset == ring.half - 1:
                come = jnp.pad(come, ((0, cut) if way > 0 else (cut, 0), (0, 0)))
            block = add(own, come).astype(bf16)
            sent.append(block)
            going[way] = ring.send(block, way)
    return add(part(0, sent), going[1], going[-1])


def per_device(
    count,
    resid,
    q_nope,
    q_rope,
    latent,
    k_rope,
    w_uk,
    w_uv,
    w_out,
    norm_gain,
    w_gate,
    w_up,
    w_down,
    routes,
    codes,
    block_order,
):
    token_rows, owned = resid.shape[0], w_gate.shape[0]
    cut = token_rows // 2
    ring = Ring(count)
    core, index = lax.axis_index("ctx"), lax.axis_index("exp")
    swap = lambda block: lax.ppermute(block, "ctx", [(0, 1), (1, 0)])

    ropes = k_rope.T
    heads = attend(
        block_order, q_nope, q_rope, (latent, swap(latent)), (ropes, swap(ropes)), w_uk, w_uv
    )

    other_heads = swap(heads)
    project = lambda rows: jnp.dot(rows, w_out, preferred_element_type=f32).astype(bf16)

    def block_of(offset):
        return jnp.bitwise_and(ring.at(offset % count) - core * ring.half, count - 1)

    def pick(own, other, block):
        first = jnp.minimum(block, ring.half - 1) * token_rows
        second = jnp.maximum(block - ring.half, 0) * token_rows
        part = lambda rows, at: lax.dynamic_slice_in_dim(rows, at, token_rows, 0, allow_negative_indices=False)
        return jnp.where(block < ring.half, part(own, first), part(other, second))

    nearby = {}

    def attention_term(offset, behind):
        if abs(offset) >= ring.half - 1:
            rows = pick(heads, other_heads, block_of(offset))
            return lax.optimization_barrier(project(after([rows], behind)[0]))
        if not nearby:
            later = after([heads, other_heads], behind)
            nearby["terms"] = [project(rows) for rows in later]
        return lax.optimization_barrier(pick(*nearby["terms"], block_of(offset)))

    residual_state = resid.astype(f32) + scatter_rows(ring, attention_term)

    code_values = codes.astype(f32)
    route_weight = route_factor * code_values / jnp.sum(code_values, axis=1, keepdims=True)
    named = routes[None] == jnp.arange(count * owned, dtype=jnp.int32)[:, None, None]
    routing = jnp.sum(jnp.where(named, route_weight[None], 0.0), axis=2)[None]
    scaled = (residual_state * norm_gain).astype(bf16)
    squares = jnp.sum(residual_state * residual_state, axis=1)
    squares = squares + swap(squares)
    inverse_rms = lax.rsqrt(squares / D + norm_epsilon)
    routing = jnp.concatenate([routing, inverse_rms[None, None]], axis=1)

    def before_hidden(rows):
        product = lambda weight: jnp.einsum("td,ldf->ltf", rows, weight, preferred_element_type=f32).astype(bf16)
        own = [product(w_gate), product(w_up)]
        return own, [swap(pre) for pre in own]

    def after_hidden(own, other, weight, scale):
        gate_pre, up_pre = [mine.astype(f32) + theirs.astype(f32) for mine, theirs in zip(own, other)]
        gate_pre = gate_pre * scale[:, None]
        hidden = (jax.nn.silu(gate_pre) * up_pre * (weight * scale)[:, :, None]).astype(bf16)
        return functools.reduce(
            jnp.add, [jnp.dot(hidden[e], w_down[e], preferred_element_type=f32) for e in range(owned)]
        ).astype(bf16)

    pre = [before_hidden(scaled)]
    below = above = scaled
    hops = count.bit_length() - 1
    far_first = [count >> (1 + number) for number in range(hops)]

    def hop(routing, number):
        other = lax.ppermute(routing, "exp", [(i, i ^ far_first[number]) for i in range(count)])
        return jnp.concatenate([routing, other], axis=0)

    for step in range(1, ring.half + 1):
        if step > 1:
            work = pre[step - 2][0] + (pre[0][1] if step == 3 else [])
            if step <= hops:
                (routing,) = after([hop(routing, step - 2)], [below])
                work = work + [routing]
            below, above = after([below, above], work)
        if step == ring.half:
            below, above = below[:cut], above[cut:]
        below, above = ring.send(below, 1), ring.send(above, -1)
        rows = jnp.concatenate([below, above], axis=0)
        if step == ring.half:
            for number in range(min(step - 1, hops - 1), hops):
                routing = hop(routing, number)
            (rows,) = after([rows], pre[step - 1][0] + (pre[step - 3][1] if step > 2 else []))
        pre.append(before_hidden(rows))

    mine = lax.dynamic_slice_in_dim(routing, index * owned, owned, 1, allow_negative_indices=False)
    offsets = jnp.arange(count, dtype=jnp.int32)
    held = [sum(bit for number, bit in enumerate(far_first) if p >> number & 1) for p in range(count)]
    entry = jnp.bitwise_xor(ring.at(offsets), index)[:, None] == jnp.array(held, jnp.int32)[None, :]
    weights = jnp.sum(jnp.where(entry[:, :, None, None], mine[None], 0.0), axis=1)
    scales = jnp.sum(jnp.where(entry[:, :, None], routing[None, :, -1], 0.0), axis=1)

    outcomes = {}

    def outcome(step, behind):
        offsets = (-step % count, step) if 0 < step < ring.half else (step,)
        weight = jnp.concatenate([weights[o] for o in offsets], axis=1)
        scale = jnp.concatenate([scales[o] for o in offsets], axis=0)
        outcomes[step] = after_hidden(after(pre[step][0], behind), pre[step][1], weight, scale)

    def expert_term(offset, behind):
        step = abs(offset)
        if step == ring.half and step > 1:
            outcome(step - 1, pre[step][0] + pre[step - 2][1])
            behind = [outcomes[step - 1]]
        if step not in outcomes:
            outcome(step, behind)
        if step in (0, ring.half):
            return outcomes[step]
        return outcomes[step][token_rows:] if offset > 0 else outcomes[step][:token_rows]

    return (residual_state + scatter_rows(ring, expert_term)).astype(bf16)


def solution(mesh):
    return jax.shard_map(
        functools.partial(per_device, mesh.shape["exp"]),
        mesh=mesh,
        in_specs=(
            P(("groups", "exp"), "ctx"),
            P(("groups", "ctx"), "exp"),
            P(("groups", "ctx"), "exp"),
            P(("groups", "ctx"), None),
            P(("groups", "ctx"), None),
            P(None, "exp"),
            P(None, "exp"),
            P("exp", "ctx"),
            P("ctx"),
            P("exp", "ctx", None),
            P("exp", "ctx", None),
            P("exp", None, "ctx"),
            P(("groups", "exp"), None),
            P(("groups", "exp"), None),
            P("groups"),
        ),
        out_specs=P(("groups", "exp"), "ctx"),
        check_vma=False,
    )
```

```python
import functools
import math

import jax
import jax.numpy as jnp
from jax import lax
from jax.experimental import pallas as pl
from jax.experimental.pallas import tpu as pltpu
from jax.sharding import PartitionSpec as P

D = 3584
NOPE = 128
ROPE = 64
VDIM = 128
BLOCK = 512

neg_large = -1e30
route_factor = 2.5
norm_epsilon = 1e-06
f32 = jnp.float32
bf16 = jnp.bfloat16


def attention_kernel(
    order_ref, q_nope_ref, q_rope_ref, own_latent_ref, other_latent_ref, own_rope_ref, other_rope_ref, w_uk_ref, w_uv_ref, out_ref
):
    core = lax.axis_index("ctx")
    rank_of = lambda block: order_ref[block]
    scale = (NOPE + ROPE) ** (-0.5) * math.log2(math.e)
    rows = q_nope_ref.shape[0]
    blocks = rows // BLOCK
    step = 256
    keys_t, values = [], []
    for latent_ref in (own_latent_ref, other_latent_ref):
        latent = latent_ref[...]
        keys_t.append(
            lax.dot_general(w_uk_ref[...], latent, (((0,), (1,)), ((), ())), preferred_element_type=f32).astype(bf16)
        )
        values.append(jnp.dot(latent, w_uv_ref[...], preferred_element_type=f32).astype(bf16))
    ropes = (own_rope_ref[...], other_rope_ref[...])
    blank = jnp.zeros_like(ropes[0])
    diagonal = lax.broadcasted_iota(jnp.int32, (step, step), 1) <= lax.broadcasted_iota(jnp.int32, (step, step), 0)
    key_cat, value_cat = [], []
    for head in range(2):
        cols = slice(head * NOPE, (head + 1) * NOPE)
        key_cat.append([
            jnp.concatenate([keys[cols, :]] + ([rope, blank] if head == 0 else [blank, rope]), axis=0)
            for keys, rope in zip(keys_t, ropes)
        ])
        value_cat.append([jnp.concatenate([held[:, cols], jnp.ones_like(held[:, cols])], axis=1) for held in values])

    def score(head, first):
        cols, part = slice(head * NOPE, (head + 1) * NOPE), slice(first, first + step)
        query = jnp.concatenate([q_nope_ref[part, cols], q_rope_ref[part, :]], axis=1)
        query_block, inside = first // BLOCK, first % BLOCK
        scores = []
        for side in (0, 1):
            owner = core if side == 0 else 1 - core
            for block in range(blocks):
                start = block * BLOCK
                if side == 0 and block == query_block:
                    seen = slice(start, start + inside + step)
                    piece = jnp.dot(query, key_cat[head][side][:, seen], preferred_element_type=f32)
                    last = jnp.where(diagonal, piece[:, inside:], neg_large)
                    piece = jnp.concatenate([piece[:, :inside], last], axis=1) if inside else last
                else:
                    seen = slice(start, start + BLOCK)
                    piece = jnp.dot(query, key_cat[head][side][:, seen], preferred_element_type=f32)
                    earlier = rank_of(owner * blocks + block) < rank_of(core * blocks + query_block)
                    piece = piece + jnp.where(earlier, 0.0, neg_large)
                scores.append((side, seen, piece))
        return scores

    units = [(head, first) for first in range(0, rows, step) for head in range(2)]
    ready = score(*units[0])
    for number, (head, first) in enumerate(units):
        scores = ready
        if number + 1 < len(units):
            ready = score(*units[number + 1])
        best = functools.reduce(jnp.maximum, [jnp.max(piece, axis=1, keepdims=True) for _, _, piece in scores])
        summed = 0.0
        for side, seen, piece in scores:
            probs = jnp.exp2((piece - best) * scale).astype(bf16)
            summed = summed + jnp.dot(probs, value_cat[head][side][seen, :], preferred_element_type=f32)
        out_ref[first : first + step, head * VDIM : (head + 1) * VDIM] = (summed[:, :VDIM] / summed[:, VDIM:]).astype(bf16)


def attend(block_order, q_nope, q_rope, latents, ropes, w_uk, w_uv):
    rows, keys = q_nope.shape[0], 2 * latents[0].shape[0]
    pairs = q_nope.shape[1] // (2 * NOPE)
    held = lambda array: pltpu.with_memory_space_constraint(array, pltpu.HBM)
    whole = lambda array: pl.BlockSpec(array.shape, lambda h, s: (0, 0))
    column = lambda array, width: pl.BlockSpec((array.shape[0], width), lambda h, s: (0, h))
    return pl.pallas_call(
        attention_kernel,
        grid_spec=pltpu.PrefetchScalarGridSpec(
            num_scalar_prefetch=1,
            grid=(pairs,),
            in_specs=[column(q_nope, 2 * NOPE), column(q_rope, 2 * ROPE)]
            + [whole(array) for array in (*latents, *ropes)]
            + [column(w_uk, 2 * NOPE), column(w_uv, 2 * VDIM)],
            out_specs=column(q_nope, 2 * VDIM),
        ),
        out_shape=jax.ShapeDtypeStruct((rows, q_nope.shape[1]), bf16),
        compiler_params=pltpu.CompilerParams(vmem_limit_bytes=12 * 1024 * 1024),
        cost_estimate=pl.CostEstimate(
            flops=7 * rows * keys * pairs * 2 * 384, bytes_accessed=8 * 1024 * 1024, transcendentals=rows * keys * pairs * 2
        ),
    )(held(block_order), held(q_nope), held(q_rope), held(latents[0]), latents[1], held(ropes[0]), ropes[1], held(w_uk), held(w_uv))


def product_kernel(rows_ref, weight_ref, out_ref):
    terms = [jnp.dot(rows_ref[e], weight_ref[e], preferred_element_type=f32) for e in range(rows_ref.shape[0])]
    out_ref[...] = functools.reduce(jnp.add, terms).astype(bf16)


def product(rows, weights):
    terms, count, depth = rows.shape
    width = weights.shape[2]
    tile = 256
    return pl.pallas_call(
        product_kernel,
        grid=(width // tile,),
        in_specs=[
            pl.BlockSpec((terms, count, depth), lambda n: (0, 0, 0)),
            pl.BlockSpec((terms, depth, tile), lambda n: (0, 0, n)),
        ],
        out_specs=pl.BlockSpec((count, tile), lambda n: (0, n)),
        out_shape=jax.ShapeDtypeStruct((count, width), bf16),
        compiler_params=pltpu.CompilerParams(vmem_limit_bytes=12 * 1024 * 1024),
        cost_estimate=pl.CostEstimate(flops=count * depth * width // 4, bytes_accessed=count * width, transcendentals=0),
    )(rows, pltpu.with_memory_space_constraint(weights, pltpu.HBM))


class Ring:
    def __init__(self, count):
        self.count, self.half = count, count // 2
        self.grid = count == 8
        order = [(2 * p if p < count // 2 else 2 * count - 1 - 2 * p) if self.grid else p for p in range(count)]
        self.up = [(order[p], order[(p + 1) % count]) for p in range(count)]
        self.down = [(t, s) for s, t in self.up]
        index = lax.axis_index("exp")
        self.place = jnp.where(index % 2 == 0, index // 2, count - 1 - index // 2) if self.grid else index

    def index_at(self, place):
        return jnp.where(place < self.half, 2 * place, 2 * self.count - 1 - 2 * place) if self.grid else place

    def at(self, offset):
        return self.index_at(lax.rem(self.place + offset, self.count))

    def send(self, block, way):
        return lax.ppermute(block, "exp", self.up if way > 0 else self.down)


def after(blocks, work):
    if not work:
        return blocks
    held = lax.optimization_barrier((tuple(blocks), tuple(work)))
    return list(held[0])


def scatter_rows(ring, part):
    add = lambda *terms: functools.reduce(jnp.add, [t.astype(f32) for t in terms])
    far = part(ring.half, [])
    sent = [far]
    cut = far.shape[0] // 2
    going = {1: ring.send(far[:cut], 1), -1: ring.send(far[cut:], -1)}
    for offset in range(ring.half - 1, 0, -1):
        behind, sent = sent, []
        for way in (1, -1):
            own, come = part(way * offset, behind), going[way]
            if offset == ring.half - 1:
                come = jnp.pad(come, ((0, cut) if way > 0 else (cut, 0), (0, 0)))
            block = add(own, come).astype(bf16)
            sent.append(block)
            going[way] = ring.send(block, way)
    return add(part(0, sent), going[1], going[-1])


def per_device(
    count,
    resid,
    q_nope,
    q_rope,
    latent,
    k_rope,
    w_uk,
    w_uv,
    w_out,
    norm_gain,
    w_gate,
    w_up,
    w_down,
    routes,
    codes,
    block_order,
):
    token_rows, owned = resid.shape[0], w_gate.shape[0]
    cut = token_rows // 2
    ring = Ring(count)
    core, index = lax.axis_index("ctx"), lax.axis_index("exp")
    swap = lambda block: lax.ppermute(block, "ctx", [(0, 1), (1, 0)])

    ropes = k_rope.T
    heads = attend(
        block_order, q_nope, q_rope, (latent, swap(latent)), (ropes, swap(ropes)), w_uk, w_uv
    )

    other_heads = swap(heads)
    project = lambda rows: jnp.dot(rows, w_out, preferred_element_type=f32).astype(bf16)

    def block_of(offset):
        return jnp.bitwise_and(ring.at(offset % count) - core * ring.half, count - 1)

    def pick(own, other, block):
        first = jnp.minimum(block, ring.half - 1) * token_rows
        second = jnp.maximum(block - ring.half, 0) * token_rows
        part = lambda rows, at: lax.dynamic_slice_in_dim(rows, at, token_rows, 0, allow_negative_indices=False)
        return jnp.where(block < ring.half, part(own, first), part(other, second))

    nearby = {}

    def attention_term(offset, behind):
        if offset == ring.half:
            return product(pick(heads, other_heads, block_of(offset))[None], w_out[None])
        if abs(offset) == ring.half - 1:
            if "first" not in nearby:
                rows = [pick(heads, other_heads, block_of(way * abs(offset))) for way in (1, -1)]
                rows = after([jnp.concatenate(rows, axis=0)], behind)[0]
                nearby["first"] = product(rows[None], w_out[None])
            return nearby["first"][:token_rows] if offset > 0 else nearby["first"][token_rows:]
        if "terms" not in nearby:
            later = after([heads, other_heads], behind)
            nearby["terms"] = [project(rows) for rows in later]
        return lax.optimization_barrier(pick(*nearby["terms"], block_of(offset)))

    residual_state = resid.astype(f32) + scatter_rows(ring, attention_term)

    code_values = codes.astype(f32)
    route_weight = route_factor * code_values / jnp.sum(code_values, axis=1, keepdims=True)
    named = routes[None] == jnp.arange(count * owned, dtype=jnp.int32)[:, None, None]
    routing = jnp.sum(jnp.where(named, route_weight[None], 0.0), axis=2)[None]
    scaled = (residual_state * norm_gain).astype(bf16)
    squares = jnp.sum(residual_state * residual_state, axis=1)
    squares = squares + swap(squares)
    inverse_rms = lax.rsqrt(squares / D + norm_epsilon)
    routing = jnp.concatenate([routing, inverse_rms[None, None]], axis=1)

    def before_hidden(rows):
        product = lambda weight: jnp.einsum("td,ldf->ltf", rows, weight, preferred_element_type=f32).astype(bf16)
        own = [product(w_gate), product(w_up)]
        return own, [swap(pre) for pre in own]

    def hidden_of(own, other, weight, scale):
        gate_pre, up_pre = [mine.astype(f32) + theirs.astype(f32) for mine, theirs in zip(own, other)]
        gate_pre = gate_pre * scale[:, None]
        return (jax.nn.silu(gate_pre) * up_pre * (weight * scale)[:, :, None]).astype(bf16)

    def down(hidden):
        return functools.reduce(
            jnp.add, [jnp.dot(hidden[e], w_down[e], preferred_element_type=f32) for e in range(owned)]
        ).astype(bf16)

    pre = [before_hidden(scaled)]
    below = above = scaled
    hops = count.bit_length() - 1
    far_first = [count >> (1 + number) for number in range(hops)]

    def hop(routing, number):
        other = lax.ppermute(routing, "exp", [(i, i ^ far_first[number]) for i in range(count)])
        return jnp.concatenate([routing, other], axis=0)

    for step in range(1, ring.half + 1):
        if step > 1:
            work = pre[step - 2][0] + (pre[0][1] if step == 3 else [])
            if step <= hops:
                (routing,) = after([hop(routing, step - 2)], [below])
                work = work + [routing]
            below, above = after([below, above], work)
        if step == ring.half:
            below, above = below[:cut], above[cut:]
        below, above = ring.send(below, 1), ring.send(above, -1)
        rows = jnp.concatenate([below, above], axis=0)
        if step == ring.half:
            for number in range(min(step - 1, hops - 1), hops):
                routing = hop(routing, number)
            (rows,) = after([rows], pre[step - 1][0] + (pre[step - 3][1] if step > 2 else []))
        pre.append(before_hidden(rows))

    mine = lax.dynamic_slice_in_dim(routing, index * owned, owned, 1, allow_negative_indices=False)
    offsets = jnp.arange(count, dtype=jnp.int32)
    held = [sum(bit for number, bit in enumerate(far_first) if p >> number & 1) for p in range(count)]
    entry = jnp.bitwise_xor(ring.at(offsets), index)[:, None] == jnp.array(held, jnp.int32)[None, :]
    weights = jnp.sum(jnp.where(entry[:, :, None, None], mine[None], 0.0), axis=1)
    scales = jnp.sum(jnp.where(entry[:, :, None], routing[None, :, -1], 0.0), axis=1)

    outcomes = {}

    def hidden(step, behind):
        offsets = (-step % count, step) if 0 < step < ring.half else (step,)
        weight = jnp.concatenate([weights[o] for o in offsets], axis=1)
        scale = jnp.concatenate([scales[o] for o in offsets], axis=0)
        return hidden_of(after(pre[step][0], behind), pre[step][1], weight, scale)

    def expert_term(offset, behind):
        step = abs(offset)
        if step == ring.half:
            before = hidden(step - 1, pre[step][0] + pre[step - 2][1])
            outcomes[step] = down(hidden(step, [before]))
            outcomes[step - 1] = product(after([before], [outcomes[step]])[0], w_down)
        if step not in outcomes:
            outcomes[step] = down(hidden(step, behind))
        if step in (0, ring.half):
            return outcomes[step]
        return outcomes[step][token_rows:] if offset > 0 else outcomes[step][:token_rows]

    return (residual_state + scatter_rows(ring, expert_term)).astype(bf16)


def solution(mesh):
    return jax.shard_map(
        functools.partial(per_device, mesh.shape["exp"]),
        mesh=mesh,
        in_specs=(
            P(("groups", "exp"), "ctx"),
            P(("groups", "ctx"), "exp"),
            P(("groups", "ctx"), "exp"),
            P(("groups", "ctx"), None),
            P(("groups", "ctx"), None),
            P(None, "exp"),
            P(None, "exp"),
            P("exp", "ctx"),
            P("ctx"),
            P("exp", "ctx", None),
            P("exp", "ctx", None),
            P("exp", None, "ctx"),
            P(("groups", "exp"), None),
            P(("groups", "exp"), None),
            P("groups"),
        ),
        out_specs=P(("groups", "exp"), "ctx"),
        check_vma=False,
    )
```

```python
import functools
import math

import jax
import jax.numpy as jnp
from jax import lax
from jax.experimental import pallas as pl
from jax.experimental.pallas import tpu as pltpu
from jax.sharding import PartitionSpec as P

D = 3584
NOPE = 128
ROPE = 64
VDIM = 128
BLOCK = 512

neg_large = -1e30
route_factor = 2.5
norm_epsilon = 1e-06
f32 = jnp.float32
bf16 = jnp.bfloat16


def attention_kernel(
    order_ref, q_nope_ref, q_rope_ref, own_latent_ref, other_latent_ref, own_rope_ref, other_rope_ref, w_uk_ref, w_uv_ref, out_ref
):
    core = lax.axis_index("ctx")
    rank_of = lambda block: order_ref[block]
    scale = (NOPE + ROPE) ** (-0.5) * math.log2(math.e)
    rows = q_nope_ref.shape[0]
    blocks = rows // BLOCK
    step = 256
    keys_t, values = [], []
    for latent_ref in (own_latent_ref, other_latent_ref):
        latent = latent_ref[...]
        keys_t.append(
            lax.dot_general(w_uk_ref[...], latent, (((0,), (1,)), ((), ())), preferred_element_type=f32).astype(bf16)
        )
        values.append(jnp.dot(latent, w_uv_ref[...], preferred_element_type=f32).astype(bf16))
    ropes = (own_rope_ref[...], other_rope_ref[...])
    blank = jnp.zeros_like(ropes[0])
    diagonal = lax.broadcasted_iota(jnp.int32, (step, step), 1) <= lax.broadcasted_iota(jnp.int32, (step, step), 0)
    key_cat, value_cat = [], []
    for head in range(2):
        cols = slice(head * NOPE, (head + 1) * NOPE)
        key_cat.append([
            jnp.concatenate([keys[cols, :]] + ([rope, blank] if head == 0 else [blank, rope]), axis=0)
            for keys, rope in zip(keys_t, ropes)
        ])
        value_cat.append([jnp.concatenate([held[:, cols], jnp.ones_like(held[:, cols])], axis=1) for held in values])

    def score(head, first):
        cols, part = slice(head * NOPE, (head + 1) * NOPE), slice(first, first + step)
        query = jnp.concatenate([q_nope_ref[part, cols], q_rope_ref[part, :]], axis=1)
        query_block, inside = first // BLOCK, first % BLOCK
        scores = []
        for side in (0, 1):
            owner = core if side == 0 else 1 - core
            for block in range(blocks):
                start = block * BLOCK
                if side == 0 and block == query_block:
                    seen = slice(start, start + inside + step)
                    piece = jnp.dot(query, key_cat[head][side][:, seen], preferred_element_type=f32)
                    last = jnp.where(diagonal, piece[:, inside:], neg_large)
                    piece = jnp.concatenate([piece[:, :inside], last], axis=1) if inside else last
                else:
                    seen = slice(start, start + BLOCK)
                    piece = jnp.dot(query, key_cat[head][side][:, seen], preferred_element_type=f32)
                    earlier = rank_of(owner * blocks + block) < rank_of(core * blocks + query_block)
                    piece = piece + jnp.where(earlier, 0.0, neg_large)
                scores.append((side, seen, piece))
        return scores

    units = [(head, first) for first in range(0, rows, step) for head in range(2)]
    ready = score(*units[0])
    for number, (head, first) in enumerate(units):
        scores = ready
        if number + 1 < len(units):
            ready = score(*units[number + 1])
        best = functools.reduce(jnp.maximum, [jnp.max(piece, axis=1, keepdims=True) for _, _, piece in scores])
        summed = 0.0
        for side, seen, piece in scores:
            probs = jnp.exp2((piece - best) * scale).astype(bf16)
            summed = summed + jnp.dot(probs, value_cat[head][side][seen, :], preferred_element_type=f32)
        out_ref[first : first + step, head * VDIM : (head + 1) * VDIM] = (summed[:, :VDIM] / summed[:, VDIM:]).astype(bf16)


def attend(block_order, q_nope, q_rope, latents, ropes, w_uk, w_uv):
    rows, keys = q_nope.shape[0], 2 * latents[0].shape[0]
    pairs = q_nope.shape[1] // (2 * NOPE)
    held = lambda array: pltpu.with_memory_space_constraint(array, pltpu.HBM)
    whole = lambda array: pl.BlockSpec(array.shape, lambda h, s: (0, 0))
    column = lambda array, width: pl.BlockSpec((array.shape[0], width), lambda h, s: (0, h))
    return pl.pallas_call(
        attention_kernel,
        grid_spec=pltpu.PrefetchScalarGridSpec(
            num_scalar_prefetch=1,
            grid=(pairs,),
            in_specs=[column(q_nope, 2 * NOPE), column(q_rope, 2 * ROPE)]
            + [whole(array) for array in (*latents, *ropes)]
            + [column(w_uk, 2 * NOPE), column(w_uv, 2 * VDIM)],
            out_specs=column(q_nope, 2 * VDIM),
        ),
        out_shape=jax.ShapeDtypeStruct((rows, q_nope.shape[1]), bf16),
        compiler_params=pltpu.CompilerParams(vmem_limit_bytes=12 * 1024 * 1024),
        cost_estimate=pl.CostEstimate(
            flops=7 * rows * keys * pairs * 2 * 384, bytes_accessed=8 * 1024 * 1024, transcendentals=rows * keys * pairs * 2
        ),
    )(held(block_order), held(q_nope), held(q_rope), held(latents[0]), latents[1], held(ropes[0]), ropes[1], held(w_uk), held(w_uv))


def product_kernel(rows_ref, *refs):
    *weight_refs, out_ref = refs
    depth = weight_refs[0].shape[1]
    terms = [
        jnp.dot(rows_ref[e, :, q * depth : (q + 1) * depth], ref[e], preferred_element_type=f32)
        for q, ref in enumerate(weight_refs)
        for e in range(rows_ref.shape[0])
    ]
    out_ref[...] = functools.reduce(jnp.add, terms).astype(bf16)


def product(rows, weights):
    terms, count, depth = rows.shape
    width = weights.shape[2]
    tile, pieces = width // 2, 4
    weights = pltpu.with_memory_space_constraint(weights, pltpu.HBM)
    piece = lambda q: pl.BlockSpec((terms, depth // pieces, tile), lambda n: (0, q, n))
    return pl.pallas_call(
        product_kernel,
        grid=(width // tile,),
        in_specs=[pl.BlockSpec((terms, count, depth), lambda n: (0, 0, 0))] + [piece(q) for q in range(pieces)],
        out_specs=pl.BlockSpec((count, tile), lambda n: (0, n)),
        out_shape=jax.ShapeDtypeStruct((count, width), bf16),
        compiler_params=pltpu.CompilerParams(vmem_limit_bytes=16 * 1024 * 1024),
        cost_estimate=pl.CostEstimate(flops=count * depth * width // 4, bytes_accessed=count * width, transcendentals=0),
    )(rows, *[weights] * pieces)


class Ring:
    def __init__(self, count):
        self.count, self.half = count, count // 2
        self.grid = count == 8
        order = [(2 * p if p < count // 2 else 2 * count - 1 - 2 * p) if self.grid else p for p in range(count)]
        self.up = [(order[p], order[(p + 1) % count]) for p in range(count)]
        self.down = [(t, s) for s, t in self.up]
        index = lax.axis_index("exp")
        self.place = jnp.where(index % 2 == 0, index // 2, count - 1 - index // 2) if self.grid else index

    def index_at(self, place):
        return jnp.where(place < self.half, 2 * place, 2 * self.count - 1 - 2 * place) if self.grid else place

    def at(self, offset):
        return self.index_at(lax.rem(self.place + offset, self.count))

    def send(self, block, way):
        return lax.ppermute(block, "exp", self.up if way > 0 else self.down)


def after(blocks, work):
    if not work:
        return blocks
    held = lax.optimization_barrier((tuple(blocks), tuple(work)))
    return list(held[0])


def scatter_rows(ring, part):
    add = lambda *terms: functools.reduce(jnp.add, [t.astype(f32) for t in terms])
    far = part(ring.half, [])
    sent = [far]
    cut = far.shape[0] // 2
    going = {1: ring.send(far[:cut], 1), -1: ring.send(far[cut:], -1)}
    for offset in range(ring.half - 1, 0, -1):
        behind, sent = sent, []
        for way in (1, -1):
            own, come = part(way * offset, behind), going[way]
            if offset == ring.half - 1:
                come = jnp.pad(come, ((0, cut) if way > 0 else (cut, 0), (0, 0)))
            block = add(own, come).astype(bf16)
            sent.append(block)
            going[way] = ring.send(block, way)
    return add(part(0, sent), going[1], going[-1])


def per_device(
    count,
    resid,
    q_nope,
    q_rope,
    latent,
    k_rope,
    w_uk,
    w_uv,
    w_out,
    norm_gain,
    w_gate,
    w_up,
    w_down,
    routes,
    codes,
    block_order,
):
    token_rows, owned = resid.shape[0], w_gate.shape[0]
    cut = token_rows // 2
    ring = Ring(count)
    core, index = lax.axis_index("ctx"), lax.axis_index("exp")
    swap = lambda block: lax.ppermute(block, "ctx", [(0, 1), (1, 0)])

    ropes = k_rope.T
    heads = attend(
        block_order, q_nope, q_rope, (latent, swap(latent)), (ropes, swap(ropes)), w_uk, w_uv
    )

    other_heads = swap(heads)
    project = lambda rows: jnp.dot(rows, w_out, preferred_element_type=f32).astype(bf16)

    def block_of(offset):
        return jnp.bitwise_and(ring.at(offset % count) - core * ring.half, count - 1)

    def pick(own, other, block):
        first = jnp.minimum(block, ring.half - 1) * token_rows
        second = jnp.maximum(block - ring.half, 0) * token_rows
        part = lambda rows, at: lax.dynamic_slice_in_dim(rows, at, token_rows, 0, allow_negative_indices=False)
        return jnp.where(block < ring.half, part(own, first), part(other, second))

    nearby = {}

    def attention_term(offset, behind):
        if offset == ring.half:
            return product(pick(heads, other_heads, block_of(offset))[None], w_out[None])
        if abs(offset) == ring.half - 1:
            if "first" not in nearby:
                rows = [pick(heads, other_heads, block_of(way * abs(offset))) for way in (1, -1)]
                rows = after([jnp.concatenate(rows, axis=0)], behind)[0]
                nearby["first"] = product(rows[None], w_out[None])
            return nearby["first"][:token_rows] if offset > 0 else nearby["first"][token_rows:]
        if "terms" not in nearby:
            later = after([heads, other_heads], behind)
            nearby["terms"] = [project(rows) for rows in later]
        return lax.optimization_barrier(pick(*nearby["terms"], block_of(offset)))

    residual_state = resid.astype(f32) + scatter_rows(ring, attention_term)

    code_values = codes.astype(f32)
    route_weight = route_factor * code_values / jnp.sum(code_values, axis=1, keepdims=True)
    named = routes[None] == jnp.arange(count * owned, dtype=jnp.int32)[:, None, None]
    routing = jnp.sum(jnp.where(named, route_weight[None], 0.0), axis=2)[None]
    scaled = (residual_state * norm_gain).astype(bf16)
    squares = jnp.sum(residual_state * residual_state, axis=1)
    squares = squares + swap(squares)
    inverse_rms = lax.rsqrt(squares / D + norm_epsilon)
    routing = jnp.concatenate([routing, inverse_rms[None, None]], axis=1)

    def before_hidden(rows):
        product = lambda weight: jnp.einsum("td,ldf->ltf", rows, weight, preferred_element_type=f32).astype(bf16)
        own = [product(w_gate), product(w_up)]
        return own, [swap(pre) for pre in own]

    def hidden_of(own, other, weight, scale):
        gate_pre, up_pre = [mine.astype(f32) + theirs.astype(f32) for mine, theirs in zip(own, other)]
        gate_pre = gate_pre * scale[:, None]
        return (jax.nn.silu(gate_pre) * up_pre * (weight * scale)[:, :, None]).astype(bf16)

    def down(hidden):
        return functools.reduce(
            jnp.add, [jnp.dot(hidden[e], w_down[e], preferred_element_type=f32) for e in range(owned)]
        ).astype(bf16)

    pre = [before_hidden(scaled)]
    below = above = scaled
    hops = count.bit_length() - 1
    far_first = [count >> (1 + number) for number in range(hops)]

    def hop(routing, number):
        other = lax.ppermute(routing, "exp", [(i, i ^ far_first[number]) for i in range(count)])
        return jnp.concatenate([routing, other], axis=0)

    for step in range(1, ring.half + 1):
        if step > 1:
            work = pre[step - 2][0] + (pre[0][1] if step == 3 else [])
            if step <= hops:
                (routing,) = after([hop(routing, step - 2)], [below])
                work = work + [routing]
            below, above = after([below, above], work)
        if step == ring.half:
            below, above = below[:cut], above[cut:]
        below, above = ring.send(below, 1), ring.send(above, -1)
        rows = jnp.concatenate([below, above], axis=0)
        if step == ring.half:
            for number in range(min(step - 1, hops - 1), hops):
                routing = hop(routing, number)
            (rows,) = after([rows], pre[step - 1][0] + (pre[step - 3][1] if step > 2 else []))
        pre.append(before_hidden(rows))

    mine = lax.dynamic_slice_in_dim(routing, index * owned, owned, 1, allow_negative_indices=False)
    offsets = jnp.arange(count, dtype=jnp.int32)
    held = [sum(bit for number, bit in enumerate(far_first) if p >> number & 1) for p in range(count)]
    entry = jnp.bitwise_xor(ring.at(offsets), index)[:, None] == jnp.array(held, jnp.int32)[None, :]
    weights = jnp.sum(jnp.where(entry[:, :, None, None], mine[None], 0.0), axis=1)
    scales = jnp.sum(jnp.where(entry[:, :, None], routing[None, :, -1], 0.0), axis=1)

    outcomes = {}

    def hidden(step, behind):
        offsets = (-step % count, step) if 0 < step < ring.half else (step,)
        weight = jnp.concatenate([weights[o] for o in offsets], axis=1)
        scale = jnp.concatenate([scales[o] for o in offsets], axis=0)
        return hidden_of(after(pre[step][0], behind), pre[step][1], weight, scale)

    def expert_term(offset, behind):
        step = abs(offset)
        if step == ring.half:
            before = hidden(step - 1, pre[step][0] + pre[step - 2][1])
            outcomes[step] = down(hidden(step, [before]))
            outcomes[step - 1] = product(after([before], [outcomes[step]])[0], w_down)
        if step not in outcomes:
            outcomes[step] = down(hidden(step, behind))
        if step in (0, ring.half):
            return outcomes[step]
        return outcomes[step][token_rows:] if offset > 0 else outcomes[step][:token_rows]

    return (residual_state + scatter_rows(ring, expert_term)).astype(bf16)


def solution(mesh):
    return jax.shard_map(
        functools.partial(per_device, mesh.shape["exp"]),
        mesh=mesh,
        in_specs=(
            P(("groups", "exp"), "ctx"),
            P(("groups", "ctx"), "exp"),
            P(("groups", "ctx"), "exp"),
            P(("groups", "ctx"), None),
            P(("groups", "ctx"), None),
            P(None, "exp"),
            P(None, "exp"),
            P("exp", "ctx"),
            P("ctx"),
            P("exp", "ctx", None),
            P("exp", "ctx", None),
            P("exp", None, "ctx"),
            P(("groups", "exp"), None),
            P(("groups", "exp"), None),
            P("groups"),
        ),
        out_specs=P(("groups", "exp"), "ctx"),
        check_vma=False,
    )
```

```python
import functools
import math

import jax
import jax.numpy as jnp
from jax import lax
from jax.experimental import pallas as pl
from jax.experimental.pallas import tpu as pltpu
from jax.sharding import PartitionSpec as P

D = 3584
NOPE = 128
ROPE = 64
VDIM = 128
BLOCK = 512

neg_large = -1e30
route_factor = 2.5
norm_epsilon = 1e-06
f32 = jnp.float32
bf16 = jnp.bfloat16


def attention_kernel(
    order_ref, q_nope_ref, q_rope_ref, own_latent_ref, other_latent_ref, own_rope_ref, other_rope_ref, w_uk_ref, w_uv_ref, out_ref
):
    core = lax.axis_index("ctx")
    rank_of = lambda block: order_ref[block]
    scale = (NOPE + ROPE) ** (-0.5) * math.log2(math.e)
    rows = q_nope_ref.shape[0]
    blocks = rows // BLOCK
    step = 256
    keys_t, values = [], []
    for latent_ref in (own_latent_ref, other_latent_ref):
        latent = latent_ref[...]
        keys_t.append(
            lax.dot_general(w_uk_ref[...], latent, (((0,), (1,)), ((), ())), preferred_element_type=f32).astype(bf16)
        )
        values.append(jnp.dot(latent, w_uv_ref[...], preferred_element_type=f32).astype(bf16))
    ropes = (own_rope_ref[...], other_rope_ref[...])
    blank = jnp.zeros_like(ropes[0])
    diagonal = lax.broadcasted_iota(jnp.int32, (step, step), 1) <= lax.broadcasted_iota(jnp.int32, (step, step), 0)
    key_cat, value_cat = [], []
    for head in range(2):
        cols = slice(head * NOPE, (head + 1) * NOPE)
        key_cat.append([
            jnp.concatenate([keys[cols, :]] + ([rope, blank] if head == 0 else [blank, rope]), axis=0)
            for keys, rope in zip(keys_t, ropes)
        ])
        value_cat.append([jnp.concatenate([held[:, cols], jnp.ones_like(held[:, cols])], axis=1) for held in values])

    def score(head, first):
        cols, part = slice(head * NOPE, (head + 1) * NOPE), slice(first, first + step)
        query = jnp.concatenate([q_nope_ref[part, cols], q_rope_ref[part, :]], axis=1)
        query_block, inside = first // BLOCK, first % BLOCK
        scores = []
        for side in (0, 1):
            owner = core if side == 0 else 1 - core
            for block in range(blocks):
                start = block * BLOCK
                if side == 0 and block == query_block:
                    seen = slice(start, start + inside + step)
                    piece = jnp.dot(query, key_cat[head][side][:, seen], preferred_element_type=f32)
                    last = jnp.where(diagonal, piece[:, inside:], neg_large)
                    piece = jnp.concatenate([piece[:, :inside], last], axis=1) if inside else last
                else:
                    seen = slice(start, start + BLOCK)
                    piece = jnp.dot(query, key_cat[head][side][:, seen], preferred_element_type=f32)
                    earlier = rank_of(owner * blocks + block) < rank_of(core * blocks + query_block)
                    piece = piece + jnp.where(earlier, 0.0, neg_large)
                scores.append((side, seen, piece))
        return scores

    units = [(head, first) for first in range(0, rows, step) for head in range(2)]
    ready = score(*units[0])
    for number, (head, first) in enumerate(units):
        scores = ready
        if number + 1 < len(units):
            ready = score(*units[number + 1])
        best = functools.reduce(jnp.maximum, [jnp.max(piece, axis=1, keepdims=True) for _, _, piece in scores])
        summed = 0.0
        for side, seen, piece in scores:
            probs = jnp.exp2((piece - best) * scale).astype(bf16)
            summed = summed + jnp.dot(probs, value_cat[head][side][seen, :], preferred_element_type=f32)
        out_ref[first : first + step, head * VDIM : (head + 1) * VDIM] = (summed[:, :VDIM] / summed[:, VDIM:]).astype(bf16)


def attend(block_order, q_nope, q_rope, latents, ropes, w_uk, w_uv):
    rows, keys = q_nope.shape[0], 2 * latents[0].shape[0]
    pairs = q_nope.shape[1] // (2 * NOPE)
    held = lambda array: pltpu.with_memory_space_constraint(array, pltpu.HBM)
    whole = lambda array: pl.BlockSpec(array.shape, lambda h, s: (0, 0))
    column = lambda array, width: pl.BlockSpec((array.shape[0], width), lambda h, s: (0, h))
    return pl.pallas_call(
        attention_kernel,
        grid_spec=pltpu.PrefetchScalarGridSpec(
            num_scalar_prefetch=1,
            grid=(pairs,),
            in_specs=[column(q_nope, 2 * NOPE), column(q_rope, 2 * ROPE)]
            + [whole(array) for array in (*latents, *ropes)]
            + [column(w_uk, 2 * NOPE), column(w_uv, 2 * VDIM)],
            out_specs=column(q_nope, 2 * VDIM),
        ),
        out_shape=jax.ShapeDtypeStruct((rows, q_nope.shape[1]), bf16),
        compiler_params=pltpu.CompilerParams(vmem_limit_bytes=12 * 1024 * 1024),
        cost_estimate=pl.CostEstimate(
            flops=7 * rows * keys * pairs * 2 * 384, bytes_accessed=8 * 1024 * 1024, transcendentals=rows * keys * pairs * 2
        ),
    )(held(block_order), held(q_nope), held(q_rope), held(latents[0]), latents[1], held(ropes[0]), ropes[1], held(w_uk), held(w_uv))


def product_kernel(rows_ref, *refs):
    *weight_refs, out_ref = refs
    depth = weight_refs[0].shape[1]
    terms = [
        jnp.dot(rows_ref[e, :, q * depth : (q + 1) * depth], ref[e], preferred_element_type=f32)
        for q, ref in enumerate(weight_refs)
        for e in range(rows_ref.shape[0])
    ]
    out_ref[...] = functools.reduce(jnp.add, terms).astype(bf16)


def product(rows, weights):
    terms, count, depth = rows.shape
    width = weights.shape[2]
    tile, pieces = width // 2, 4
    weights = pltpu.with_memory_space_constraint(weights, pltpu.HBM)
    piece = lambda q: pl.BlockSpec((terms, depth // pieces, tile), lambda n: (0, q, n))
    return pl.pallas_call(
        product_kernel,
        grid=(width // tile,),
        in_specs=[pl.BlockSpec((terms, count, depth), lambda n: (0, 0, 0))] + [piece(q) for q in range(pieces)],
        out_specs=pl.BlockSpec((count, tile), lambda n: (0, n)),
        out_shape=jax.ShapeDtypeStruct((count, width), bf16),
        compiler_params=pltpu.CompilerParams(vmem_limit_bytes=16 * 1024 * 1024),
        cost_estimate=pl.CostEstimate(flops=count * depth * width // 4, bytes_accessed=count * width, transcendentals=0),
    )(rows, *[weights] * pieces)


class Ring:
    def __init__(self, count):
        self.count, self.half = count, count // 2
        self.grid = count == 8
        order = [(2 * p if p < count // 2 else 2 * count - 1 - 2 * p) if self.grid else p for p in range(count)]
        self.up = [(order[p], order[(p + 1) % count]) for p in range(count)]
        self.down = [(t, s) for s, t in self.up]
        index = lax.axis_index("exp")
        self.place = jnp.where(index % 2 == 0, index // 2, count - 1 - index // 2) if self.grid else index

    def index_at(self, place):
        return jnp.where(place < self.half, 2 * place, 2 * self.count - 1 - 2 * place) if self.grid else place

    def at(self, offset):
        return self.index_at(lax.rem(self.place + offset, self.count))

    def send(self, block, way):
        return lax.ppermute(block, "exp", self.up if way > 0 else self.down)


def after(blocks, work):
    if not work:
        return blocks
    held = lax.optimization_barrier((tuple(blocks), tuple(work)))
    return list(held[0])


def scatter_rows(ring, part):
    add = lambda *terms: functools.reduce(jnp.add, [t.astype(f32) for t in terms])
    far = part(ring.half, [])
    sent = [far]
    cut = far.shape[0] // 2
    going = {1: ring.send(far[:cut], 1), -1: ring.send(far[cut:], -1)}
    for offset in range(ring.half - 1, 0, -1):
        behind, sent = sent, []
        for way in (1, -1):
            own, come = part(way * offset, behind), going[way]
            if offset == ring.half - 1:
                come = jnp.pad(come, ((0, cut) if way > 0 else (cut, 0), (0, 0)))
            block = add(own, come).astype(bf16)
            sent.append(block)
            going[way] = ring.send(block, way)
    return add(part(0, sent), going[1], going[-1])


def per_device(
    count,
    resid,
    q_nope,
    q_rope,
    latent,
    k_rope,
    w_uk,
    w_uv,
    w_out,
    norm_gain,
    w_gate,
    w_up,
    w_down,
    routes,
    codes,
    block_order,
):
    token_rows, owned = resid.shape[0], w_gate.shape[0]
    cut = token_rows // 2
    ring = Ring(count)
    core, index = lax.axis_index("ctx"), lax.axis_index("exp")
    swap = lambda block: lax.ppermute(block, "ctx", [(0, 1), (1, 0)])

    ropes = k_rope.T
    heads = attend(
        block_order, q_nope, q_rope, (latent, swap(latent)), (ropes, swap(ropes)), w_uk, w_uv
    )

    other_heads = swap(heads)
    project = lambda rows: jnp.dot(rows, w_out, preferred_element_type=f32).astype(bf16)

    def block_of(offset):
        return jnp.bitwise_and(ring.at(offset % count) - core * ring.half, count - 1)

    def pick(own, other, block):
        first = jnp.minimum(block, ring.half - 1) * token_rows
        second = jnp.maximum(block - ring.half, 0) * token_rows
        part = lambda rows, at: lax.dynamic_slice_in_dim(rows, at, token_rows, 0, allow_negative_indices=False)
        return jnp.where(block < ring.half, part(own, first), part(other, second))

    nearby = {}

    def attention_term(offset, behind):
        if offset == ring.half:
            return product(pick(heads, other_heads, block_of(offset))[None], w_out[None])
        if abs(offset) == ring.half - 1:
            if "first" not in nearby:
                rows = [pick(heads, other_heads, block_of(way * abs(offset))) for way in (1, -1)]
                rows = after([jnp.concatenate(rows, axis=0)], behind)[0]
                nearby["first"] = product(rows[None], w_out[None])
            return nearby["first"][:token_rows] if offset > 0 else nearby["first"][token_rows:]
        if "terms" not in nearby:
            later = after([heads, other_heads], behind)
            nearby["terms"] = [project(rows) for rows in later]
        return lax.optimization_barrier(pick(*nearby["terms"], block_of(offset)))

    residual_state = resid.astype(f32) + scatter_rows(ring, attention_term)

    code_values = codes.astype(f32)
    route_weight = route_factor * code_values / jnp.sum(code_values, axis=1, keepdims=True)
    named = routes[None] == jnp.arange(count * owned, dtype=jnp.int32)[:, None, None]
    routing = jnp.sum(jnp.where(named, route_weight[None], 0.0), axis=2)[None]
    scaled = (residual_state * norm_gain).astype(bf16)
    squares = jnp.sum(residual_state * residual_state, axis=1)
    squares = squares + swap(squares)
    inverse_rms = lax.rsqrt(squares / D + norm_epsilon)
    routing = jnp.concatenate([routing, inverse_rms[None, None]], axis=1)

    def before_hidden(rows):
        product = lambda weight: jnp.einsum("td,ldf->ltf", rows, weight, preferred_element_type=f32).astype(bf16)
        own = [product(w_gate), product(w_up)]
        return own

    def summed(own):
        return own, [swap(pre) for pre in own]

    def hidden_of(own, other, weight, scale):
        gate_pre, up_pre = [mine.astype(f32) + theirs.astype(f32) for mine, theirs in zip(own, other)]
        gate_pre = gate_pre * scale[:, None]
        return (jax.nn.silu(gate_pre) * up_pre * (weight * scale)[:, :, None]).astype(bf16)

    def down(hidden):
        return functools.reduce(
            jnp.add, [jnp.dot(hidden[e], w_down[e], preferred_element_type=f32) for e in range(owned)]
        ).astype(bf16)

    pre = [(before_hidden(scaled), None)]
    below = above = scaled
    hops = count.bit_length() - 1
    far_first = [count >> (1 + number) for number in range(hops)]

    def hop(routing, number):
        other = lax.ppermute(routing, "exp", [(i, i ^ far_first[number]) for i in range(count)])
        return jnp.concatenate([routing, other], axis=0)

    for step in range(1, ring.half + 1):
        if step > 1:
            work = list(pre[step - 2][0])
            if step <= hops:
                (routing,) = after([hop(routing, step - 2)], [below])
                work = work + [routing]
            below, above = after([below, above], work)
        if step == ring.half:
            below, above = below[:cut], above[cut:]
        below, above = ring.send(below, 1), ring.send(above, -1)
        rows = jnp.concatenate([below, above], axis=0)
        if step == ring.half:
            for number in range(min(step - 1, hops - 1), hops):
                routing = hop(routing, number)
            (rows,) = after([rows], pre[step - 1][0] + (pre[step - 3][1] if step > 3 else []))
        pre.append(summed(before_hidden(rows)))

    mine = lax.dynamic_slice_in_dim(routing, index * owned, owned, 1, allow_negative_indices=False)
    offsets = jnp.arange(count, dtype=jnp.int32)
    held = [sum(bit for number, bit in enumerate(far_first) if p >> number & 1) for p in range(count)]
    entry = jnp.bitwise_xor(ring.at(offsets), index)[:, None] == jnp.array(held, jnp.int32)[None, :]
    weights = jnp.sum(jnp.where(entry[:, :, None, None], mine[None], 0.0), axis=1)
    scales = jnp.sum(jnp.where(entry[:, :, None], routing[None, :, -1], 0.0), axis=1)

    outcomes = {}

    def hidden(step, behind):
        offsets = (-step % count, step) if 0 < step < ring.half else (step,)
        weight = jnp.concatenate([weights[o] for o in offsets], axis=1)
        scale = jnp.concatenate([scales[o] for o in offsets], axis=0)
        return hidden_of(after(pre[step][0], behind), pre[step][1], weight, scale)

    def expert_term(offset, behind):
        step = abs(offset)
        if step == ring.half:
            before = hidden(step - 1, pre[step][0] + pre[step - 2][1])
            outcomes[step] = down(hidden(step, [before]))
            outcomes[step - 1] = product(after([before], [outcomes[step]])[0], w_down)
        if step == 1:
            pre[0] = summed(after(pre[0][0], behind))
        if step not in outcomes:
            outcomes[step] = down(hidden(step, behind))
        if step in (0, ring.half):
            return outcomes[step]
        return outcomes[step][token_rows:] if offset > 0 else outcomes[step][:token_rows]

    return (residual_state + scatter_rows(ring, expert_term)).astype(bf16)


def solution(mesh):
    return jax.shard_map(
        functools.partial(per_device, mesh.shape["exp"]),
        mesh=mesh,
        in_specs=(
            P(("groups", "exp"), "ctx"),
            P(("groups", "ctx"), "exp"),
            P(("groups", "ctx"), "exp"),
            P(("groups", "ctx"), None),
            P(("groups", "ctx"), None),
            P(None, "exp"),
            P(None, "exp"),
            P("exp", "ctx"),
            P("ctx"),
            P("exp", "ctx", None),
            P("exp", "ctx", None),
            P("exp", None, "ctx"),
            P(("groups", "exp"), None),
            P(("groups", "exp"), None),
            P("groups"),
        ),
        out_specs=P(("groups", "exp"), "ctx"),
        check_vma=False,
    )
```

```python
import functools
import math

import jax
import jax.numpy as jnp
from jax import lax
from jax.experimental import pallas as pl
from jax.experimental.pallas import tpu as pltpu
from jax.sharding import PartitionSpec as P

D = 3584
NOPE = 128
ROPE = 64
VDIM = 128
BLOCK = 512

neg_large = -1e30
route_factor = 2.5
norm_epsilon = 1e-06
f32 = jnp.float32
bf16 = jnp.bfloat16


def attention_kernel(
    order_ref, q_nope_ref, q_rope_ref, own_latent_ref, other_latent_ref, own_rope_ref, other_rope_ref, w_uk_ref, w_uv_ref, out_ref
):
    core = lax.axis_index("ctx")
    rank_of = lambda block: order_ref[block]
    scale = (NOPE + ROPE) ** (-0.5) * math.log2(math.e)
    rows = q_nope_ref.shape[0]
    blocks = rows // BLOCK
    step = 256
    keys_t, values = [], []
    for latent_ref in (own_latent_ref, other_latent_ref):
        latent = latent_ref[...]
        keys_t.append(
            lax.dot_general(w_uk_ref[...], latent, (((0,), (1,)), ((), ())), preferred_element_type=f32).astype(bf16)
        )
        values.append(jnp.dot(latent, w_uv_ref[...], preferred_element_type=f32).astype(bf16))
    ropes = (own_rope_ref[...], other_rope_ref[...])
    blank = jnp.zeros_like(ropes[0])
    diagonal = lax.broadcasted_iota(jnp.int32, (step, step), 1) <= lax.broadcasted_iota(jnp.int32, (step, step), 0)
    key_cat, value_cat = [], []
    for head in range(2):
        cols = slice(head * NOPE, (head + 1) * NOPE)
        key_cat.append([
            jnp.concatenate([keys[cols, :]] + ([rope, blank] if head == 0 else [blank, rope]), axis=0)
            for keys, rope in zip(keys_t, ropes)
        ])
        value_cat.append([jnp.concatenate([held[:, cols], jnp.ones_like(held[:, cols])], axis=1) for held in values])

    def score(head, first):
        cols, part = slice(head * NOPE, (head + 1) * NOPE), slice(first, first + step)
        query = jnp.concatenate([q_nope_ref[part, cols], q_rope_ref[part, :]], axis=1)
        query_block, inside = first // BLOCK, first % BLOCK
        scores = []
        for side in (0, 1):
            owner = core if side == 0 else 1 - core
            for block in range(blocks):
                start = block * BLOCK
                if side == 0 and block == query_block:
                    seen = slice(start, start + inside + step)
                    piece = jnp.dot(query, key_cat[head][side][:, seen], preferred_element_type=f32)
                    last = jnp.where(diagonal, piece[:, inside:], neg_large)
                    piece = jnp.concatenate([piece[:, :inside], last], axis=1) if inside else last
                else:
                    seen = slice(start, start + BLOCK)
                    piece = jnp.dot(query, key_cat[head][side][:, seen], preferred_element_type=f32)
                    earlier = rank_of(owner * blocks + block) < rank_of(core * blocks + query_block)
                    piece = piece + jnp.where(earlier, 0.0, neg_large)
                scores.append((side, seen, piece))
        return scores

    units = [(head, first) for first in range(0, rows, step) for head in range(2)]
    ready = score(*units[0])
    for number, (head, first) in enumerate(units):
        scores = ready
        if number + 1 < len(units):
            ready = score(*units[number + 1])
        best = functools.reduce(jnp.maximum, [jnp.max(piece, axis=1, keepdims=True) for _, _, piece in scores])
        summed = 0.0
        for side, seen, piece in scores:
            probs = jnp.exp2((piece - best) * scale).astype(bf16)
            summed = summed + jnp.dot(probs, value_cat[head][side][seen, :], preferred_element_type=f32)
        out_ref[first : first + step, head * VDIM : (head + 1) * VDIM] = (summed[:, :VDIM] / summed[:, VDIM:]).astype(bf16)


def attend(block_order, q_nope, q_rope, latents, ropes, w_uk, w_uv):
    rows, keys = q_nope.shape[0], 2 * latents[0].shape[0]
    pairs = q_nope.shape[1] // (2 * NOPE)
    held = lambda array: pltpu.with_memory_space_constraint(array, pltpu.HBM)
    whole = lambda array: pl.BlockSpec(array.shape, lambda h, s: (0, 0))
    column = lambda array, width: pl.BlockSpec((array.shape[0], width), lambda h, s: (0, h))
    return pl.pallas_call(
        attention_kernel,
        grid_spec=pltpu.PrefetchScalarGridSpec(
            num_scalar_prefetch=1,
            grid=(pairs,),
            in_specs=[column(q_nope, 2 * NOPE), column(q_rope, 2 * ROPE)]
            + [whole(array) for array in (*latents, *ropes)]
            + [column(w_uk, 2 * NOPE), column(w_uv, 2 * VDIM)],
            out_specs=column(q_nope, 2 * VDIM),
        ),
        out_shape=jax.ShapeDtypeStruct((rows, q_nope.shape[1]), bf16),
        compiler_params=pltpu.CompilerParams(vmem_limit_bytes=12 * 1024 * 1024),
        cost_estimate=pl.CostEstimate(
            flops=7 * rows * keys * pairs * 2 * 384, bytes_accessed=8 * 1024 * 1024, transcendentals=rows * keys * pairs * 2
        ),
    )(held(block_order), held(q_nope), held(q_rope), held(latents[0]), latents[1], held(ropes[0]), ropes[1], held(w_uk), held(w_uv))


def product_kernel(rows_ref, *refs):
    *weight_refs, out_ref = refs
    depth = weight_refs[0].shape[1]
    terms = [
        jnp.dot(rows_ref[e, :, q * depth : (q + 1) * depth], ref[e], preferred_element_type=f32)
        for q, ref in enumerate(weight_refs)
        for e in range(rows_ref.shape[0])
    ]
    out_ref[...] = functools.reduce(jnp.add, terms).astype(bf16)


def product(rows, weights):
    terms, count, depth = rows.shape
    width = weights.shape[2]
    tile, pieces = width // 2, 4
    weights = pltpu.with_memory_space_constraint(weights, pltpu.HBM)
    piece = lambda q: pl.BlockSpec((terms, depth // pieces, tile), lambda n: (0, q, n))
    return pl.pallas_call(
        product_kernel,
        grid=(width // tile,),
        in_specs=[pl.BlockSpec((terms, count, depth), lambda n: (0, 0, 0))] + [piece(q) for q in range(pieces)],
        out_specs=pl.BlockSpec((count, tile), lambda n: (0, n)),
        out_shape=jax.ShapeDtypeStruct((count, width), bf16),
        compiler_params=pltpu.CompilerParams(vmem_limit_bytes=16 * 1024 * 1024),
        cost_estimate=pl.CostEstimate(flops=count * depth * width // 4, bytes_accessed=count * width, transcendentals=0),
    )(rows, *[weights] * pieces)


class Ring:
    def __init__(self, count):
        self.count, self.half = count, count // 2
        self.grid = count == 8
        order = [(2 * p if p < count // 2 else 2 * count - 1 - 2 * p) if self.grid else p for p in range(count)]
        self.up = [(order[p], order[(p + 1) % count]) for p in range(count)]
        self.down = [(t, s) for s, t in self.up]
        index = lax.axis_index("exp")
        self.place = jnp.where(index % 2 == 0, index // 2, count - 1 - index // 2) if self.grid else index

    def index_at(self, place):
        return jnp.where(place < self.half, 2 * place, 2 * self.count - 1 - 2 * place) if self.grid else place

    def at(self, offset):
        return self.index_at(lax.rem(self.place + offset, self.count))

    def send(self, block, way):
        return lax.ppermute(block, "exp", self.up if way > 0 else self.down)


def after(blocks, work):
    if not work:
        return blocks
    held = lax.optimization_barrier((tuple(blocks), tuple(work)))
    return list(held[0])


def scatter_rows(ring, part):
    add = lambda *terms: functools.reduce(jnp.add, [t.astype(f32) for t in terms])
    far = part(ring.half, [])
    sent = [far]
    cut = far.shape[0] // 2
    going = {1: ring.send(far[:cut], 1), -1: ring.send(far[cut:], -1)}
    for offset in range(ring.half - 1, 0, -1):
        behind, sent = sent, []
        for way in (1, -1):
            own, come = part(way * offset, behind), going[way]
            if offset == ring.half - 1:
                come = jnp.pad(come, ((0, cut) if way > 0 else (cut, 0), (0, 0)))
            block = add(own, come).astype(bf16)
            sent.append(block)
            going[way] = ring.send(block, way)
    return add(part(0, sent), going[1], going[-1])


def per_device(
    count,
    resid,
    q_nope,
    q_rope,
    latent,
    k_rope,
    w_uk,
    w_uv,
    w_out,
    norm_gain,
    w_gate,
    w_up,
    w_down,
    routes,
    codes,
    block_order,
):
    token_rows, owned = resid.shape[0], w_gate.shape[0]
    cut = token_rows // 2
    ring = Ring(count)
    core, index = lax.axis_index("ctx"), lax.axis_index("exp")
    swap = lambda block: lax.ppermute(block, "ctx", [(0, 1), (1, 0)])

    ropes = k_rope.T
    heads = attend(
        block_order, q_nope, q_rope, (latent, swap(latent)), (ropes, swap(ropes)), w_uk, w_uv
    )

    other_heads = swap(heads)
    project = lambda rows: jnp.dot(rows, w_out, preferred_element_type=f32).astype(bf16)

    def block_of(offset):
        return jnp.bitwise_and(ring.at(offset % count) - core * ring.half, count - 1)

    def pick(own, other, block):
        first = jnp.minimum(block, ring.half - 1) * token_rows
        second = jnp.maximum(block - ring.half, 0) * token_rows
        part = lambda rows, at: lax.dynamic_slice_in_dim(rows, at, token_rows, 0, allow_negative_indices=False)
        return jnp.where(block < ring.half, part(own, first), part(other, second))

    nearby = {}

    def attention_term(offset, behind):
        if offset == ring.half:
            return product(pick(heads, other_heads, block_of(offset))[None], w_out[None])
        if abs(offset) == ring.half - 1:
            if "first" not in nearby:
                rows = [pick(heads, other_heads, block_of(way * abs(offset))) for way in (1, -1)]
                rows = after([jnp.concatenate(rows, axis=0)], behind)[0]
                nearby["first"] = product(rows[None], w_out[None])
            return nearby["first"][:token_rows] if offset > 0 else nearby["first"][token_rows:]
        if "terms" not in nearby:
            later = after([heads, other_heads], behind)
            nearby["terms"] = [project(rows) for rows in later]
        return lax.optimization_barrier(pick(*nearby["terms"], block_of(offset)))

    residual_state = resid.astype(f32) + scatter_rows(ring, attention_term)

    code_values = codes.astype(f32)
    route_weight = route_factor * code_values / jnp.sum(code_values, axis=1, keepdims=True)
    named = routes[None] == jnp.arange(count * owned, dtype=jnp.int32)[:, None, None]
    routing = jnp.sum(jnp.where(named, route_weight[None], 0.0), axis=2)[None]
    scaled = (residual_state * norm_gain).astype(bf16)
    squares = jnp.sum(residual_state * residual_state, axis=1)
    squares = squares + swap(squares)
    inverse_rms = lax.rsqrt(squares / D + norm_epsilon)
    routing = jnp.concatenate([routing, inverse_rms[None, None]], axis=1)

    def before_hidden(rows):
        product = lambda weight: jnp.einsum("td,ldf->ltf", rows, weight, preferred_element_type=f32).astype(bf16)
        own = [product(w_gate), product(w_up)]
        return own

    def summed(own):
        return own, [swap(pre) for pre in own]

    def hidden_of(own, other, weight, scale):
        gate_pre, up_pre = [mine.astype(f32) + theirs.astype(f32) for mine, theirs in zip(own, other)]
        gate_pre = gate_pre * scale[:, None]
        return (jax.nn.silu(gate_pre) * up_pre * (weight * scale)[:, :, None]).astype(bf16)

    def down(hidden):
        return functools.reduce(
            jnp.add, [jnp.dot(hidden[e], w_down[e], preferred_element_type=f32) for e in range(owned)]
        ).astype(bf16)

    pre = [(before_hidden(scaled), None)]
    below = above = scaled
    hops = count.bit_length() - 1
    far_first = [count >> (1 + number) for number in range(hops)]

    def hop(routing, number):
        other = lax.ppermute(routing, "exp", [(i, i ^ far_first[number]) for i in range(count)])
        return jnp.concatenate([routing, other], axis=0)

    for step in range(1, ring.half + 1):
        if step > 1:
            work = list(pre[step - 2][0])
            if step <= hops:
                (routing,) = after([hop(routing, step - 2)], [below])
                work = work + [routing]
            below, above = after([below, above], work)
        if step == ring.half:
            below, above = below[:cut], above[cut:]
        below, above = ring.send(below, 1), ring.send(above, -1)
        rows = jnp.concatenate([below, above], axis=0)
        if step == ring.half:
            for number in range(min(step - 1, hops - 1), hops):
                routing = hop(routing, number)
            (rows,) = after([rows], pre[step - 1][0])
        if step == ring.half - 1 and step > 2:
            (rows,) = after([rows], pre[step - 2][1])
        pre.append(summed(before_hidden(rows)))

    mine = lax.dynamic_slice_in_dim(routing, index * owned, owned, 1, allow_negative_indices=False)
    offsets = jnp.arange(count, dtype=jnp.int32)
    held = [sum(bit for number, bit in enumerate(far_first) if p >> number & 1) for p in range(count)]
    entry = jnp.bitwise_xor(ring.at(offsets), index)[:, None] == jnp.array(held, jnp.int32)[None, :]
    weights = jnp.sum(jnp.where(entry[:, :, None, None], mine[None], 0.0), axis=1)
    scales = jnp.sum(jnp.where(entry[:, :, None], routing[None, :, -1], 0.0), axis=1)

    outcomes = {}

    def hidden(step, behind):
        offsets = (-step % count, step) if 0 < step < ring.half else (step,)
        weight = jnp.concatenate([weights[o] for o in offsets], axis=1)
        scale = jnp.concatenate([scales[o] for o in offsets], axis=0)
        return hidden_of(after(pre[step][0], behind), pre[step][1], weight, scale)

    def expert_term(offset, behind):
        step = abs(offset)
        if step == ring.half:
            before = hidden(step - 1, pre[step][0] + pre[step - 2][1])
            outcomes[step] = down(hidden(step, [before]))
            outcomes[step - 1] = product(after([before], [outcomes[step]])[0], w_down)
        if step == 1:
            pre[0] = summed(after(pre[0][0], behind))
        if step not in outcomes:
            outcomes[step] = down(hidden(step, behind))
        if step in (0, ring.half):
            return outcomes[step]
        return outcomes[step][token_rows:] if offset > 0 else outcomes[step][:token_rows]

    return (residual_state + scatter_rows(ring, expert_term)).astype(bf16)


def solution(mesh):
    return jax.shard_map(
        functools.partial(per_device, mesh.shape["exp"]),
        mesh=mesh,
        in_specs=(
            P(("groups", "exp"), "ctx"),
            P(("groups", "ctx"), "exp"),
            P(("groups", "ctx"), "exp"),
            P(("groups", "ctx"), None),
            P(("groups", "ctx"), None),
            P(None, "exp"),
            P(None, "exp"),
            P("exp", "ctx"),
            P("ctx"),
            P("exp", "ctx", None),
            P("exp", "ctx", None),
            P("exp", None, "ctx"),
            P(("groups", "exp"), None),
            P(("groups", "exp"), None),
            P("groups"),
        ),
        out_specs=P(("groups", "exp"), "ctx"),
        check_vma=False,
    )
```

```python
import functools
import math

import jax
import jax.numpy as jnp
from jax import lax
from jax.experimental import pallas as pl
from jax.experimental.pallas import tpu as pltpu
from jax.sharding import PartitionSpec as P

D = 3584
NOPE = 128
ROPE = 64
VDIM = 128
BLOCK = 512

neg_large = -1e30
route_factor = 2.5
norm_epsilon = 1e-06
f32 = jnp.float32
bf16 = jnp.bfloat16


def attention_kernel(
    order_ref, q_nope_ref, q_rope_ref, own_latent_ref, other_latent_ref, own_rope_ref, other_rope_ref, w_uk_ref, w_uv_ref, out_ref
):
    core = lax.axis_index("ctx")
    rank_of = lambda block: order_ref[block]
    scale = (NOPE + ROPE) ** (-0.5) * math.log2(math.e)
    rows = q_nope_ref.shape[0]
    blocks = rows // BLOCK
    step = 256
    keys_t, values = [], []
    for latent_ref in (own_latent_ref, other_latent_ref):
        latent = latent_ref[...]
        keys_t.append(
            lax.dot_general(w_uk_ref[...], latent, (((0,), (1,)), ((), ())), preferred_element_type=f32).astype(bf16)
        )
        values.append(jnp.dot(latent, w_uv_ref[...], preferred_element_type=f32).astype(bf16))
    ropes = (own_rope_ref[...], other_rope_ref[...])
    blank = jnp.zeros_like(ropes[0])
    diagonal = lax.broadcasted_iota(jnp.int32, (step, step), 1) <= lax.broadcasted_iota(jnp.int32, (step, step), 0)
    key_cat, value_cat = [], []
    for head in range(2):
        cols = slice(head * NOPE, (head + 1) * NOPE)
        key_cat.append([
            jnp.concatenate([keys[cols, :]] + ([rope, blank] if head == 0 else [blank, rope]), axis=0)
            for keys, rope in zip(keys_t, ropes)
        ])
        value_cat.append([jnp.concatenate([held[:, cols], jnp.ones_like(held[:, cols])], axis=1) for held in values])

    def score(head, first):
        cols, part = slice(head * NOPE, (head + 1) * NOPE), slice(first, first + step)
        query = jnp.concatenate([q_nope_ref[part, cols], q_rope_ref[part, :]], axis=1)
        query_block, inside = first // BLOCK, first % BLOCK
        scores = []
        for side in (0, 1):
            owner = core if side == 0 else 1 - core
            for block in range(blocks):
                start = block * BLOCK
                if side == 0 and block == query_block:
                    seen, lift = slice(start, start + inside + step), 0.0
                    piece = jnp.dot(query, key_cat[head][side][:, seen], preferred_element_type=f32)
                    last = jnp.where(diagonal, piece[:, inside:], neg_large)
                    piece = jnp.concatenate([piece[:, :inside], last], axis=1) if inside else last
                else:
                    seen = slice(start, start + BLOCK)
                    piece = jnp.dot(query, key_cat[head][side][:, seen], preferred_element_type=f32)
                    earlier = rank_of(owner * blocks + block) < rank_of(core * blocks + query_block)
                    lift = jnp.where(earlier, 0.0, neg_large)
                scores.append((side, seen, piece, lift))
        return scores

    units = [(head, first) for first in range(0, rows, step) for head in range(2)]
    ready = score(*units[0])
    for number, (head, first) in enumerate(units):
        scores = ready
        if number + 1 < len(units):
            ready = score(*units[number + 1])
        best = functools.reduce(jnp.maximum, [jnp.max(piece, axis=1, keepdims=True) + lift for _, _, piece, lift in scores])
        summed = 0.0
        for side, seen, piece, lift in scores:
            probs = jnp.exp2((piece - (best - lift)) * scale).astype(bf16)
            summed = summed + jnp.dot(probs, value_cat[head][side][seen, :], preferred_element_type=f32)
        out_ref[first : first + step, head * VDIM : (head + 1) * VDIM] = (summed[:, :VDIM] / summed[:, VDIM:]).astype(bf16)


def attend(block_order, q_nope, q_rope, latents, ropes, w_uk, w_uv):
    rows, keys = q_nope.shape[0], 2 * latents[0].shape[0]
    pairs = q_nope.shape[1] // (2 * NOPE)
    held = lambda array: pltpu.with_memory_space_constraint(array, pltpu.HBM)
    whole = lambda array: pl.BlockSpec(array.shape, lambda h, s: (0, 0))
    column = lambda array, width: pl.BlockSpec((array.shape[0], width), lambda h, s: (0, h))
    return pl.pallas_call(
        attention_kernel,
        grid_spec=pltpu.PrefetchScalarGridSpec(
            num_scalar_prefetch=1,
            grid=(pairs,),
            in_specs=[column(q_nope, 2 * NOPE), column(q_rope, 2 * ROPE)]
            + [whole(array) for array in (*latents, *ropes)]
            + [column(w_uk, 2 * NOPE), column(w_uv, 2 * VDIM)],
            out_specs=column(q_nope, 2 * VDIM),
        ),
        out_shape=jax.ShapeDtypeStruct((rows, q_nope.shape[1]), bf16),
        compiler_params=pltpu.CompilerParams(vmem_limit_bytes=12 * 1024 * 1024),
        cost_estimate=pl.CostEstimate(
            flops=7 * rows * keys * pairs * 2 * 384, bytes_accessed=8 * 1024 * 1024, transcendentals=rows * keys * pairs * 2
        ),
    )(held(block_order), held(q_nope), held(q_rope), held(latents[0]), latents[1], held(ropes[0]), ropes[1], held(w_uk), held(w_uv))


def product_kernel(rows_ref, *refs):
    *weight_refs, out_ref = refs
    depth = weight_refs[0].shape[1]
    terms = [
        jnp.dot(rows_ref[e, :, q * depth : (q + 1) * depth], ref[e], preferred_element_type=f32)
        for q, ref in enumerate(weight_refs)
        for e in range(rows_ref.shape[0])
    ]
    out_ref[...] = functools.reduce(jnp.add, terms).astype(bf16)


def product(rows, weights):
    terms, count, depth = rows.shape
    width = weights.shape[2]
    tile, pieces = width // 2, 4
    weights = pltpu.with_memory_space_constraint(weights, pltpu.HBM)
    piece = lambda q: pl.BlockSpec((terms, depth // pieces, tile), lambda n: (0, q, n))
    return pl.pallas_call(
        product_kernel,
        grid=(width // tile,),
        in_specs=[pl.BlockSpec((terms, count, depth), lambda n: (0, 0, 0))] + [piece(q) for q in range(pieces)],
        out_specs=pl.BlockSpec((count, tile), lambda n: (0, n)),
        out_shape=jax.ShapeDtypeStruct((count, width), bf16),
        compiler_params=pltpu.CompilerParams(vmem_limit_bytes=16 * 1024 * 1024),
        cost_estimate=pl.CostEstimate(flops=count * depth * width // 4, bytes_accessed=count * width, transcendentals=0),
    )(rows, *[weights] * pieces)


class Ring:
    def __init__(self, count):
        self.count, self.half = count, count // 2
        self.grid = count == 8
        order = [(2 * p if p < count // 2 else 2 * count - 1 - 2 * p) if self.grid else p for p in range(count)]
        self.up = [(order[p], order[(p + 1) % count]) for p in range(count)]
        self.down = [(t, s) for s, t in self.up]
        index = lax.axis_index("exp")
        self.place = jnp.where(index % 2 == 0, index // 2, count - 1 - index // 2) if self.grid else index

    def index_at(self, place):
        return jnp.where(place < self.half, 2 * place, 2 * self.count - 1 - 2 * place) if self.grid else place

    def at(self, offset):
        return self.index_at(lax.rem(self.place + offset, self.count))

    def send(self, block, way):
        return lax.ppermute(block, "exp", self.up if way > 0 else self.down)


def after(blocks, work):
    if not work:
        return blocks
    held = lax.optimization_barrier((tuple(blocks), tuple(work)))
    return list(held[0])


def scatter_rows(ring, part):
    add = lambda *terms: functools.reduce(jnp.add, [t.astype(f32) for t in terms])
    far = part(ring.half, [])
    sent = [far]
    cut = far.shape[0] // 2
    going = {1: ring.send(far[:cut], 1), -1: ring.send(far[cut:], -1)}
    for offset in range(ring.half - 1, 0, -1):
        behind, sent = sent, []
        for way in (1, -1):
            own, come = part(way * offset, behind), going[way]
            if offset == ring.half - 1:
                come = jnp.pad(come, ((0, cut) if way > 0 else (cut, 0), (0, 0)))
            block = add(own, come).astype(bf16)
            sent.append(block)
            going[way] = ring.send(block, way)
    return add(part(0, sent), going[1], going[-1])


def per_device(
    count,
    resid,
    q_nope,
    q_rope,
    latent,
    k_rope,
    w_uk,
    w_uv,
    w_out,
    norm_gain,
    w_gate,
    w_up,
    w_down,
    routes,
    codes,
    block_order,
):
    token_rows, owned = resid.shape[0], w_gate.shape[0]
    cut = token_rows // 2
    ring = Ring(count)
    core, index = lax.axis_index("ctx"), lax.axis_index("exp")
    swap = lambda block: lax.ppermute(block, "ctx", [(0, 1), (1, 0)])

    ropes = k_rope.T
    heads = attend(
        block_order, q_nope, q_rope, (latent, swap(latent)), (ropes, swap(ropes)), w_uk, w_uv
    )

    other_heads = swap(heads)
    project = lambda rows: jnp.dot(rows, w_out, preferred_element_type=f32).astype(bf16)

    def block_of(offset):
        return jnp.bitwise_and(ring.at(offset % count) - core * ring.half, count - 1)

    def pick(own, other, block):
        first = jnp.minimum(block, ring.half - 1) * token_rows
        second = jnp.maximum(block - ring.half, 0) * token_rows
        part = lambda rows, at: lax.dynamic_slice_in_dim(rows, at, token_rows, 0, allow_negative_indices=False)
        return jnp.where(block < ring.half, part(own, first), part(other, second))

    nearby = {}

    def attention_term(offset, behind):
        if offset == ring.half:
            return product(pick(heads, other_heads, block_of(offset))[None], w_out[None])
        if abs(offset) == ring.half - 1:
            if "first" not in nearby:
                rows = [pick(heads, other_heads, block_of(way * abs(offset))) for way in (1, -1)]
                rows = after([jnp.concatenate(rows, axis=0)], behind)[0]
                nearby["first"] = product(rows[None], w_out[None])
            return nearby["first"][:token_rows] if offset > 0 else nearby["first"][token_rows:]
        if "terms" not in nearby:
            later = after([heads, other_heads], behind)
            nearby["terms"] = [project(rows) for rows in later]
        return lax.optimization_barrier(pick(*nearby["terms"], block_of(offset)))

    residual_state = resid.astype(f32) + scatter_rows(ring, attention_term)

    code_values = codes.astype(f32)
    route_weight = route_factor * code_values / jnp.sum(code_values, axis=1, keepdims=True)
    named = routes[None] == jnp.arange(count * owned, dtype=jnp.int32)[:, None, None]
    routing = jnp.sum(jnp.where(named, route_weight[None], 0.0), axis=2)[None]
    scaled = (residual_state * norm_gain).astype(bf16)
    squares = jnp.sum(residual_state * residual_state, axis=1)
    squares = squares + swap(squares)
    inverse_rms = lax.rsqrt(squares / D + norm_epsilon)
    routing = jnp.concatenate([routing, inverse_rms[None, None]], axis=1)

    def times(rows, weight):
        return jnp.einsum("td,ldf->ltf", rows, weight, preferred_element_type=f32).astype(bf16)

    def before_hidden(rows):
        return [times(rows, w_gate), times(rows, w_up)]

    def summed(own):
        return own, [swap(pre) for pre in own]

    def hidden_of(own, other, weight, scale):
        gate_pre, up_pre = [mine.astype(f32) + theirs.astype(f32) for mine, theirs in zip(own, other)]
        gate_pre = gate_pre * scale[:, None]
        return (jax.nn.silu(gate_pre) * up_pre * (weight * scale)[:, :, None]).astype(bf16)

    def down(hidden):
        return functools.reduce(
            jnp.add, [jnp.dot(hidden[e], w_down[e], preferred_element_type=f32) for e in range(owned)]
        ).astype(bf16)

    pre = [([times(scaled, w_up)], None)]
    below = above = scaled
    hops = count.bit_length() - 1
    far_first = [count >> (1 + number) for number in range(hops)]

    def hop(routing, number):
        other = lax.ppermute(routing, "exp", [(i, i ^ far_first[number]) for i in range(count)])
        return jnp.concatenate([routing, other], axis=0)

    for step in range(1, ring.half + 1):
        if step > 1:
            work = list(pre[step - 2][0])
            if step <= hops:
                (routing,) = after([hop(routing, step - 2)], [below])
                work = work + [routing]
            below, above = after([below, above], work)
        if step == ring.half:
            below, above = below[:cut], above[cut:]
        below, above = ring.send(below, 1), ring.send(above, -1)
        rows = jnp.concatenate([below, above], axis=0)
        if step == ring.half:
            for number in range(min(step - 1, hops - 1), hops):
                routing = hop(routing, number)
            (rows,) = after([rows], pre[step - 1][0])
        if step == ring.half - 1 and step > 2:
            (rows,) = after([rows], pre[step - 2][1])
        pre.append(summed(before_hidden(rows)))

    mine = lax.dynamic_slice_in_dim(routing, index * owned, owned, 1, allow_negative_indices=False)
    offsets = jnp.arange(count, dtype=jnp.int32)
    held = [sum(bit for number, bit in enumerate(far_first) if p >> number & 1) for p in range(count)]
    entry = jnp.bitwise_xor(ring.at(offsets), index)[:, None] == jnp.array(held, jnp.int32)[None, :]
    weights = jnp.sum(jnp.where(entry[:, :, None, None], mine[None], 0.0), axis=1)
    scales = jnp.sum(jnp.where(entry[:, :, None], routing[None, :, -1], 0.0), axis=1)

    outcomes = {}

    def hidden(step, behind):
        offsets = (-step % count, step) if 0 < step < ring.half else (step,)
        weight = jnp.concatenate([weights[o] for o in offsets], axis=1)
        scale = jnp.concatenate([scales[o] for o in offsets], axis=0)
        return hidden_of(after(pre[step][0], behind), pre[step][1], weight, scale)

    def expert_term(offset, behind):
        step = abs(offset)
        if step == ring.half:
            before = hidden(step - 1, pre[step][0] + pre[step - 2][1])
            outcomes[step] = down(hidden(step, [before]))
            outcomes[step - 1] = product(after([before], [outcomes[step]])[0], w_down)
        if step == 1 and pre[0][1] is None:
            own_rows, own_up = after([scaled, *pre[0][0]], behind)
            pre[0] = summed([times(own_rows, w_gate), own_up])
        if step not in outcomes:
            outcomes[step] = down(hidden(step, behind))
        if step in (0, ring.half):
            return outcomes[step]
        return outcomes[step][token_rows:] if offset > 0 else outcomes[step][:token_rows]

    return (residual_state + scatter_rows(ring, expert_term)).astype(bf16)


def solution(mesh):
    return jax.shard_map(
        functools.partial(per_device, mesh.shape["exp"]),
        mesh=mesh,
        in_specs=(
            P(("groups", "exp"), "ctx"),
            P(("groups", "ctx"), "exp"),
            P(("groups", "ctx"), "exp"),
            P(("groups", "ctx"), None),
            P(("groups", "ctx"), None),
            P(None, "exp"),
            P(None, "exp"),
            P("exp", "ctx"),
            P("ctx"),
            P("exp", "ctx", None),
            P("exp", "ctx", None),
            P("exp", None, "ctx"),
            P(("groups", "exp"), None),
            P(("groups", "exp"), None),
            P("groups"),
        ),
        out_specs=P(("groups", "exp"), "ctx"),
        check_vma=False,
    )
```

```python
import functools
import math

import jax
import jax.numpy as jnp
from jax import lax
from jax.experimental import pallas as pl
from jax.experimental.pallas import tpu as pltpu
from jax.sharding import PartitionSpec as P

D = 3584
NOPE = 128
ROPE = 64
VDIM = 128
BLOCK = 512

neg_large = -1e30
route_factor = 2.5
norm_epsilon = 1e-06
f32 = jnp.float32
bf16 = jnp.bfloat16


def attention_kernel(
    order_ref, q_nope_ref, q_rope_ref, own_latent_ref, other_latent_ref, own_rope_ref, other_rope_ref, w_uk_ref, w_uv_ref, out_ref
):
    core = lax.axis_index("ctx")
    rank_of = lambda block: order_ref[block]
    scale = (NOPE + ROPE) ** (-0.5) * math.log2(math.e)
    rows = q_nope_ref.shape[0]
    blocks = rows // BLOCK
    step = 256
    keys_t, values = [], []
    for latent_ref in (own_latent_ref, other_latent_ref):
        latent = latent_ref[...]
        keys_t.append(
            lax.dot_general(w_uk_ref[...], latent, (((0,), (1,)), ((), ())), preferred_element_type=f32).astype(bf16)
        )
        values.append(jnp.dot(latent, w_uv_ref[...], preferred_element_type=f32).astype(bf16))
    ropes = (own_rope_ref[...], other_rope_ref[...])
    blank = jnp.zeros_like(ropes[0])
    diagonal = lax.broadcasted_iota(jnp.int32, (step, step), 1) <= lax.broadcasted_iota(jnp.int32, (step, step), 0)
    key_cat, value_cat = [], []
    for head in range(2):
        cols = slice(head * NOPE, (head + 1) * NOPE)
        key_cat.append([
            jnp.concatenate([keys[cols, :]] + ([rope, blank] if head == 0 else [blank, rope]), axis=0)
            for keys, rope in zip(keys_t, ropes)
        ])
        value_cat.append([jnp.concatenate([held[:, cols], jnp.ones_like(held[:, cols])], axis=1) for held in values])

    def score(head, first):
        cols, part = slice(head * NOPE, (head + 1) * NOPE), slice(first, first + step)
        query = jnp.concatenate([q_nope_ref[part, cols], q_rope_ref[part, :]], axis=1)
        query_block, inside = first // BLOCK, first % BLOCK
        scores = []
        for side in (0, 1):
            owner = core if side == 0 else 1 - core
            for block in range(blocks):
                start = block * BLOCK
                if side == 0 and block == query_block:
                    seen = slice(start, start + inside + step)
                    piece = jnp.dot(query, key_cat[head][side][:, seen], preferred_element_type=f32)
                    last = jnp.where(diagonal, piece[:, inside:], neg_large)
                    piece = jnp.concatenate([piece[:, :inside], last], axis=1) if inside else last
                else:
                    seen = slice(start, start + BLOCK)
                    piece = jnp.dot(query, key_cat[head][side][:, seen], preferred_element_type=f32)
                    earlier = rank_of(owner * blocks + block) < rank_of(core * blocks + query_block)
                    piece = piece + jnp.where(earlier, 0.0, neg_large)
                scores.append((side, seen, piece))
        return scores

    units = [(head, first) for first in range(0, rows, step) for head in range(2)]
    ready = score(*units[0])
    for number, (head, first) in enumerate(units):
        scores = ready
        if number + 1 < len(units):
            ready = score(*units[number + 1])
        best = functools.reduce(jnp.maximum, [jnp.max(piece, axis=1, keepdims=True) for _, _, piece in scores])
        summed = 0.0
        for side, seen, piece in scores:
            probs = jnp.exp2((piece - best) * scale).astype(bf16)
            summed = summed + jnp.dot(probs, value_cat[head][side][seen, :], preferred_element_type=f32)
        out_ref[first : first + step, head * VDIM : (head + 1) * VDIM] = (summed[:, :VDIM] / summed[:, VDIM:]).astype(bf16)


def attend(block_order, q_nope, q_rope, latents, ropes, w_uk, w_uv):
    rows, keys = q_nope.shape[0], 2 * latents[0].shape[0]
    pairs = q_nope.shape[1] // (2 * NOPE)
    held = lambda array: pltpu.with_memory_space_constraint(array, pltpu.HBM)
    whole = lambda array: pl.BlockSpec(array.shape, lambda h, s: (0, 0))
    column = lambda array, width: pl.BlockSpec((array.shape[0], width), lambda h, s: (0, h))
    return pl.pallas_call(
        attention_kernel,
        grid_spec=pltpu.PrefetchScalarGridSpec(
            num_scalar_prefetch=1,
            grid=(pairs,),
            in_specs=[column(q_nope, 2 * NOPE), column(q_rope, 2 * ROPE)]
            + [whole(array) for array in (*latents, *ropes)]
            + [column(w_uk, 2 * NOPE), column(w_uv, 2 * VDIM)],
            out_specs=column(q_nope, 2 * VDIM),
        ),
        out_shape=jax.ShapeDtypeStruct((rows, q_nope.shape[1]), bf16),
        compiler_params=pltpu.CompilerParams(vmem_limit_bytes=12 * 1024 * 1024),
        cost_estimate=pl.CostEstimate(
            flops=7 * rows * keys * pairs * 2 * 384, bytes_accessed=8 * 1024 * 1024, transcendentals=rows * keys * pairs * 2
        ),
    )(held(block_order), held(q_nope), held(q_rope), held(latents[0]), latents[1], held(ropes[0]), ropes[1], held(w_uk), held(w_uv))


def product_kernel(rows_ref, *refs):
    *weight_refs, out_ref = refs
    depth = weight_refs[0].shape[1]
    terms = [
        jnp.dot(rows_ref[e, :, q * depth : (q + 1) * depth], ref[e], preferred_element_type=f32)
        for q, ref in enumerate(weight_refs)
        for e in range(rows_ref.shape[0])
    ]
    out_ref[...] = functools.reduce(jnp.add, terms).astype(bf16)


def product(rows, weights):
    terms, count, depth = rows.shape
    width = weights.shape[2]
    tile, pieces = width // 2, 4
    weights = pltpu.with_memory_space_constraint(weights, pltpu.HBM)
    piece = lambda q: pl.BlockSpec((terms, depth // pieces, tile), lambda n: (0, q, n))
    return pl.pallas_call(
        product_kernel,
        grid=(width // tile,),
        in_specs=[pl.BlockSpec((terms, count, depth), lambda n: (0, 0, 0))] + [piece(q) for q in range(pieces)],
        out_specs=pl.BlockSpec((count, tile), lambda n: (0, n)),
        out_shape=jax.ShapeDtypeStruct((count, width), bf16),
        compiler_params=pltpu.CompilerParams(vmem_limit_bytes=16 * 1024 * 1024),
        cost_estimate=pl.CostEstimate(flops=count * depth * width // 4, bytes_accessed=count * width, transcendentals=0),
    )(rows, *[weights] * pieces)


class Ring:
    def __init__(self, count):
        self.count, self.half = count, count // 2
        self.grid = count == 8
        order = [(2 * p if p < count // 2 else 2 * count - 1 - 2 * p) if self.grid else p for p in range(count)]
        self.up = [(order[p], order[(p + 1) % count]) for p in range(count)]
        self.down = [(t, s) for s, t in self.up]
        index = lax.axis_index("exp")
        self.place = jnp.where(index % 2 == 0, index // 2, count - 1 - index // 2) if self.grid else index

    def index_at(self, place):
        return jnp.where(place < self.half, 2 * place, 2 * self.count - 1 - 2 * place) if self.grid else place

    def at(self, offset):
        return self.index_at(lax.rem(self.place + offset, self.count))

    def send(self, block, way):
        return lax.ppermute(block, "exp", self.up if way > 0 else self.down)


def after(blocks, work):
    if not work:
        return blocks
    held = lax.optimization_barrier((tuple(blocks), tuple(work)))
    return list(held[0])


def scatter_rows(ring, part):
    add = lambda *terms: functools.reduce(jnp.add, [t.astype(f32) for t in terms])
    far = part(ring.half, [])
    sent = [far]
    cut = far.shape[0] // 2
    going = {1: ring.send(far[:cut], 1), -1: ring.send(far[cut:], -1)}
    for offset in range(ring.half - 1, 0, -1):
        behind, sent = sent, []
        for way in (1, -1):
            own, come = part(way * offset, behind), going[way]
            if offset == ring.half - 1:
                come = jnp.pad(come, ((0, cut) if way > 0 else (cut, 0), (0, 0)))
            block = add(own, come).astype(bf16)
            sent.append(block)
            going[way] = ring.send(block, way)
    return add(part(0, sent), going[1], going[-1])


def per_device(
    count,
    resid,
    q_nope,
    q_rope,
    latent,
    k_rope,
    w_uk,
    w_uv,
    w_out,
    norm_gain,
    w_gate,
    w_up,
    w_down,
    routes,
    codes,
    block_order,
):
    token_rows, owned = resid.shape[0], w_gate.shape[0]
    cut = token_rows // 2
    ring = Ring(count)
    core, index = lax.axis_index("ctx"), lax.axis_index("exp")
    swap = lambda block: lax.ppermute(block, "ctx", [(0, 1), (1, 0)])

    ropes = k_rope.T
    heads = attend(
        block_order, q_nope, q_rope, (latent, swap(latent)), (ropes, swap(ropes)), w_uk, w_uv
    )

    other_heads = swap(heads)
    project = lambda rows: jnp.dot(rows, w_out, preferred_element_type=f32).astype(bf16)

    def block_of(offset):
        return jnp.bitwise_and(ring.at(offset % count) - core * ring.half, count - 1)

    def pick(own, other, block):
        first = jnp.minimum(block, ring.half - 1) * token_rows
        second = jnp.maximum(block - ring.half, 0) * token_rows
        part = lambda rows, at: lax.dynamic_slice_in_dim(rows, at, token_rows, 0, allow_negative_indices=False)
        return jnp.where(block < ring.half, part(own, first), part(other, second))

    nearby = {}

    def attention_term(offset, behind):
        if offset == ring.half:
            return product(pick(heads, other_heads, block_of(offset))[None], w_out[None])
        if abs(offset) == ring.half - 1:
            if "first" not in nearby:
                rows = [pick(heads, other_heads, block_of(way * abs(offset))) for way in (1, -1)]
                rows = after([jnp.concatenate(rows, axis=0)], behind)[0]
                nearby["first"] = product(rows[None], w_out[None])
            return nearby["first"][:token_rows] if offset > 0 else nearby["first"][token_rows:]
        if "terms" not in nearby:
            later = after([heads, other_heads], behind)
            nearby["terms"] = [project(rows) for rows in later]
        return lax.optimization_barrier(pick(*nearby["terms"], block_of(offset)))

    residual_state = resid.astype(f32) + scatter_rows(ring, attention_term)

    code_values = codes.astype(f32)
    route_weight = route_factor * code_values / jnp.sum(code_values, axis=1, keepdims=True)
    named = routes[None] == jnp.arange(count * owned, dtype=jnp.int32)[:, None, None]
    routing = jnp.sum(jnp.where(named, route_weight[None], 0.0), axis=2)[None]
    scaled = (residual_state * norm_gain).astype(bf16)
    squares = jnp.sum(residual_state * residual_state, axis=1)
    squares = squares + swap(squares)
    inverse_rms = lax.rsqrt(squares / D + norm_epsilon)
    routing = jnp.concatenate([routing, inverse_rms[None, None]], axis=1)

    def before_hidden(rows):
        product = lambda weight: jnp.einsum("td,ldf->ltf", rows, weight, preferred_element_type=f32).astype(bf16)
        own = [product(w_gate), product(w_up)]
        return own

    def summed(own):
        return own, [swap(pre) for pre in own]

    def hidden_of(own, other, weight, scale):
        gate_pre, up_pre = [mine.astype(f32) + theirs.astype(f32) for mine, theirs in zip(own, other)]
        gate_pre = gate_pre * scale[:, None]
        return (jax.nn.silu(gate_pre) * up_pre * (weight * scale)[:, :, None]).astype(bf16)

    def down(hidden):
        return functools.reduce(
            jnp.add, [jnp.dot(hidden[e], w_down[e], preferred_element_type=f32) for e in range(owned)]
        ).astype(bf16)

    pre = [(before_hidden(scaled), None)]
    below = above = scaled
    hops = count.bit_length() - 1
    far_first = [count >> (1 + number) for number in range(hops)]

    def hop(routing, number):
        other = lax.ppermute(routing, "exp", [(i, i ^ far_first[number]) for i in range(count)])
        return jnp.concatenate([routing, other], axis=0)

    for step in range(1, ring.half + 1):
        if step > 1:
            work = list(pre[step - 2][0])
            if step <= hops:
                if step > 2:
                    work = work + [routing]
                    (routing,) = after([routing], [below])
                routing = hop(routing, step - 2)
            below, above = after([below, above], work)
        if step == ring.half:
            below, above = below[:cut], above[cut:]
        below, above = ring.send(below, 1), ring.send(above, -1)
        rows = jnp.concatenate([below, above], axis=0)
        if step == ring.half:
            for number in range(min(step - 1, hops - 1), hops):
                routing = hop(routing, number)
            (rows,) = after([rows], pre[step - 1][0])
        if step == ring.half - 1 and step > 2:
            (rows,) = after([rows], pre[step - 2][1])
        pre.append(summed(before_hidden(rows)))

    mine = lax.dynamic_slice_in_dim(routing, index * owned, owned, 1, allow_negative_indices=False)
    offsets = jnp.arange(count, dtype=jnp.int32)
    held = [sum(bit for number, bit in enumerate(far_first) if p >> number & 1) for p in range(count)]
    entry = jnp.bitwise_xor(ring.at(offsets), index)[:, None] == jnp.array(held, jnp.int32)[None, :]
    weights = jnp.sum(jnp.where(entry[:, :, None, None], mine[None], 0.0), axis=1)
    scales = jnp.sum(jnp.where(entry[:, :, None], routing[None, :, -1], 0.0), axis=1)

    outcomes = {}

    def hidden(step, behind):
        offsets = (-step % count, step) if 0 < step < ring.half else (step,)
        weight = jnp.concatenate([weights[o] for o in offsets], axis=1)
        scale = jnp.concatenate([scales[o] for o in offsets], axis=0)
        return hidden_of(after(pre[step][0], behind), pre[step][1], weight, scale)

    def expert_term(offset, behind):
        step = abs(offset)
        if step == ring.half:
            before = hidden(step - 1, pre[step][0] + pre[step - 2][1])
            outcomes[step] = down(hidden(step, [before]))
            outcomes[step - 1] = product(after([before], [outcomes[step]])[0], w_down)
        if step == 1:
            pre[0] = summed(after(pre[0][0], behind))
        if step not in outcomes:
            outcomes[step] = down(hidden(step, behind))
        if step in (0, ring.half):
            return outcomes[step]
        return outcomes[step][token_rows:] if offset > 0 else outcomes[step][:token_rows]

    return (residual_state + scatter_rows(ring, expert_term)).astype(bf16)


def solution(mesh):
    return jax.shard_map(
        functools.partial(per_device, mesh.shape["exp"]),
        mesh=mesh,
        in_specs=(
            P(("groups", "exp"), "ctx"),
            P(("groups", "ctx"), "exp"),
            P(("groups", "ctx"), "exp"),
            P(("groups", "ctx"), None),
            P(("groups", "ctx"), None),
            P(None, "exp"),
            P(None, "exp"),
            P("exp", "ctx"),
            P("ctx"),
            P("exp", "ctx", None),
            P("exp", "ctx", None),
            P("exp", None, "ctx"),
            P(("groups", "exp"), None),
            P(("groups", "exp"), None),
            P("groups"),
        ),
        out_specs=P(("groups", "exp"), "ctx"),
        check_vma=False,
    )
```

```python
import functools
import math

import jax
import jax.numpy as jnp
from jax import lax
from jax.experimental import pallas as pl
from jax.experimental.pallas import tpu as pltpu
from jax.sharding import PartitionSpec as P

D = 3584
NOPE = 128
ROPE = 64
VDIM = 128
BLOCK = 512

neg_large = -1e30
route_factor = 2.5
norm_epsilon = 1e-06
f32 = jnp.float32
bf16 = jnp.bfloat16


def attention_kernel(
    order_ref, q_nope_ref, q_rope_ref, own_latent_ref, other_latent_ref, own_rope_ref, other_rope_ref, w_uk_ref, w_uv_ref, out_ref
):
    core = lax.axis_index("ctx")
    rank_of = lambda block: order_ref[block]
    scale = (NOPE + ROPE) ** (-0.5) * math.log2(math.e)
    rows = q_nope_ref.shape[0]
    blocks = rows // BLOCK
    step = 256
    keys_t, values = [], []
    for latent_ref in (own_latent_ref, other_latent_ref):
        latent = latent_ref[...]
        keys_t.append(
            lax.dot_general(w_uk_ref[...], latent, (((0,), (1,)), ((), ())), preferred_element_type=f32).astype(bf16)
        )
        values.append(jnp.dot(latent, w_uv_ref[...], preferred_element_type=f32).astype(bf16))
    ropes = (own_rope_ref[...], other_rope_ref[...])
    blank = jnp.zeros_like(ropes[0])
    diagonal = lax.broadcasted_iota(jnp.int32, (step, step), 1) <= lax.broadcasted_iota(jnp.int32, (step, step), 0)
    key_cat, value_cat = [], []
    for head in range(2):
        cols = slice(head * NOPE, (head + 1) * NOPE)
        key_cat.append([
            jnp.concatenate([keys[cols, :]] + ([rope, blank] if head == 0 else [blank, rope]), axis=0)
            for keys, rope in zip(keys_t, ropes)
        ])
        value_cat.append([jnp.concatenate([held[:, cols], jnp.ones_like(held[:, cols])], axis=1) for held in values])

    def score(head, first):
        cols, part = slice(head * NOPE, (head + 1) * NOPE), slice(first, first + step)
        query = jnp.concatenate([q_nope_ref[part, cols], q_rope_ref[part, :]], axis=1)
        query_block, inside = first // BLOCK, first % BLOCK
        scores = []
        for side in (0, 1):
            owner = core if side == 0 else 1 - core
            for block in range(blocks):
                start = block * BLOCK
                if side == 0 and block == query_block:
                    seen = slice(start, start + inside + step)
                    piece = jnp.dot(query, key_cat[head][side][:, seen], preferred_element_type=f32)
                    last = jnp.where(diagonal, piece[:, inside:], neg_large)
                    piece = jnp.concatenate([piece[:, :inside], last], axis=1) if inside else last
                else:
                    seen = slice(start, start + BLOCK)
                    piece = jnp.dot(query, key_cat[head][side][:, seen], preferred_element_type=f32)
                    earlier = rank_of(owner * blocks + block) < rank_of(core * blocks + query_block)
                    piece = piece + jnp.where(earlier, 0.0, neg_large)
                scores.append((side, seen, piece))
        return scores

    units = [(head, first) for first in range(0, rows, step) for head in range(2)]
    ready = [score(*unit) for unit in units[:2]]
    for number, (head, first) in enumerate(units):
        scores = ready.pop(0)
        if number + 2 < len(units):
            ready.append(score(*units[number + 2]))
        best = functools.reduce(jnp.maximum, [jnp.max(piece, axis=1, keepdims=True) for _, _, piece in scores])
        summed = 0.0
        for side, seen, piece in scores:
            probs = jnp.exp2((piece - best) * scale).astype(bf16)
            summed = summed + jnp.dot(probs, value_cat[head][side][seen, :], preferred_element_type=f32)
        out_ref[first : first + step, head * VDIM : (head + 1) * VDIM] = (summed[:, :VDIM] / summed[:, VDIM:]).astype(bf16)


def attend(block_order, q_nope, q_rope, latents, ropes, w_uk, w_uv):
    rows, keys = q_nope.shape[0], 2 * latents[0].shape[0]
    pairs = q_nope.shape[1] // (2 * NOPE)
    held = lambda array: pltpu.with_memory_space_constraint(array, pltpu.HBM)
    whole = lambda array: pl.BlockSpec(array.shape, lambda h, s: (0, 0))
    column = lambda array, width: pl.BlockSpec((array.shape[0], width), lambda h, s: (0, h))
    return pl.pallas_call(
        attention_kernel,
        grid_spec=pltpu.PrefetchScalarGridSpec(
            num_scalar_prefetch=1,
            grid=(pairs,),
            in_specs=[column(q_nope, 2 * NOPE), column(q_rope, 2 * ROPE)]
            + [whole(array) for array in (*latents, *ropes)]
            + [column(w_uk, 2 * NOPE), column(w_uv, 2 * VDIM)],
            out_specs=column(q_nope, 2 * VDIM),
        ),
        out_shape=jax.ShapeDtypeStruct((rows, q_nope.shape[1]), bf16),
        compiler_params=pltpu.CompilerParams(vmem_limit_bytes=24 * 1024 * 1024),
        cost_estimate=pl.CostEstimate(
            flops=7 * rows * keys * pairs * 2 * 384, bytes_accessed=8 * 1024 * 1024, transcendentals=rows * keys * pairs * 2
        ),
    )(held(block_order), held(q_nope), held(q_rope), held(latents[0]), latents[1], held(ropes[0]), ropes[1], held(w_uk), held(w_uv))


def product_kernel(rows_ref, *refs):
    *weight_refs, out_ref = refs
    depth = weight_refs[0].shape[1]
    terms = [
        jnp.dot(rows_ref[e, :, q * depth : (q + 1) * depth], ref[e], preferred_element_type=f32)
        for q, ref in enumerate(weight_refs)
        for e in range(rows_ref.shape[0])
    ]
    out_ref[...] = functools.reduce(jnp.add, terms).astype(bf16)


def product(rows, weights):
    terms, count, depth = rows.shape
    width = weights.shape[2]
    tile, pieces = width // 2, 4
    weights = pltpu.with_memory_space_constraint(weights, pltpu.HBM)
    piece = lambda q: pl.BlockSpec((terms, depth // pieces, tile), lambda n: (0, q, n))
    return pl.pallas_call(
        product_kernel,
        grid=(width // tile,),
        in_specs=[pl.BlockSpec((terms, count, depth), lambda n: (0, 0, 0))] + [piece(q) for q in range(pieces)],
        out_specs=pl.BlockSpec((count, tile), lambda n: (0, n)),
        out_shape=jax.ShapeDtypeStruct((count, width), bf16),
        compiler_params=pltpu.CompilerParams(vmem_limit_bytes=16 * 1024 * 1024),
        cost_estimate=pl.CostEstimate(flops=count * depth * width // 4, bytes_accessed=count * width, transcendentals=0),
    )(rows, *[weights] * pieces)


class Ring:
    def __init__(self, count):
        self.count, self.half = count, count // 2
        self.grid = count == 8
        order = [(2 * p if p < count // 2 else 2 * count - 1 - 2 * p) if self.grid else p for p in range(count)]
        self.up = [(order[p], order[(p + 1) % count]) for p in range(count)]
        self.down = [(t, s) for s, t in self.up]
        index = lax.axis_index("exp")
        self.place = jnp.where(index % 2 == 0, index // 2, count - 1 - index // 2) if self.grid else index

    def index_at(self, place):
        return jnp.where(place < self.half, 2 * place, 2 * self.count - 1 - 2 * place) if self.grid else place

    def at(self, offset):
        return self.index_at(lax.rem(self.place + offset, self.count))

    def send(self, block, way):
        return lax.ppermute(block, "exp", self.up if way > 0 else self.down)


def after(blocks, work):
    if not work:
        return blocks
    held = lax.optimization_barrier((tuple(blocks), tuple(work)))
    return list(held[0])


def scatter_rows(ring, part):
    add = lambda *terms: functools.reduce(jnp.add, [t.astype(f32) for t in terms])
    far = part(ring.half, [])
    sent = [far]
    cut = far.shape[0] // 2
    going = {1: ring.send(far[:cut], 1), -1: ring.send(far[cut:], -1)}
    for offset in range(ring.half - 1, 0, -1):
        behind, sent = sent, []
        for way in (1, -1):
            own, come = part(way * offset, behind), going[way]
            if offset == ring.half - 1:
                come = jnp.pad(come, ((0, cut) if way > 0 else (cut, 0), (0, 0)))
            block = add(own, come).astype(bf16)
            sent.append(block)
            going[way] = ring.send(block, way)
    return add(part(0, sent), going[1], going[-1])


def per_device(
    count,
    resid,
    q_nope,
    q_rope,
    latent,
    k_rope,
    w_uk,
    w_uv,
    w_out,
    norm_gain,
    w_gate,
    w_up,
    w_down,
    routes,
    codes,
    block_order,
):
    token_rows, owned = resid.shape[0], w_gate.shape[0]
    cut = token_rows // 2
    ring = Ring(count)
    core, index = lax.axis_index("ctx"), lax.axis_index("exp")
    swap = lambda block: lax.ppermute(block, "ctx", [(0, 1), (1, 0)])

    ropes = k_rope.T
    heads = attend(
        block_order, q_nope, q_rope, (latent, swap(latent)), (ropes, swap(ropes)), w_uk, w_uv
    )

    other_heads = swap(heads)
    project = lambda rows: jnp.dot(rows, w_out, preferred_element_type=f32).astype(bf16)

    def block_of(offset):
        return jnp.bitwise_and(ring.at(offset % count) - core * ring.half, count - 1)

    def pick(own, other, block):
        first = jnp.minimum(block, ring.half - 1) * token_rows
        second = jnp.maximum(block - ring.half, 0) * token_rows
        part = lambda rows, at: lax.dynamic_slice_in_dim(rows, at, token_rows, 0, allow_negative_indices=False)
        return jnp.where(block < ring.half, part(own, first), part(other, second))

    nearby = {}

    def attention_term(offset, behind):
        if offset == ring.half:
            return product(pick(heads, other_heads, block_of(offset))[None], w_out[None])
        if abs(offset) == ring.half - 1:
            if "first" not in nearby:
                rows = [pick(heads, other_heads, block_of(way * abs(offset))) for way in (1, -1)]
                rows = after([jnp.concatenate(rows, axis=0)], behind)[0]
                nearby["first"] = product(rows[None], w_out[None])
            return nearby["first"][:token_rows] if offset > 0 else nearby["first"][token_rows:]
        if "terms" not in nearby:
            later = after([heads, other_heads], behind)
            nearby["terms"] = [project(rows) for rows in later]
        return lax.optimization_barrier(pick(*nearby["terms"], block_of(offset)))

    residual_state = resid.astype(f32) + scatter_rows(ring, attention_term)

    code_values = codes.astype(f32)
    route_weight = route_factor * code_values / jnp.sum(code_values, axis=1, keepdims=True)
    named = routes[None] == jnp.arange(count * owned, dtype=jnp.int32)[:, None, None]
    routing = jnp.sum(jnp.where(named, route_weight[None], 0.0), axis=2)[None]
    scaled = (residual_state * norm_gain).astype(bf16)
    squares = jnp.sum(residual_state * residual_state, axis=1)
    squares = squares + swap(squares)
    inverse_rms = lax.rsqrt(squares / D + norm_epsilon)
    routing = jnp.concatenate([routing, inverse_rms[None, None]], axis=1)

    def before_hidden(rows):
        product = lambda weight: jnp.einsum("td,ldf->ltf", rows, weight, preferred_element_type=f32).astype(bf16)
        own = [product(w_gate), product(w_up)]
        return own

    def summed(own):
        return own, [swap(pre) for pre in own]

    def hidden_of(own, other, weight, scale):
        gate_pre, up_pre = [mine.astype(f32) + theirs.astype(f32) for mine, theirs in zip(own, other)]
        gate_pre = gate_pre * scale[:, None]
        return (jax.nn.silu(gate_pre) * up_pre * (weight * scale)[:, :, None]).astype(bf16)

    def down(hidden):
        return functools.reduce(
            jnp.add, [jnp.dot(hidden[e], w_down[e], preferred_element_type=f32) for e in range(owned)]
        ).astype(bf16)

    pre = [(before_hidden(scaled), None)]
    below = above = scaled
    hops = count.bit_length() - 1
    far_first = [count >> (1 + number) for number in range(hops)]

    def hop(routing, number):
        other = lax.ppermute(routing, "exp", [(i, i ^ far_first[number]) for i in range(count)])
        return jnp.concatenate([routing, other], axis=0)

    for step in range(1, ring.half + 1):
        if step > 1:
            work = list(pre[step - 2][0])
            if step <= hops:
                (routing,) = after([hop(routing, step - 2)], [below])
                work = work + [routing]
            below, above = after([below, above], work)
        if step == ring.half:
            below, above = below[:cut], above[cut:]
        below, above = ring.send(below, 1), ring.send(above, -1)
        rows = jnp.concatenate([below, above], axis=0)
        if step == ring.half:
            for number in range(min(step - 1, hops - 1), hops):
                routing = hop(routing, number)
            (rows,) = after([rows], pre[step - 1][0])
        if step == ring.half - 1 and step > 2:
            (rows,) = after([rows], pre[step - 2][1])
        pre.append(summed(before_hidden(rows)))

    mine = lax.dynamic_slice_in_dim(routing, index * owned, owned, 1, allow_negative_indices=False)
    offsets = jnp.arange(count, dtype=jnp.int32)
    held = [sum(bit for number, bit in enumerate(far_first) if p >> number & 1) for p in range(count)]
    entry = jnp.bitwise_xor(ring.at(offsets), index)[:, None] == jnp.array(held, jnp.int32)[None, :]
    weights = jnp.sum(jnp.where(entry[:, :, None, None], mine[None], 0.0), axis=1)
    scales = jnp.sum(jnp.where(entry[:, :, None], routing[None, :, -1], 0.0), axis=1)

    outcomes = {}

    def hidden(step, behind):
        offsets = (-step % count, step) if 0 < step < ring.half else (step,)
        weight = jnp.concatenate([weights[o] for o in offsets], axis=1)
        scale = jnp.concatenate([scales[o] for o in offsets], axis=0)
        return hidden_of(after(pre[step][0], behind), pre[step][1], weight, scale)

    def expert_term(offset, behind):
        step = abs(offset)
        if step == ring.half:
            before = hidden(step - 1, pre[step][0] + pre[step - 2][1])
            outcomes[step] = down(hidden(step, [before]))
            outcomes[step - 1] = product(after([before], [outcomes[step]])[0], w_down)
        if step == 1:
            pre[0] = summed(after(pre[0][0], behind))
        if step not in outcomes:
            outcomes[step] = down(hidden(step, behind))
        if step in (0, ring.half):
            return outcomes[step]
        return outcomes[step][token_rows:] if offset > 0 else outcomes[step][:token_rows]

    return (residual_state + scatter_rows(ring, expert_term)).astype(bf16)


def solution(mesh):
    return jax.shard_map(
        functools.partial(per_device, mesh.shape["exp"]),
        mesh=mesh,
        in_specs=(
            P(("groups", "exp"), "ctx"),
            P(("groups", "ctx"), "exp"),
            P(("groups", "ctx"), "exp"),
            P(("groups", "ctx"), None),
            P(("groups", "ctx"), None),
            P(None, "exp"),
            P(None, "exp"),
            P("exp", "ctx"),
            P("ctx"),
            P("exp", "ctx", None),
            P("exp", "ctx", None),
            P("exp", None, "ctx"),
            P(("groups", "exp"), None),
            P(("groups", "exp"), None),
            P("groups"),
        ),
        out_specs=P(("groups", "exp"), "ctx"),
        check_vma=False,
    )
```

```python
import functools
import math

import jax
import jax.numpy as jnp
from jax import lax
from jax.experimental import pallas as pl
from jax.experimental.pallas import tpu as pltpu
from jax.sharding import PartitionSpec as P

D = 3584
NOPE = 128
ROPE = 64
VDIM = 128
BLOCK = 512

neg_large = -1e30
route_factor = 2.5
norm_epsilon = 1e-06
f32 = jnp.float32
bf16 = jnp.bfloat16


def attention_kernel(
    order_ref, q_nope_ref, q_rope_ref, own_latent_ref, other_latent_ref, own_rope_ref, other_rope_ref, w_uk_ref, w_uv_ref, out_ref
):
    core = lax.axis_index("ctx")
    rank_of = lambda block: order_ref[block]
    scale = (NOPE + ROPE) ** (-0.5) * math.log2(math.e)
    rows = q_nope_ref.shape[0]
    blocks = rows // BLOCK
    step = 256
    keys_t, values = [], []
    for latent_ref in (own_latent_ref, other_latent_ref):
        latent = latent_ref[...]
        keys_t.append(
            lax.dot_general(w_uk_ref[...], latent, (((0,), (1,)), ((), ())), preferred_element_type=f32).astype(bf16)
        )
        values.append(jnp.dot(latent, w_uv_ref[...], preferred_element_type=f32).astype(bf16))
    ropes = (own_rope_ref[...], other_rope_ref[...])
    blank = jnp.zeros_like(ropes[0])
    diagonal = lax.broadcasted_iota(jnp.int32, (step, step), 1) <= lax.broadcasted_iota(jnp.int32, (step, step), 0)
    key_cat, value_cat = [], []
    for head in range(2):
        cols = slice(head * NOPE, (head + 1) * NOPE)
        key_cat.append([
            jnp.concatenate([keys[cols, :]] + ([rope, blank] if head == 0 else [blank, rope]), axis=0)
            for keys, rope in zip(keys_t, ropes)
        ])
        value_cat.append([jnp.concatenate([held[:, cols], jnp.ones_like(held[:, cols])], axis=1) for held in values])

    def score(head, first):
        cols, part = slice(head * NOPE, (head + 1) * NOPE), slice(first, first + step)
        query = jnp.concatenate([q_nope_ref[part, cols], q_rope_ref[part, :]], axis=1)
        query_block, inside = first // BLOCK, first % BLOCK
        scores = []
        for side in (0, 1):
            owner = core if side == 0 else 1 - core
            for block in range(blocks):
                start = block * BLOCK
                if side == 0 and block == query_block:
                    seen = slice(start, start + inside + step)
                    piece = jnp.dot(query, key_cat[head][side][:, seen], preferred_element_type=f32)
                    last = jnp.where(diagonal, piece[:, inside:], neg_large)
                    piece = jnp.concatenate([piece[:, :inside], last], axis=1) if inside else last
                else:
                    seen = slice(start, start + BLOCK)
                    piece = jnp.dot(query, key_cat[head][side][:, seen], preferred_element_type=f32)
                    earlier = rank_of(owner * blocks + block) < rank_of(core * blocks + query_block)
                    piece = piece + jnp.where(earlier, 0.0, neg_large)
                scores.append((side, seen, piece))
        return scores

    units = [(head, first) for first in range(0, rows, step) for head in range(2)]
    ready = score(*units[0])
    for number, (head, first) in enumerate(units):
        scores = ready
        if number + 1 < len(units):
            ready = score(*units[number + 1])
        best = functools.reduce(jnp.maximum, [jnp.max(piece, axis=1, keepdims=True) for _, _, piece in scores])
        summed = 0.0
        for side, seen, piece in scores:
            probs = jnp.exp2((piece - best) * scale).astype(bf16)
            summed = summed + jnp.dot(probs, value_cat[head][side][seen, :], preferred_element_type=f32)
        out_ref[first : first + step, head * VDIM : (head + 1) * VDIM] = (summed[:, :VDIM] / summed[:, VDIM:]).astype(bf16)


def attend(block_order, q_nope, q_rope, latents, ropes, w_uk, w_uv):
    rows, keys = q_nope.shape[0], 2 * latents[0].shape[0]
    pairs = q_nope.shape[1] // (2 * NOPE)
    held = lambda array: pltpu.with_memory_space_constraint(array, pltpu.HBM)
    whole = lambda array: pl.BlockSpec(array.shape, lambda h, s: (0, 0))
    column = lambda array, width: pl.BlockSpec((array.shape[0], width), lambda h, s: (0, h))
    return pl.pallas_call(
        attention_kernel,
        grid_spec=pltpu.PrefetchScalarGridSpec(
            num_scalar_prefetch=1,
            grid=(pairs,),
            in_specs=[column(q_nope, 2 * NOPE), column(q_rope, 2 * ROPE)]
            + [whole(array) for array in (*latents, *ropes)]
            + [column(w_uk, 2 * NOPE), column(w_uv, 2 * VDIM)],
            out_specs=column(q_nope, 2 * VDIM),
        ),
        out_shape=jax.ShapeDtypeStruct((rows, q_nope.shape[1]), bf16),
        compiler_params=pltpu.CompilerParams(vmem_limit_bytes=12 * 1024 * 1024),
        cost_estimate=pl.CostEstimate(
            flops=7 * rows * keys * pairs * 2 * 384, bytes_accessed=8 * 1024 * 1024, transcendentals=rows * keys * pairs * 2
        ),
    )(held(block_order), held(q_nope), held(q_rope), held(latents[0]), latents[1], held(ropes[0]), ropes[1], held(w_uk), held(w_uv))


def product_kernel(rows_ref, *refs):
    *weight_refs, out_ref = refs
    depth = weight_refs[0].shape[1]
    terms = [
        jnp.dot(rows_ref[e, :, q * depth : (q + 1) * depth], ref[e], preferred_element_type=f32)
        for q, ref in enumerate(weight_refs)
        for e in range(rows_ref.shape[0])
    ]
    out_ref[...] = functools.reduce(jnp.add, terms).astype(bf16)


def product(rows, weights):
    terms, count, depth = rows.shape
    width = weights.shape[2]
    tile, pieces = width // 2, 4
    weights = pltpu.with_memory_space_constraint(weights, pltpu.HBM)
    piece = lambda q: pl.BlockSpec((terms, depth // pieces, tile), lambda n: (0, q, n))
    return pl.pallas_call(
        product_kernel,
        grid=(width // tile,),
        in_specs=[pl.BlockSpec((terms, count, depth), lambda n: (0, 0, 0))] + [piece(q) for q in range(pieces)],
        out_specs=pl.BlockSpec((count, tile), lambda n: (0, n)),
        out_shape=jax.ShapeDtypeStruct((count, width), bf16),
        compiler_params=pltpu.CompilerParams(vmem_limit_bytes=16 * 1024 * 1024),
        cost_estimate=pl.CostEstimate(flops=count * depth * width // 4, bytes_accessed=count * width, transcendentals=0),
    )(rows, *[weights] * pieces)


class Ring:
    def __init__(self, count):
        self.count, self.half = count, count // 2
        self.grid = count == 8
        order = [(2 * p if p < count // 2 else 2 * count - 1 - 2 * p) if self.grid else p for p in range(count)]
        self.up = [(order[p], order[(p + 1) % count]) for p in range(count)]
        self.down = [(t, s) for s, t in self.up]
        index = lax.axis_index("exp")
        self.place = jnp.where(index % 2 == 0, index // 2, count - 1 - index // 2) if self.grid else index

    def index_at(self, place):
        return jnp.where(place < self.half, 2 * place, 2 * self.count - 1 - 2 * place) if self.grid else place

    def at(self, offset):
        return self.index_at(lax.rem(self.place + offset, self.count))

    def send(self, block, way):
        return lax.ppermute(block, "exp", self.up if way > 0 else self.down)


def after(blocks, work):
    if not work:
        return blocks
    held = lax.optimization_barrier((tuple(blocks), tuple(work)))
    return list(held[0])


def scatter_rows(ring, part):
    add = lambda *terms: functools.reduce(jnp.add, [t.astype(f32) for t in terms])
    far = part(ring.half, [])
    sent = [far]
    cut = far.shape[0] // 2
    going = {1: ring.send(far[:cut], 1), -1: ring.send(far[cut:], -1)}
    for offset in range(ring.half - 1, 0, -1):
        behind, sent = sent, []
        for way in (1, -1):
            own, come = part(way * offset, behind), going[way]
            if offset == ring.half - 1:
                come = jnp.pad(come, ((0, cut) if way > 0 else (cut, 0), (0, 0)))
            block = add(own, come).astype(bf16)
            sent.append(block)
            going[way] = ring.send(block, way)
    return add(part(0, sent), going[1], going[-1])


def per_device(
    count,
    resid,
    q_nope,
    q_rope,
    latent,
    k_rope,
    w_uk,
    w_uv,
    w_out,
    norm_gain,
    w_gate,
    w_up,
    w_down,
    routes,
    codes,
    block_order,
):
    token_rows, owned = resid.shape[0], w_gate.shape[0]
    cut = token_rows // 2
    ring = Ring(count)
    core, index = lax.axis_index("ctx"), lax.axis_index("exp")
    swap = lambda block: lax.ppermute(block, "ctx", [(0, 1), (1, 0)])

    ropes = k_rope.T
    heads = attend(
        block_order, q_nope, q_rope, (latent, swap(latent)), (ropes, swap(ropes)), w_uk, w_uv
    )

    project = lambda rows: jnp.dot(rows, w_out, preferred_element_type=f32).astype(bf16)

    def block_of(offset):
        return jnp.bitwise_and(ring.at(offset % count) - core * ring.half, count - 1)

    def pick(own, other, block):
        first = jnp.minimum(block, ring.half - 1) * token_rows
        second = jnp.maximum(block - ring.half, 0) * token_rows
        part = lambda rows, at: lax.dynamic_slice_in_dim(rows, at, token_rows, 0, allow_negative_indices=False)
        return jnp.where(block < ring.half, part(own, first), part(other, second))

    far = block_of(ring.half)
    first = jnp.bitwise_and(far, ring.half - 1) * token_rows
    mine = lax.dynamic_slice_in_dim(heads, first, token_rows, 0, allow_negative_indices=False)
    theirs = swap(mine)
    far_rows = jnp.where(far < ring.half, mine, theirs)
    other_heads = swap(after([heads], [theirs])[0])
    nearby = {}

    def attention_term(offset, behind):
        if offset == ring.half:
            return product(far_rows[None], w_out[None])
        if abs(offset) == ring.half - 1:
            if "first" not in nearby:
                rows = [pick(heads, other_heads, block_of(way * abs(offset))) for way in (1, -1)]
                rows = after([jnp.concatenate(rows, axis=0)], behind)[0]
                nearby["first"] = product(rows[None], w_out[None])
            return nearby["first"][:token_rows] if offset > 0 else nearby["first"][token_rows:]
        if "terms" not in nearby:
            later = after([heads, other_heads], behind)
            nearby["terms"] = [project(rows) for rows in later]
        return lax.optimization_barrier(pick(*nearby["terms"], block_of(offset)))

    residual_state = resid.astype(f32) + scatter_rows(ring, attention_term)

    code_values = codes.astype(f32)
    route_weight = route_factor * code_values / jnp.sum(code_values, axis=1, keepdims=True)
    named = routes[None] == jnp.arange(count * owned, dtype=jnp.int32)[:, None, None]
    routing = jnp.sum(jnp.where(named, route_weight[None], 0.0), axis=2)[None]
    scaled = (residual_state * norm_gain).astype(bf16)
    squares = jnp.sum(residual_state * residual_state, axis=1)
    squares = squares + swap(squares)
    inverse_rms = lax.rsqrt(squares / D + norm_epsilon)
    routing = jnp.concatenate([routing, inverse_rms[None, None]], axis=1)

    def before_hidden(rows):
        product = lambda weight: jnp.einsum("td,ldf->ltf", rows, weight, preferred_element_type=f32).astype(bf16)
        own = [product(w_gate), product(w_up)]
        return own

    def summed(own):
        return own, [swap(pre) for pre in own]

    def hidden_of(own, other, weight, scale):
        gate_pre, up_pre = [mine.astype(f32) + theirs.astype(f32) for mine, theirs in zip(own, other)]
        gate_pre = gate_pre * scale[:, None]
        return (jax.nn.silu(gate_pre) * up_pre * (weight * scale)[:, :, None]).astype(bf16)

    def down(hidden):
        return functools.reduce(
            jnp.add, [jnp.dot(hidden[e], w_down[e], preferred_element_type=f32) for e in range(owned)]
        ).astype(bf16)

    pre = [(before_hidden(scaled), None)]
    below = above = scaled
    hops = count.bit_length() - 1
    far_first = [count >> (1 + number) for number in range(hops)]

    def hop(routing, number):
        other = lax.ppermute(routing, "exp", [(i, i ^ far_first[number]) for i in range(count)])
        return jnp.concatenate([routing, other], axis=0)

    for step in range(1, ring.half + 1):
        if step > 1:
            work = list(pre[step - 2][0])
            if step <= hops:
                (routing,) = after([hop(routing, step - 2)], [below])
                work = work + [routing]
            below, above = after([below, above], work)
        if step == ring.half:
            below, above = below[:cut], above[cut:]
        below, above = ring.send(below, 1), ring.send(above, -1)
        rows = jnp.concatenate([below, above], axis=0)
        if step == ring.half:
            for number in range(min(step - 1, hops - 1), hops):
                routing = hop(routing, number)
            (rows,) = after([rows], pre[step - 1][0])
        if step == ring.half - 1 and step > 2:
            (rows,) = after([rows], pre[step - 2][1])
        pre.append(summed(before_hidden(rows)))

    mine = lax.dynamic_slice_in_dim(routing, index * owned, owned, 1, allow_negative_indices=False)
    offsets = jnp.arange(count, dtype=jnp.int32)
    held = [sum(bit for number, bit in enumerate(far_first) if p >> number & 1) for p in range(count)]
    entry = jnp.bitwise_xor(ring.at(offsets), index)[:, None] == jnp.array(held, jnp.int32)[None, :]
    weights = jnp.sum(jnp.where(entry[:, :, None, None], mine[None], 0.0), axis=1)
    scales = jnp.sum(jnp.where(entry[:, :, None], routing[None, :, -1], 0.0), axis=1)

    outcomes = {}

    def hidden(step, behind):
        offsets = (-step % count, step) if 0 < step < ring.half else (step,)
        weight = jnp.concatenate([weights[o] for o in offsets], axis=1)
        scale = jnp.concatenate([scales[o] for o in offsets], axis=0)
        return hidden_of(after(pre[step][0], behind), pre[step][1], weight, scale)

    def expert_term(offset, behind):
        step = abs(offset)
        if step == ring.half:
            before = hidden(step - 1, pre[step][0] + pre[step - 2][1])
            outcomes[step] = down(hidden(step, [before]))
            outcomes[step - 1] = product(after([before], [outcomes[step]])[0], w_down)
        if step == 1:
            pre[0] = summed(after(pre[0][0], behind))
        if step not in outcomes:
            outcomes[step] = down(hidden(step, behind))
        if step in (0, ring.half):
            return outcomes[step]
        return outcomes[step][token_rows:] if offset > 0 else outcomes[step][:token_rows]

    return (residual_state + scatter_rows(ring, expert_term)).astype(bf16)


def solution(mesh):
    return jax.shard_map(
        functools.partial(per_device, mesh.shape["exp"]),
        mesh=mesh,
        in_specs=(
            P(("groups", "exp"), "ctx"),
            P(("groups", "ctx"), "exp"),
            P(("groups", "ctx"), "exp"),
            P(("groups", "ctx"), None),
            P(("groups", "ctx"), None),
            P(None, "exp"),
            P(None, "exp"),
            P("exp", "ctx"),
            P("ctx"),
            P("exp", "ctx", None),
            P("exp", "ctx", None),
            P("exp", None, "ctx"),
            P(("groups", "exp"), None),
            P(("groups", "exp"), None),
            P("groups"),
        ),
        out_specs=P(("groups", "exp"), "ctx"),
        check_vma=False,
    )
```

```python
import functools
import math

import jax
import jax.numpy as jnp
from jax import lax
from jax.experimental import pallas as pl
from jax.experimental.pallas import tpu as pltpu
from jax.sharding import PartitionSpec as P

D = 3584
NOPE = 128
ROPE = 64
VDIM = 128
BLOCK = 512

neg_large = -1e30
route_factor = 2.5
norm_epsilon = 1e-06
f32 = jnp.float32
bf16 = jnp.bfloat16


def attention_kernel(
    order_ref, q_nope_ref, q_rope_ref, own_latent_ref, other_latent_ref, own_rope_ref, other_rope_ref, w_uk_ref, w_uv_ref, out_ref
):
    core = lax.axis_index("ctx")
    rank_of = lambda block: order_ref[block]
    scale = (NOPE + ROPE) ** (-0.5) * math.log2(math.e)
    rows = q_nope_ref.shape[0]
    blocks = rows // BLOCK
    step = 256
    keys_t, values = [], []
    for latent_ref in (own_latent_ref, other_latent_ref):
        latent = latent_ref[...]
        keys_t.append(
            lax.dot_general(w_uk_ref[...], latent, (((0,), (1,)), ((), ())), preferred_element_type=f32).astype(bf16)
        )
        values.append(jnp.dot(latent, w_uv_ref[...], preferred_element_type=f32).astype(bf16))
    ropes = (own_rope_ref[...], other_rope_ref[...])
    blank = jnp.zeros_like(ropes[0])
    diagonal = lax.broadcasted_iota(jnp.int32, (step, step), 1) <= lax.broadcasted_iota(jnp.int32, (step, step), 0)
    key_cat, value_cat = [], []
    for head in range(2):
        cols = slice(head * NOPE, (head + 1) * NOPE)
        key_cat.append([
            jnp.concatenate([keys[cols, :]] + ([rope, blank] if head == 0 else [blank, rope]), axis=0)
            for keys, rope in zip(keys_t, ropes)
        ])
        value_cat.append([jnp.concatenate([held[:, cols], jnp.ones_like(held[:, cols])], axis=1) for held in values])

    def score(head, first):
        cols, part = slice(head * NOPE, (head + 1) * NOPE), slice(first, first + step)
        query = jnp.concatenate([q_nope_ref[part, cols], q_rope_ref[part, :]], axis=1)
        query_block, inside = first // BLOCK, first % BLOCK
        scores = []
        for side in (0, 1):
            owner = core if side == 0 else 1 - core
            for block in range(blocks):
                start = block * BLOCK
                if side == 0 and block == query_block:
                    seen = slice(start, start + inside + step)
                    piece = jnp.dot(query, key_cat[head][side][:, seen], preferred_element_type=f32)
                    last = jnp.where(diagonal, piece[:, inside:], neg_large)
                    piece = jnp.concatenate([piece[:, :inside], last], axis=1) if inside else last
                else:
                    seen = slice(start, start + BLOCK)
                    piece = jnp.dot(query, key_cat[head][side][:, seen], preferred_element_type=f32)
                    earlier = rank_of(owner * blocks + block) < rank_of(core * blocks + query_block)
                    piece = piece + jnp.where(earlier, 0.0, neg_large)
                scores.append((side, seen, piece))
        return scores

    units = [(head, first) for first in range(0, rows, step) for head in range(2)]
    ready = score(*units[0])
    for number, (head, first) in enumerate(units):
        scores = ready
        if number + 1 < len(units):
            ready = score(*units[number + 1])
        best = functools.reduce(jnp.maximum, [jnp.max(piece, axis=1, keepdims=True) for _, _, piece in scores])
        summed = 0.0
        for side, seen, piece in scores:
            probs = jnp.exp2((piece - best) * scale).astype(bf16)
            summed = summed + jnp.dot(probs, value_cat[head][side][seen, :], preferred_element_type=f32)
        out_ref[first : first + step, head * VDIM : (head + 1) * VDIM] = (summed[:, :VDIM] / summed[:, VDIM:]).astype(bf16)


def attend(block_order, q_nope, q_rope, latents, ropes, w_uk, w_uv):
    rows, keys = q_nope.shape[0], 2 * latents[0].shape[0]
    pairs = q_nope.shape[1] // (2 * NOPE)
    held = lambda array: pltpu.with_memory_space_constraint(array, pltpu.HBM)
    whole = lambda array: pl.BlockSpec(array.shape, lambda h, s: (0, 0))
    column = lambda array, width: pl.BlockSpec((array.shape[0], width), lambda h, s: (0, h))
    return pl.pallas_call(
        attention_kernel,
        grid_spec=pltpu.PrefetchScalarGridSpec(
            num_scalar_prefetch=1,
            grid=(pairs,),
            in_specs=[column(q_nope, 2 * NOPE), column(q_rope, 2 * ROPE)]
            + [whole(array) for array in (*latents, *ropes)]
            + [column(w_uk, 2 * NOPE), column(w_uv, 2 * VDIM)],
            out_specs=column(q_nope, 2 * VDIM),
        ),
        out_shape=jax.ShapeDtypeStruct((rows, q_nope.shape[1]), bf16),
        compiler_params=pltpu.CompilerParams(vmem_limit_bytes=12 * 1024 * 1024),
        cost_estimate=pl.CostEstimate(
            flops=7 * rows * keys * pairs * 2 * 384, bytes_accessed=8 * 1024 * 1024, transcendentals=rows * keys * pairs * 2
        ),
    )(held(block_order), held(q_nope), held(q_rope), held(latents[0]), latents[1], held(ropes[0]), ropes[1], held(w_uk), held(w_uv))


def product_kernel(rows_ref, *refs):
    *weight_refs, out_ref = refs
    depth = weight_refs[0].shape[1]
    terms = [
        jnp.dot(rows_ref[e, :, q * depth : (q + 1) * depth], ref[e], preferred_element_type=f32)
        for q, ref in enumerate(weight_refs)
        for e in range(rows_ref.shape[0])
    ]
    out_ref[...] = functools.reduce(jnp.add, terms).astype(bf16)


def product(rows, weights):
    terms, count, depth = rows.shape
    width = weights.shape[2]
    tile, pieces = width // 2, 8
    weights = pltpu.with_memory_space_constraint(weights, pltpu.HBM)
    piece = lambda q: pl.BlockSpec((terms, depth // pieces, tile), lambda n: (0, q, n))
    return pl.pallas_call(
        product_kernel,
        grid=(width // tile,),
        in_specs=[pl.BlockSpec((terms, count, depth), lambda n: (0, 0, 0))] + [piece(q) for q in range(pieces)],
        out_specs=pl.BlockSpec((count, tile), lambda n: (0, n)),
        out_shape=jax.ShapeDtypeStruct((count, width), bf16),
        compiler_params=pltpu.CompilerParams(vmem_limit_bytes=16 * 1024 * 1024),
        cost_estimate=pl.CostEstimate(flops=count * depth * width // 4, bytes_accessed=count * width, transcendentals=0),
    )(rows, *[weights] * pieces)


class Ring:
    def __init__(self, count):
        self.count, self.half = count, count // 2
        self.grid = count == 8
        order = [(2 * p if p < count // 2 else 2 * count - 1 - 2 * p) if self.grid else p for p in range(count)]
        self.up = [(order[p], order[(p + 1) % count]) for p in range(count)]
        self.down = [(t, s) for s, t in self.up]
        index = lax.axis_index("exp")
        self.place = jnp.where(index % 2 == 0, index // 2, count - 1 - index // 2) if self.grid else index

    def index_at(self, place):
        return jnp.where(place < self.half, 2 * place, 2 * self.count - 1 - 2 * place) if self.grid else place

    def at(self, offset):
        return self.index_at(lax.rem(self.place + offset, self.count))

    def send(self, block, way):
        return lax.ppermute(block, "exp", self.up if way > 0 else self.down)


def after(blocks, work):
    if not work:
        return blocks
    held = lax.optimization_barrier((tuple(blocks), tuple(work)))
    return list(held[0])


def scatter_rows(ring, part):
    add = lambda *terms: functools.reduce(jnp.add, [t.astype(f32) for t in terms])
    far = part(ring.half, [])
    sent = [far]
    cut = far.shape[0] // 2
    going = {1: ring.send(far[:cut], 1), -1: ring.send(far[cut:], -1)}
    for offset in range(ring.half - 1, 0, -1):
        behind, sent = sent, []
        for way in (1, -1):
            own, come = part(way * offset, behind), going[way]
            if offset == ring.half - 1:
                come = jnp.pad(come, ((0, cut) if way > 0 else (cut, 0), (0, 0)))
            block = add(own, come).astype(bf16)
            sent.append(block)
            going[way] = ring.send(block, way)
    return add(part(0, sent), going[1], going[-1])


def per_device(
    count,
    resid,
    q_nope,
    q_rope,
    latent,
    k_rope,
    w_uk,
    w_uv,
    w_out,
    norm_gain,
    w_gate,
    w_up,
    w_down,
    routes,
    codes,
    block_order,
):
    token_rows, owned = resid.shape[0], w_gate.shape[0]
    cut = token_rows // 2
    ring = Ring(count)
    core, index = lax.axis_index("ctx"), lax.axis_index("exp")
    swap = lambda block: lax.ppermute(block, "ctx", [(0, 1), (1, 0)])

    ropes = k_rope.T
    heads = attend(
        block_order, q_nope, q_rope, (latent, swap(latent)), (ropes, swap(ropes)), w_uk, w_uv
    )

    project = lambda rows: jnp.dot(rows, w_out, preferred_element_type=f32).astype(bf16)

    def block_of(offset):
        return jnp.bitwise_and(ring.at(offset % count) - core * ring.half, count - 1)

    def pick(own, other, block):
        first = jnp.minimum(block, ring.half - 1) * token_rows
        second = jnp.maximum(block - ring.half, 0) * token_rows
        part = lambda rows, at: lax.dynamic_slice_in_dim(rows, at, token_rows, 0, allow_negative_indices=False)
        return jnp.where(block < ring.half, part(own, first), part(other, second))

    far = block_of(ring.half)
    first = jnp.bitwise_and(far, ring.half - 1) * token_rows
    mine = lax.dynamic_slice_in_dim(heads, first, token_rows, 0, allow_negative_indices=False)
    theirs = swap(mine)
    far_rows = jnp.where(far < ring.half, mine, theirs)
    other_heads = swap(after([heads], [theirs])[0])
    nearby = {}

    def attention_term(offset, behind):
        if offset == ring.half:
            return product(far_rows[None], w_out[None])
        if abs(offset) == ring.half - 1:
            if "first" not in nearby:
                rows = [pick(heads, other_heads, block_of(way * abs(offset))) for way in (1, -1)]
                rows = after([jnp.concatenate(rows, axis=0)], behind)[0]
                nearby["first"] = product(rows[None], w_out[None])
            return nearby["first"][:token_rows] if offset > 0 else nearby["first"][token_rows:]
        if "terms" not in nearby:
            later = after([heads, other_heads], behind)
            nearby["terms"] = [project(rows) for rows in later]
        return lax.optimization_barrier(pick(*nearby["terms"], block_of(offset)))

    residual_state = resid.astype(f32) + scatter_rows(ring, attention_term)

    code_values = codes.astype(f32)
    route_weight = route_factor * code_values / jnp.sum(code_values, axis=1, keepdims=True)
    named = routes[None] == jnp.arange(count * owned, dtype=jnp.int32)[:, None, None]
    routing = jnp.sum(jnp.where(named, route_weight[None], 0.0), axis=2)[None]
    scaled = (residual_state * norm_gain).astype(bf16)
    squares = jnp.sum(residual_state * residual_state, axis=1)
    squares = squares + swap(squares)
    inverse_rms = lax.rsqrt(squares / D + norm_epsilon)
    routing = jnp.concatenate([routing, inverse_rms[None, None]], axis=1)

    def before_hidden(rows):
        product = lambda weight: jnp.einsum("td,ldf->ltf", rows, weight, preferred_element_type=f32).astype(bf16)
        own = [product(w_gate), product(w_up)]
        return own

    def summed(own):
        return own, [swap(pre) for pre in own]

    def hidden_of(own, other, weight, scale):
        gate_pre, up_pre = [mine.astype(f32) + theirs.astype(f32) for mine, theirs in zip(own, other)]
        gate_pre = gate_pre * scale[:, None]
        return (jax.nn.silu(gate_pre) * up_pre * (weight * scale)[:, :, None]).astype(bf16)

    def down(hidden):
        return functools.reduce(
            jnp.add, [jnp.dot(hidden[e], w_down[e], preferred_element_type=f32) for e in range(owned)]
        ).astype(bf16)

    pre = [(before_hidden(scaled), None)]
    below = above = scaled
    hops = count.bit_length() - 1
    far_first = [count >> (1 + number) for number in range(hops)]

    def hop(routing, number):
        other = lax.ppermute(routing, "exp", [(i, i ^ far_first[number]) for i in range(count)])
        return jnp.concatenate([routing, other], axis=0)

    for step in range(1, ring.half + 1):
        if step > 1:
            work = list(pre[step - 2][0])
            if step <= hops:
                (routing,) = after([hop(routing, step - 2)], [below])
                work = work + [routing]
            below, above = after([below, above], work)
        if step == ring.half:
            below, above = below[:cut], above[cut:]
        below, above = ring.send(below, 1), ring.send(above, -1)
        rows = jnp.concatenate([below, above], axis=0)
        if step == ring.half:
            for number in range(min(step - 1, hops - 1), hops):
                routing = hop(routing, number)
            (rows,) = after([rows], pre[step - 1][0])
        if step == ring.half - 1 and step > 2:
            (rows,) = after([rows], pre[step - 2][1])
        pre.append(summed(before_hidden(rows)))

    mine = lax.dynamic_slice_in_dim(routing, index * owned, owned, 1, allow_negative_indices=False)
    offsets = jnp.arange(count, dtype=jnp.int32)
    held = [sum(bit for number, bit in enumerate(far_first) if p >> number & 1) for p in range(count)]
    entry = jnp.bitwise_xor(ring.at(offsets), index)[:, None] == jnp.array(held, jnp.int32)[None, :]
    weights = jnp.sum(jnp.where(entry[:, :, None, None], mine[None], 0.0), axis=1)
    scales = jnp.sum(jnp.where(entry[:, :, None], routing[None, :, -1], 0.0), axis=1)

    outcomes = {}

    def hidden(step, behind):
        offsets = (-step % count, step) if 0 < step < ring.half else (step,)
        weight = jnp.concatenate([weights[o] for o in offsets], axis=1)
        scale = jnp.concatenate([scales[o] for o in offsets], axis=0)
        return hidden_of(after(pre[step][0], behind), pre[step][1], weight, scale)

    def expert_term(offset, behind):
        step = abs(offset)
        if step == ring.half:
            before = hidden(step - 1, pre[step][0] + pre[step - 2][1])
            outcomes[step] = down(hidden(step, [before]))
            outcomes[step - 1] = product(after([before], [outcomes[step]])[0], w_down)
        if step == 1:
            pre[0] = summed(after(pre[0][0], behind))
        if step not in outcomes:
            outcomes[step] = down(hidden(step, behind))
        if step in (0, ring.half):
            return outcomes[step]
        return outcomes[step][token_rows:] if offset > 0 else outcomes[step][:token_rows]

    return (residual_state + scatter_rows(ring, expert_term)).astype(bf16)


def solution(mesh):
    return jax.shard_map(
        functools.partial(per_device, mesh.shape["exp"]),
        mesh=mesh,
        in_specs=(
            P(("groups", "exp"), "ctx"),
            P(("groups", "ctx"), "exp"),
            P(("groups", "ctx"), "exp"),
            P(("groups", "ctx"), None),
            P(("groups", "ctx"), None),
            P(None, "exp"),
            P(None, "exp"),
            P("exp", "ctx"),
            P("ctx"),
            P("exp", "ctx", None),
            P("exp", "ctx", None),
            P("exp", None, "ctx"),
            P(("groups", "exp"), None),
            P(("groups", "exp"), None),
            P("groups"),
        ),
        out_specs=P(("groups", "exp"), "ctx"),
        check_vma=False,
    )
```
